32 devices in a mesh: row: 2 (over x), col: 4 (over z), depth: 4 (over y, core).
Axes of the slice: x: 2, y: 2, z: 4, core: 2. Of those that a mesh axis runs over, the one named last changes fastest.
Arguments:
- k_parts: bfloat16 [2, 1024, 1024], P(None, 'row', 'col'), as said below
- p_parts: bfloat16 [2, 1024, 1024], P(None, 'row', 'col'), as said below
- k_mask: int32 [16, 16], P('row', 'col'), may hold values from 0 to 1, as said below
- p_mask: int32 [16, 16], P('row', 'col'), may hold values from 0 to 1, as said below
- atoms: int32 [16], replicated, may hold values from 0 to 3, as said below
- classes: int32 [4, 4], replicated, may hold values from 0 to 3
- rates: float32 [4], replicated, may hold values from 0.5 to 8
Outputs:
- derivative: float32 [2, 1024, 1024], P(None, ('row', 'depth'), 'col')
The draws below stay inside these ranges and needn't reach their ends.
Inputs may be any that keep to these rules, and one draw needn't show every extreme that they name: k_parts[0] is symmetric and k_parts[1] antisymmetric, so the Kohn-Sham matrix is Hermitian. p_parts[0] is symmetric and p_parts[1] antisymmetric, so the density matrix is Hermitian. `k_mask`: symmetric; every diagonal tile is kept; each tile row keeps a band of tiles around the diagonal of its own half-width, from 0 to 4 tiles, besides scattered tiles further away. `p_mask`: symmetric; every diagonal tile is kept; each tile row keeps a band of tiles around the diagonal of its own half-width, from 0 to 4 tiles, besides scattered tiles further away. `atoms`: never falling along the tiles; every atom block holds at least one tile.
All inputs are finite; a program needn't handle non-finite values.
Results may differ from the reference program's by a relative error of at most 0.0003.
Values may be sent and summed in bfloat16 or wider, within the bound.
No kernel may reach another device: no remote copies, remote signals or barrier semaphores. Data moves between devices by JAX's collectives and lax.ppermute only.
A program may use at most 64 MiB of HBM per device.

```python
import math
import jax
import jax.numpy as jnp

TILE = 64
NCLASS = 4
N = 1024
NT = 16
NA = 4


def hermitian_pair(key):
    first = jax.random.normal(jax.random.fold_in(key, 1), (N, N), jnp.float32)
    second = jax.random.normal(jax.random.fold_in(key, 2), (N, N), jnp.float32)
    scale = (2.0 * TILE) ** (-0.5)
    real_part = (first + first.T) * scale
    imag_part = (second - second.T) * scale
    return jnp.stack((real_part, imag_part)).astype(jnp.bfloat16)


def band_mask(key):
    widths = jax.random.randint(jax.random.fold_in(key, 1), (NT,), 0, NT // 4 + 1)
    distant = jax.random.randint(jax.random.fold_in(key, 2), (NT, NT), 0, 8) == 0
    places = jnp.arange(NT, dtype=jnp.int32)
    spacing = jnp.abs(places[:, None] - places[None, :])
    reach = jnp.maximum(widths[:, None], widths[None, :])
    keep = (spacing <= reach) | distant | distant.T
    return keep.astype(jnp.int32)


def draw_k_parts(key, part):
    return hermitian_pair(jax.random.fold_in(key, 11))


def draw_p_parts(key, part):
    return hermitian_pair(jax.random.fold_in(key, 12))


def draw_k_mask(key, part):
    return band_mask(jax.random.fold_in(key, 21))


def draw_p_mask(key, part):
    return band_mask(jax.random.fold_in(key, 22))


def draw_atoms(key, part):
    candidates = jnp.arange(1, NT, dtype=jnp.int32)
    shuffled = jax.random.permutation(jax.random.fold_in(key, 31), candidates)
    bounds = shuffled[:NA - 1]
    places = jnp.arange(NT, dtype=jnp.int32)
    return jnp.sum((bounds[None, :] <= places[:, None]).astype(jnp.int32), axis=1).astype(jnp.int32)


def set_ends(result, key, least, top_value):
    longest = result.shape.index(max(result.shape))
    spots = []
    for shift in (0, 1):
        where = [jax.random.randint(jax.random.fold_in(key, axis), (), 0, length) for axis, length in enumerate(result.shape)]
        where[longest] = (where[longest] + shift) % result.shape[longest]
        spots.append(tuple(where))
    return result.at[spots[0]].set(least).at[spots[1]].set(top_value)


def setup_inputs(seed: int = 0) -> dict:
    splits = jax.random.split(jax.random.key(seed), 8)
    return {
        "k_parts": draw_k_parts(jax.random.fold_in(splits[7], 71), 0),
        "p_parts": draw_p_parts(jax.random.fold_in(splits[7], 71), 0),
        "k_mask": draw_k_mask(jax.random.fold_in(splits[7], 71), 0),
        "p_mask": draw_p_mask(jax.random.fold_in(splits[7], 71), 0),
        "atoms": draw_atoms(jax.random.fold_in(splits[7], 71), 0),
        "classes": set_ends(jax.random.randint(splits[5], (NA, NA), 0, NCLASS), jax.random.fold_in(splits[5], 1), 0, NCLASS - 1).astype(jnp.int32),
        "rates": jnp.clip(jnp.exp(jax.random.uniform(splits[6], (NCLASS,), jnp.float32, math.log(0.5), math.log(8.0))), 0.5, 8.0),
    }


def expand_tiles(mask):
    return jnp.repeat(jnp.repeat(mask, TILE, 0), TILE, 1).astype(jnp.bfloat16)


def product(left, right):
    return jnp.dot(left, right, preferred_element_type=jnp.float32)


def reference(k_parts, p_parts, k_mask, p_mask, atoms, classes, rates):
    k_full = k_parts * expand_tiles(k_mask)[None]
    p_full = p_parts * expand_tiles(p_mask)[None]
    k_real, k_imag = k_full[0], k_full[1]
    p_real, p_imag = p_full[0], p_full[1]
    z_real = product(k_real, p_real) - product(k_imag, p_imag) - product(p_real, k_real) + product(p_imag, k_imag)
    z_imag = product(k_real, p_imag) + product(k_imag, p_real) - product(p_real, k_imag) - product(p_imag, k_real)
    atom_rows = jnp.repeat(atoms, TILE)
    kinds = classes[atom_rows[:, None], atom_rows[None, :]]
    differ = (atom_rows[:, None] != atom_rows[None, :]).astype(rates.dtype)
    gamma = rates[kinds] * differ
    p_float = p_full.astype(rates.dtype)
    return jnp.stack((z_imag - gamma * p_float[0], -z_real - gamma * p_float[1]))
```

```python
import functools

import jax
import jax.numpy as jnp
from jax import lax
from jax.experimental import pallas as pl
from jax.experimental.pallas import tpu as pltpu
from jax.sharding import PartitionSpec as P

TILE = 64


def tile_row(mask_ref, tile, width, dtype):
    lanes = lax.broadcasted_iota(jnp.int32, (1, width), 1) // TILE
    row = jnp.zeros((1, width), jnp.float32)
    for place in range(width // TILE):
        row = jnp.where(lanes == place, mask_ref[tile, place].astype(jnp.float32), row)
    return row.astype(dtype)


def strip_kernel(place, k_mask, p_mask, k_ref, p_ref, out_ref):
    rows, width = k_ref.shape[1:]
    tiles = rows // TILE
    for tile in range(tiles):
        span = pl.ds(tile * TILE, TILE)
        for slot, mask_ref, ref in ((0, k_mask, k_ref), (2, p_mask, p_ref)):
            row = tile_row(mask_ref, place[2] * tiles + tile, width, ref.dtype)
            for part in range(2):
                out_ref[slot + part, span, :] = ref[part, span, :] * row


def mask_strip(place, k_mask, p_mask, k_parts, p_parts, out_rows):
    width = k_parts.shape[2]
    block = pl.BlockSpec((2, out_rows, width), lambda g, place, km, pm: (0, place[2], 0))
    return pl.pallas_call(
        strip_kernel,
        grid_spec=pltpu.PrefetchScalarGridSpec(
            num_scalar_prefetch=3,
            grid=(1,),
            in_specs=[block, block],
            out_specs=pl.BlockSpec((4, out_rows, width), lambda g, *_: (0, 0, 0)),
        ),
        out_shape=jax.ShapeDtypeStruct((4, out_rows, width), k_parts.dtype),
        name="mask_strip",
    )(place, k_mask, p_mask, k_parts, p_parts)


def product_kernel(
    rows_n, cols_n, depth, place, k_mask, p_mask, atoms, classes, rates, k_ref, p_ref, *refs
):
    row_strips = refs[:cols_n]
    col_strips = refs[cols_n : cols_n + (rows_n - 1) * depth]
    out_ref, left, right = refs[cols_n + (rows_n - 1) * depth :]
    out_rows, width = row_strips[0].shape[1:]
    here = k_ref.shape[1]
    row, col, layer = place[0], place[1], place[2]
    own = row_strips[0]
    for shift, ref in enumerate(row_strips):
        at = pl.ds(pl.multiple_of(lax.rem(col - shift + cols_n, cols_n) * width, width), width)
        k_re, k_im, p_re, p_im = ref[0], ref[1], ref[2], ref[3]
        top, low = pl.ds(0, out_rows), pl.ds(out_rows, out_rows)
        left[0, top, at] = k_re
        left[0, low, at] = k_im
        left[1, top, at] = -k_im
        left[1, low, at] = k_re
        left[2, top, at] = -p_re
        left[2, low, at] = -p_im
        left[3, top, at] = p_im
        left[3, low, at] = -p_re
    for tile in range(here // TILE):
        span = pl.ds(tile * TILE, TILE)
        at = pl.ds(pl.multiple_of(row * here + tile * TILE, TILE), TILE)
        for slot, mask_ref, ref in ((2, k_mask, k_ref), (0, p_mask, p_ref)):
            factor = tile_row(mask_ref, tile, width, ref.dtype)
            for part in range(2):
                right[slot + part, at, :] = ref[part, span, :] * factor
    for index, ref in enumerate(col_strips):
        shift, flip = index // depth + 1, index % depth
        start = lax.rem(row - shift + rows_n, rows_n) * here + (layer ^ flip) * out_rows
        at = pl.ds(pl.multiple_of(start, out_rows), out_rows)
        right[2, at, :] = ref[0]
        right[3, at, :] = ref[1]
        right[0, at, :] = ref[2]
        right[1, at, :] = ref[3]
    total = jnp.zeros((2 * out_rows, width), jnp.float32)
    for slot in range(4):
        total += jnp.dot(left[slot], right[slot], preferred_element_type=jnp.float32)
    z_re, z_im = total[:out_rows], total[out_rows:]
    lanes = lax.broadcasted_iota(jnp.int32, (1, width), 1) // TILE
    row_tiles, col_tiles = out_rows // TILE, width // TILE
    for tile in range(row_tiles):
        span = pl.ds(tile * TILE, TILE)
        atom_row = atoms[(row * depth + layer) * row_tiles + tile]
        gamma = jnp.zeros((1, width), jnp.float32)
        for spot in range(col_tiles):
            atom_col = atoms[col * col_tiles + spot]
            rate = jnp.where(atom_row != atom_col, rates[classes[atom_row, atom_col]], 0.0)
            gamma = jnp.where(lanes == spot, rate, gamma)
        cut = slice(tile * TILE, (tile + 1) * TILE)
        out_ref[0, span, :] = z_im[cut] - gamma * own[2, span, :].astype(jnp.float32)
        out_ref[1, span, :] = -z_re[cut] - gamma * own[3, span, :].astype(jnp.float32)


def exchange(x, axis, perm):
    return lax.ppermute(x, axis, perm)


def body(k_parts, p_parts, k_mask, p_mask, atoms, classes, rates):
    rows_n, cols_n, depth = (lax.axis_size(a) for a in ("row", "col", "depth"))
    place = jnp.stack([lax.axis_index(a) for a in ("row", "col", "depth")]).astype(jnp.int32)
    here, width = k_parts.shape[1:]
    out_rows = here // depth
    strip = mask_strip(place, k_mask, p_mask, k_parts, p_parts, out_rows)
    col_strips = []
    for shift in range(1, rows_n):
        pieces = {0: exchange(strip, "row", [(i, (i + shift) % rows_n) for i in range(rows_n)])}
        stride = depth // 2
        while stride:
            perm = [(i, i ^ stride) for i in range(depth)]
            for flip in list(pieces):
                pieces[flip ^ stride] = exchange(pieces[flip], "depth", perm)
            stride //= 2
        col_strips += [pieces[flip] for flip in range(depth)]
    row_strips = [strip]
    for shift in range(1, cols_n):
        row_strips.append(
            exchange(strip, "col", [(i, (i + shift) % cols_n) for i in range(cols_n)])
        )
    total_rows = here * rows_n
    need = 2 * (4 * total_rows * width * 2 + 12 * out_rows * total_rows * 2 + 4 * here * width * 2)
    smem = pl.BlockSpec(memory_space=pltpu.SMEM)
    vmem = pl.BlockSpec(memory_space=pltpu.VMEM)
    n_vec = 2 + len(row_strips) + len(col_strips)
    return pl.pallas_call(
        functools.partial(product_kernel, rows_n, cols_n, depth),
        in_specs=[smem] * 6 + [vmem] * n_vec,
        out_specs=vmem,
        out_shape=jax.ShapeDtypeStruct((2, out_rows, width), jnp.float32),
        scratch_shapes=[
            pltpu.VMEM((4, 2 * out_rows, total_rows), k_parts.dtype),
            pltpu.VMEM((4, total_rows, width), k_parts.dtype),
        ],
        compiler_params=pltpu.CompilerParams(vmem_limit_bytes=need + (4 << 20)),
        name="commutator",
    )(place, k_mask, p_mask, atoms, classes, rates, k_parts, p_parts, *row_strips, *col_strips)


def solution(mesh):
    return jax.shard_map(
        body,
        mesh=mesh,
        in_specs=(
            P(None, "row", "col"),
            P(None, "row", "col"),
            P("row", "col"),
            P("row", "col"),
            P(),
            P(),
            P(),
        ),
        out_specs=P(None, ("row", "depth"), "col"),
        check_vma=False,
    )
```

```python
import functools

import jax
import jax.numpy as jnp
from jax import lax
from jax.experimental import pallas as pl
from jax.experimental.pallas import tpu as pltpu
from jax.sharding import PartitionSpec as P

TILE = 64

SMEM = pl.BlockSpec(memory_space=pltpu.SMEM)
VMEM = pl.BlockSpec(memory_space=pltpu.VMEM)
ANY = pl.BlockSpec(memory_space=pl.ANY)


def params(*shapes):
    total = sum(functools.reduce(lambda a, b: a * b, s) * w for s, w in shapes)
    return pltpu.CompilerParams(vmem_limit_bytes=2 * total + (4 << 20))


def tile_row(mask_ref, tile, width, dtype):
    lanes = lax.broadcasted_iota(jnp.int32, (1, width), 1) // TILE
    row = jnp.zeros((1, width), jnp.float32)
    for place in range(width // TILE):
        row = jnp.where(lanes == place, mask_ref[place, tile].astype(jnp.float32), row)
    return row.astype(dtype)


def strip_kernel(k_mask, p_mask, k_ref, p_ref, out_ref, held, sems):
    rows = out_ref.shape[1]
    width = out_ref.shape[2]
    layer = lax.axis_index("depth")
    span = pl.ds(pl.multiple_of(layer * rows, rows), rows)
    copies = [
        pltpu.make_async_copy(ref.at[:, span, :], held.at[pl.ds(2 * i, 2)], sems.at[i])
        for i, ref in enumerate((k_ref, p_ref))
    ]
    for copy in copies:
        copy.start()
    tiles = rows // TILE
    for i, mask_ref in enumerate((k_mask, p_mask)):
        factors = [tile_row(mask_ref, layer * tiles + t, width, held.dtype) for t in range(tiles)]
        copies[i].wait()
        for tile, factor in enumerate(factors):
            at = pl.ds(tile * TILE, TILE)
            for part in (2 * i, 2 * i + 1):
                out_ref[part, at, :] = held[part, at, :] * factor


def mask_strip(k_mask, p_mask, k_parts, p_parts, out_rows):
    shape = (4, out_rows, k_parts.shape[2])
    return pl.pallas_call(
        strip_kernel,
        in_specs=[SMEM, SMEM, ANY, ANY],
        out_specs=VMEM,
        out_shape=jax.ShapeDtypeStruct(shape, k_parts.dtype),
        scratch_shapes=[pltpu.VMEM(shape, k_parts.dtype), pltpu.SemaphoreType.DMA((2,))],
        compiler_params=params((shape, 4)),
        name="mask_strip",
    )(k_mask, p_mask, k_parts, p_parts)


def local_kernel(k_mask, p_mask, atoms, classes, rates, k_ref, p_ref, own, right_ref, damp_ref):
    here, width = k_ref.shape[1:]
    out_rows = own.shape[1]
    row, col, layer = (lax.axis_index(a) for a in ("row", "col", "depth"))
    for tile in range(here // TILE):
        span = pl.ds(tile * TILE, TILE)
        for slot, mask_ref, ref in ((2, k_mask, k_ref), (0, p_mask, p_ref)):
            factor = tile_row(mask_ref, tile, width, ref.dtype)
            for part in range(2):
                right_ref[slot + part, span, :] = ref[part, span, :] * factor
    lanes = lax.broadcasted_iota(jnp.int32, (1, width), 1) // TILE
    row_tiles, col_tiles = out_rows // TILE, width // TILE
    first = (row * lax.axis_size("depth") + layer) * row_tiles
    for tile in range(row_tiles):
        span = pl.ds(tile * TILE, TILE)
        atom_row = atoms[first + tile]
        gamma = jnp.zeros((1, width), jnp.float32)
        for spot in range(col_tiles):
            atom_col = atoms[col * col_tiles + spot]
            rate = jnp.where(atom_row != atom_col, rates[classes[atom_row, atom_col]], 0.0)
            gamma = jnp.where(lanes == spot, rate, gamma)
        for part in range(2):
            damp_ref[part, span, :] = gamma * own[2 + part, span, :].astype(jnp.float32)


def local_part(k_mask, p_mask, atoms, classes, rates, k_parts, p_parts, strip):
    here, width = k_parts.shape[1:]
    out_rows = strip.shape[1]
    return pl.pallas_call(
        local_kernel,
        in_specs=[SMEM] * 5 + [VMEM] * 3,
        out_specs=[VMEM, VMEM],
        out_shape=[
            jax.ShapeDtypeStruct((4, here, width), k_parts.dtype),
            jax.ShapeDtypeStruct((2, out_rows, width), jnp.float32),
        ],
        compiler_params=params(((4, here, width), 4), ((4, out_rows, width), 4)),
        cost_estimate=pl.CostEstimate(
            flops=8 * here * width, bytes_accessed=20 * here * width, transcendentals=0
        ),
        name="local_part",
    )(k_mask, p_mask, atoms, classes, rates, k_parts, p_parts, strip)


def place_left(left, ref, at, rows):
    k_re, k_im, p_re, p_im = ref[0], ref[1], ref[2], ref[3]
    top, low = pl.ds(0, rows), pl.ds(rows, rows)
    left[0, top, at] = k_re
    left[0, low, at] = k_im
    left[1, top, at] = -k_im
    left[1, low, at] = k_re
    left[2, top, at] = -p_re
    left[2, low, at] = -p_im
    left[3, top, at] = p_im
    left[3, low, at] = -p_re


def product_kernel(rows_n, cols_n, depth, near, damp, own, *refs):
    ups = refs[: cols_n - 1]
    downs = refs[cols_n - 1 : 2 * (cols_n - 1)]
    strips = refs[2 * (cols_n - 1) : -3]
    out_ref, left, far = refs[-3:]
    out_rows, width = own.shape[1:]
    here = near.shape[1]
    row, col, layer = (lax.axis_index(a) for a in ("row", "col", "depth"))

    def columns(block):
        return pl.ds(pl.multiple_of(block * width, width), width)

    place_left(left, own, columns(col), out_rows)
    for step in range(1, cols_n):

        @pl.when(col >= step)
        def _():
            place_left(left, ups[step - 1], columns(col - step), out_rows)

        @pl.when(col + step < cols_n)
        def _():
            place_left(left, downs[step - 1], columns(col + step), out_rows)

    for index, ref in enumerate(strips):
        other, flip = index // depth, index % depth
        at = pl.ds(pl.multiple_of((layer ^ flip) * out_rows, out_rows), out_rows)
        for slot in range(4):
            far[other, slot, at, :] = ref[(slot + 2) % 4]
    total = jnp.zeros((2 * out_rows, width), jnp.float32)
    for shift in range(rows_n):
        half = lax.rem(row - shift + rows_n, rows_n)
        at = pl.ds(pl.multiple_of(half * here, here), here)
        for slot in range(4):
            right = near[slot] if shift == 0 else far[shift - 1, slot]
            total += jnp.dot(left[slot, :, at], right, preferred_element_type=jnp.float32)
    out_ref[0] = total[out_rows:] - damp[0]
    out_ref[1] = -total[:out_rows] - damp[1]


def body(k_parts, p_parts, k_mask, p_mask, atoms, classes, rates):
    rows_n, cols_n, depth = (lax.axis_size(a) for a in ("row", "col", "depth"))
    here, width = k_parts.shape[1:]
    out_rows = here // depth
    k_mask, p_mask = k_mask.T, p_mask.T
    strip = mask_strip(k_mask, p_mask, k_parts, p_parts, out_rows)
    ups, downs = [strip], [strip]
    for step in range(1, cols_n):
        ups.append(lax.ppermute(ups[-1], "col", [(i, i + 1) for i in range(step - 1, cols_n - 1)]))
        downs.append(lax.ppermute(downs[-1], "col", [(i, i - 1) for i in range(1, cols_n - step + 1)]))
    strips = []
    for shift in range(1, rows_n):
        perm = [(i, (i + shift) % rows_n) for i in range(rows_n)]
        pieces = {0: lax.ppermute(strip, "row", perm)}
        stride = depth // 2
        while stride:
            perm = [(i, i ^ stride) for i in range(depth)]
            for flip in list(pieces):
                pieces[flip ^ stride] = lax.ppermute(pieces[flip], "depth", perm)
            stride //= 2
        strips += [pieces[flip] for flip in range(depth)]
    near, damp = local_part(k_mask, p_mask, atoms, classes, rates, k_parts, p_parts, strip)
    total_rows = here * rows_n
    operands = [near, damp, strip] + ups[1:] + downs[1:] + strips
    return pl.pallas_call(
        functools.partial(product_kernel, rows_n, cols_n, depth),
        in_specs=[VMEM] * len(operands),
        out_specs=VMEM,
        out_shape=jax.ShapeDtypeStruct((2, out_rows, width), jnp.float32),
        scratch_shapes=[
            pltpu.VMEM((4, 2 * out_rows, total_rows), k_parts.dtype),
            pltpu.VMEM((rows_n - 1, 4, here, width), k_parts.dtype),
        ],
        compiler_params=params(
            ((4, total_rows, width), 4), ((16, out_rows, total_rows), 2), ((2, out_rows, width), 8)
        ),
        name="commutator",
    )(*operands)


def solution(mesh):
    return jax.shard_map(
        body,
        mesh=mesh,
        in_specs=(
            P(None, "row", "col"),
            P(None, "row", "col"),
            P("row", "col"),
            P("row", "col"),
            P(),
            P(),
            P(),
        ),
        out_specs=P(None, ("row", "depth"), "col"),
        check_vma=False,
    )
```

```python
import functools

import jax
import jax.numpy as jnp
from jax import lax
from jax.experimental import pallas as pl
from jax.experimental.pallas import tpu as pltpu
from jax.sharding import PartitionSpec as P

TILE = 64

SMEM = pl.BlockSpec(memory_space=pltpu.SMEM)
VMEM = pl.BlockSpec(memory_space=pltpu.VMEM)


def params(*shapes):
    total = sum(functools.reduce(lambda a, b: a * b, s) * w for s, w in shapes)
    return pltpu.CompilerParams(vmem_limit_bytes=2 * total + (4 << 20))


def tile_row(mask_ref, tile, width, dtype):
    lanes = lax.broadcasted_iota(jnp.int32, (1, width), 1) // TILE
    row = jnp.zeros((1, width), jnp.float32)
    for place in range(width // TILE):
        row = jnp.where(lanes == place, mask_ref[place, tile].astype(jnp.float32), row)
    return row.astype(dtype)


def send_kernel(k_mask, p_mask, k_ref, p_ref, strip_ref, share_ref, held, masks, sems, mask_sems):
    out_rows, width = strip_ref.shape[1:]
    share_rows = share_ref.shape[1]
    layer = lax.axis_index("depth")
    mask_copies = [
        pltpu.make_async_copy(ref, masks.at[i], mask_sems.at[i])
        for i, ref in enumerate((k_mask, p_mask))
    ]
    for copy in mask_copies:
        copy.start()
    parts = []
    base = 0
    for first, ref in (
        (layer * out_rows, strip_ref),
        (lax.rem(layer, k_ref.shape[1] // share_rows) * share_rows, share_ref),
    ):
        rows = ref.shape[1]
        span = pl.ds(pl.multiple_of(first, rows), rows)
        for i, source in enumerate((k_ref, p_ref)):
            spot = held.at[pl.ds(2 * i, 2), pl.ds(base, rows)]
            copy = pltpu.make_async_copy(source.at[:, span, :], spot, sems.at[len(parts)])
            copy.start()
            parts.append((copy, i, ref, base, rows, first // TILE))
        base += rows
    for copy in mask_copies:
        copy.wait()
    for copy, i, ref, base, rows, tile in parts:
        copy.wait()
        for step in range(rows // TILE):
            factor = tile_row(masks.at[i], tile + step, width, held.dtype)
            here, there = pl.ds(base + step * TILE, TILE), pl.ds(step * TILE, TILE)
            for part in (2 * i, 2 * i + 1):
                ref[part, there, :] = held[part, here, :] * factor


def mask_for_sending(k_mask, p_mask, k_parts, p_parts, out_rows, share_rows):
    width, dtype = k_parts.shape[2], k_parts.dtype
    rows = out_rows + share_rows
    hbm = pl.BlockSpec(memory_space=pltpu.HBM)
    return pl.pallas_call(
        send_kernel,
        in_specs=[hbm] * 4,
        out_specs=[VMEM, VMEM],
        out_shape=[
            jax.ShapeDtypeStruct((4, out_rows, width), dtype),
            jax.ShapeDtypeStruct((4, share_rows, width), dtype),
        ],
        scratch_shapes=[
            pltpu.VMEM((4, rows, width), dtype),
            pltpu.SMEM((2,) + k_mask.shape, k_mask.dtype),
            pltpu.SemaphoreType.DMA((4,)),
            pltpu.SemaphoreType.DMA((2,)),
        ],
        name="mask_for_sending",
    )(k_mask, p_mask, k_parts, p_parts)


def local_kernel(k_mask, p_mask, atoms, classes, rates, k_ref, p_ref, own, right_ref, damp_ref):
    here, width = k_ref.shape[1:]
    out_rows = own.shape[1]
    row, col, layer = (lax.axis_index(a) for a in ("row", "col", "depth"))
    for tile in range(here // TILE):
        span = pl.ds(tile * TILE, TILE)
        for slot, mask_ref, ref in ((2, k_mask, k_ref), (0, p_mask, p_ref)):
            factor = tile_row(mask_ref, tile, width, ref.dtype)
            for part in range(2):
                right_ref[slot + part, span, :] = ref[part, span, :] * factor
    lanes = lax.broadcasted_iota(jnp.int32, (1, width), 1) // TILE
    row_tiles, col_tiles = out_rows // TILE, width // TILE
    first = (row * lax.axis_size("depth") + layer) * row_tiles
    for tile in range(row_tiles):
        span = pl.ds(tile * TILE, TILE)
        atom_row = atoms[first + tile]
        gamma = jnp.zeros((1, width), jnp.float32)
        for spot in range(col_tiles):
            atom_col = atoms[col * col_tiles + spot]
            rate = jnp.where(atom_row != atom_col, rates[classes[atom_row, atom_col]], 0.0)
            gamma = jnp.where(lanes == spot, rate, gamma)
        for part in range(2):
            damp_ref[part, span, :] = gamma * own[2 + part, span, :].astype(jnp.float32)


def local_part(k_mask, p_mask, atoms, classes, rates, k_parts, p_parts, strip):
    here, width = k_parts.shape[1:]
    out_rows = strip.shape[1]
    return pl.pallas_call(
        local_kernel,
        in_specs=[SMEM] * 5 + [VMEM] * 3,
        out_specs=[VMEM, VMEM],
        out_shape=[
            jax.ShapeDtypeStruct((4, here, width), k_parts.dtype),
            jax.ShapeDtypeStruct((2, out_rows, width), jnp.float32),
        ],
        compiler_params=params(((4, here, width), 4), ((4, out_rows, width), 4)),
        cost_estimate=pl.CostEstimate(
            flops=8 * here * width, bytes_accessed=20 * here * width, transcendentals=0
        ),
        name="local_part",
    )(k_mask, p_mask, atoms, classes, rates, k_parts, p_parts, strip)


def place_left(left, ref, at, rows):
    k_re, k_im, p_re, p_im = ref[0], ref[1], ref[2], ref[3]
    top, low = pl.ds(0, rows), pl.ds(rows, rows)
    left[0, top, at] = k_re
    left[0, low, at] = k_im
    left[1, top, at] = -k_im
    left[1, low, at] = k_re
    left[2, top, at] = -p_re
    left[2, low, at] = -p_im
    left[3, top, at] = p_im
    left[3, low, at] = -p_re


def early_kernel(cols_n, near, own, *refs):
    ups = refs[: cols_n // 2 - 1]
    downs = refs[cols_n // 2 - 1 : -2]
    left, total_ref = refs[-2:]
    out_rows, width = own.shape[1:]
    here = near.shape[1]
    row, col = lax.axis_index("row"), lax.axis_index("col")

    def columns(shift):
        block = lax.rem(col + shift + cols_n, cols_n)
        return pl.ds(pl.multiple_of(block * width, width), width)

    place_left(left, own, columns(0), out_rows)
    for step, ref in enumerate(ups, 1):
        place_left(left, ref, columns(-step), out_rows)
    for step, ref in enumerate(downs, 1):
        place_left(left, ref, columns(step), out_rows)
    left[:, :, columns(-(cols_n // 2))] = jnp.zeros((4, 2 * out_rows, width), left.dtype)
    total = jnp.zeros((2 * out_rows, width), jnp.float32)
    at = pl.ds(pl.multiple_of(row * here, here), here)
    for slot in range(4):
        total += jnp.dot(left[slot, :, at], near[slot], preferred_element_type=jnp.float32)
    total_ref[...] = total


def early_product(near, strip, ups, downs, cols_n):
    out_rows, width = strip.shape[1:]
    left = (4, 2 * out_rows, cols_n * width)
    operands = [near, strip] + ups + downs
    return pl.pallas_call(
        functools.partial(early_kernel, cols_n),
        in_specs=[VMEM] * len(operands),
        out_specs=[VMEM, VMEM],
        out_shape=[
            jax.ShapeDtypeStruct(left, near.dtype),
            jax.ShapeDtypeStruct((2 * out_rows, width), jnp.float32),
        ],
        compiler_params=params((near.shape, 2), (left, 4), ((2 * out_rows, width), 4)),
        cost_estimate=pl.CostEstimate(
            flops=2 * 8 * out_rows * near.shape[1] * width * 40,
            bytes_accessed=left[0] * left[1] * left[2] * 4,
            transcendentals=0,
        ),
        name="early_product",
    )(*operands)


def product_kernel(rows_n, cols_n, split, near, damp, left, early, last, *refs):
    shares = refs[:-3]
    out_ref, left_last, total = refs[-3:]
    out_rows, width = last.shape[1:]
    here = near.shape[1]
    row, col, layer = (lax.axis_index(a) for a in ("row", "col", "depth"))
    place_left(left_last, last, pl.ds(0, width), out_rows)
    value = early[...]
    rights = [(row * here, near, 0)]
    for index, ref in enumerate(shares):
        rows = ref.shape[1]
        other = lax.rem(row - index // split - 1 + rows_n, rows_n)
        mine = lax.rem(layer, split) ^ (index % split)
        rights.append((other * here + mine * rows, ref, 2))
        at = pl.ds(pl.multiple_of(rights[-1][0], rows), rows)
        for slot in range(4):
            right = ref[(slot + 2) % 4]
            value += jnp.dot(left[slot, :, at], right, preferred_element_type=jnp.float32)
    total[...] = value
    start = lax.rem(col + cols_n - cols_n // 2, cols_n) * width
    for first, ref, turn in rights:

        @pl.when((start >= first) & (start < first + ref.shape[1]))
        def _():
            at = pl.ds(pl.multiple_of(start - first, width), width)
            value = total[...]
            for slot in range(4):
                right = ref[(slot + turn) % 4, at, :]
                value += jnp.dot(left_last[slot], right, preferred_element_type=jnp.float32)
            total[...] = value

    out_ref[0] = total[pl.ds(out_rows, out_rows), :] - damp[0]
    out_ref[1] = -total[pl.ds(0, out_rows), :] - damp[1]


def body(k_parts, p_parts, k_mask, p_mask, atoms, classes, rates):
    rows_n, cols_n, depth = (lax.axis_size(a) for a in ("row", "col", "depth"))
    here, width = k_parts.shape[1:]
    out_rows = here // depth
    split = 2 if depth % 2 == 0 else 1
    k_mask, p_mask = k_mask.T, p_mask.T
    strip, share = mask_for_sending(k_mask, p_mask, k_parts, p_parts, out_rows, here // split)
    ups, downs = [strip], [strip]
    for step in range(1, cols_n // 2 + 1):
        ups.append(lax.ppermute(ups[-1], "col", [(i, (i + 1) % cols_n) for i in range(cols_n)]))
    for step in range(1, cols_n - cols_n // 2):
        downs.append(lax.ppermute(downs[-1], "col", [(i, (i - 1) % cols_n) for i in range(cols_n)]))
    shares = []
    for shift in range(1, rows_n):
        perm = [(i, (i + shift) % rows_n) for i in range(rows_n)]
        shares.append(lax.ppermute(share, "row", perm))
        if split == 2:
            shares.append(lax.ppermute(shares[-1], "depth", [(i, i ^ 1) for i in range(depth)]))
    near, damp = local_part(k_mask, p_mask, atoms, classes, rates, k_parts, p_parts, strip)
    left, early = early_product(near, strip, ups[1:-1], downs[1:], cols_n)
    operands = [near, damp, left, early, ups[-1]] + shares
    block = (4, 2 * out_rows, width)
    return pl.pallas_call(
        functools.partial(product_kernel, rows_n, cols_n, split),
        in_specs=[VMEM] * len(operands),
        out_specs=VMEM,
        out_shape=jax.ShapeDtypeStruct((2, out_rows, width), jnp.float32),
        scratch_shapes=[
            pltpu.VMEM(block, k_parts.dtype),
            pltpu.VMEM((2 * out_rows, width), jnp.float32),
        ],
        compiler_params=params(
            ((4, rows_n * here, width), 2), (left.shape, 2), (block, 4), ((2 * out_rows, width), 16)
        ),
        name="commutator",
    )(*operands)


def solution(mesh):
    return jax.shard_map(
        body,
        mesh=mesh,
        in_specs=(
            P(None, "row", "col"),
            P(None, "row", "col"),
            P("row", "col"),
            P("row", "col"),
            P(),
            P(),
            P(),
        ),
        out_specs=P(None, ("row", "depth"), "col"),
        check_vma=False,
    )
```

```python
import functools

import jax
import jax.numpy as jnp
from jax import lax
from jax.experimental import pallas as pl
from jax.experimental.pallas import tpu as pltpu
from jax.sharding import PartitionSpec as P

TILE = 64

HBM = pl.BlockSpec(memory_space=pltpu.HBM)
SMEM = pl.BlockSpec(memory_space=pltpu.SMEM)
VMEM = pl.BlockSpec(memory_space=pltpu.VMEM)


def params(*shapes):
    total = sum(functools.reduce(lambda a, b: a * b, s) * w for s, w in shapes)
    return pltpu.CompilerParams(vmem_limit_bytes=2 * total + (4 << 20))


def tile_row(mask_ref, tile, width, dtype):
    lanes = lax.broadcasted_iota(jnp.int32, (1, width), 1) // TILE
    row = jnp.zeros((1, width), jnp.float32)
    for place in range(width // TILE):
        row = jnp.where(lanes == place, mask_ref[place, tile].astype(jnp.float32), row)
    return row.astype(dtype)


def fetch_masks(sources, masks, sems):
    copies = [
        pltpu.make_async_copy(ref, masks.at[i], sems.at[i]) for i, ref in enumerate(sources)
    ]
    for copy in copies:
        copy.start()
    return copies


def strip_kernel(k_mask, p_mask, k_ref, p_ref, strip_ref, held, masks, sems, mask_sems):
    rows, width = strip_ref.shape[1:]
    first = lax.axis_index("depth") * rows
    mask_copies = fetch_masks((k_mask, p_mask), masks, mask_sems)
    span = pl.ds(pl.multiple_of(first, rows), rows)
    copies = [
        pltpu.make_async_copy(ref.at[:, span, :], held.at[pl.ds(2 * i, 2)], sems.at[i])
        for i, ref in enumerate((k_ref, p_ref))
    ]
    for copy in copies:
        copy.start()
    for copy in mask_copies:
        copy.wait()
    for i, copy in enumerate(copies):
        copy.wait()
        for tile in range(rows // TILE):
            factor = tile_row(masks.at[i], first // TILE + tile, width, held.dtype)
            at = pl.ds(tile * TILE, TILE)
            for part in (2 * i, 2 * i + 1):
                strip_ref[part, at, :] = held[part, at, :] * factor


def mask_strip(k_mask, p_mask, k_parts, p_parts, out_rows):
    shape, dtype = (4, out_rows, k_parts.shape[2]), k_parts.dtype
    return pl.pallas_call(
        strip_kernel,
        in_specs=[HBM] * 4,
        out_specs=VMEM,
        out_shape=jax.ShapeDtypeStruct(shape, dtype),
        scratch_shapes=[
            pltpu.VMEM(shape, dtype),
            pltpu.SMEM((2,) + k_mask.shape, k_mask.dtype),
            pltpu.SemaphoreType.DMA((2,)),
            pltpu.SemaphoreType.DMA((2,)),
        ],
        name="mask_strip",
    )(k_mask, p_mask, k_parts, p_parts)


def local_kernel(
    atoms,
    classes,
    rates,
    k_mask,
    p_mask,
    k_ref,
    p_ref,
    strip,
    near,
    share,
    damp,
    held,
    own,
    masks,
    sems,
    mask_sems,
):
    here, width = near.shape[1:]
    out_rows, share_rows = damp.shape[1], share.shape[1]
    row, col, layer = (lax.axis_index(a) for a in ("row", "col", "depth"))
    mask_copies = fetch_masks((k_mask, p_mask), masks, mask_sems)
    own_copy = pltpu.make_async_copy(strip.at[pl.ds(2, 2)], own, sems.at[2])
    copies = [
        pltpu.make_async_copy(ref, held.at[pl.ds(2 * i, 2)], sems.at[i])
        for i, ref in enumerate((p_ref, k_ref))
    ]
    for copy in copies + [own_copy]:
        copy.start()
    for copy in mask_copies:
        copy.wait()
    for i, copy in enumerate(copies):
        copy.wait()
        for tile in range(here // TILE):
            factor = tile_row(masks.at[1 - i], tile, width, held.dtype)
            at = pl.ds(tile * TILE, TILE)
            for part in (2 * i, 2 * i + 1):
                near[part, at, :] = held[part, at, :] * factor
    mine = lax.rem(layer, here // share_rows) * share_rows
    share[...] = near[:, pl.ds(pl.multiple_of(mine, share_rows), share_rows), :]
    own_copy.wait()
    lanes = lax.broadcasted_iota(jnp.int32, (1, width), 1) // TILE
    row_tiles, col_tiles = out_rows // TILE, width // TILE
    first = (row * lax.axis_size("depth") + layer) * row_tiles
    for tile in range(row_tiles):
        at = pl.ds(tile * TILE, TILE)
        atom_row = atoms[first + tile]
        gamma = jnp.zeros((1, width), jnp.float32)
        for spot in range(col_tiles):
            atom_col = atoms[col * col_tiles + spot]
            rate = jnp.where(atom_row != atom_col, rates[classes[atom_row, atom_col]], 0.0)
            gamma = jnp.where(lanes == spot, rate, gamma)
        for part in range(2):
            damp[part, at, :] = gamma * own[part, at, :].astype(jnp.float32)


def local_part(k_mask, p_mask, atoms, classes, rates, k_parts, p_parts, strip, share_rows):
    here, width = k_parts.shape[1:]
    out_rows, dtype = strip.shape[1], strip.dtype
    return pl.pallas_call(
        local_kernel,
        in_specs=[SMEM] * 3 + [HBM] * 5,
        out_specs=[VMEM] * 3,
        out_shape=[
            jax.ShapeDtypeStruct((4, here, width), dtype),
            jax.ShapeDtypeStruct((4, share_rows, width), dtype),
            jax.ShapeDtypeStruct((2, out_rows, width), jnp.float32),
        ],
        scratch_shapes=[
            pltpu.VMEM((4, here, width), dtype),
            pltpu.VMEM((2, out_rows, width), dtype),
            pltpu.SMEM((2,) + k_mask.shape, k_mask.dtype),
            pltpu.SemaphoreType.DMA((3,)),
            pltpu.SemaphoreType.DMA((2,)),
        ],
        cost_estimate=pl.CostEstimate(
            flops=8 * here * width, bytes_accessed=20 * here * width, transcendentals=0
        ),
        name="local_part",
    )(atoms, classes, rates, k_mask, p_mask, k_parts, p_parts, strip)


def place_left(left, ref, at, rows):
    k_re, k_im, p_re, p_im = ref[0], ref[1], ref[2], ref[3]
    top, low = pl.ds(0, rows), pl.ds(rows, rows)
    left[0, top, at] = k_re
    left[0, low, at] = k_im
    left[1, top, at] = -k_im
    left[1, low, at] = k_re
    left[2, top, at] = -p_re
    left[2, low, at] = -p_im
    left[3, top, at] = p_im
    left[3, low, at] = -p_re


def early_kernel(cols_n, near, own, *refs):
    ups = refs[: cols_n // 2 - 1]
    downs = refs[cols_n // 2 - 1 : -2]
    left, total_ref = refs[-2:]
    out_rows, width = own.shape[1:]
    here = near.shape[1]
    row, col = lax.axis_index("row"), lax.axis_index("col")

    def columns(shift):
        block = lax.rem(col + shift + cols_n, cols_n)
        return pl.ds(pl.multiple_of(block * width, width), width)

    place_left(left, own, columns(0), out_rows)
    for step, ref in enumerate(ups, 1):
        place_left(left, ref, columns(-step), out_rows)
    for step, ref in enumerate(downs, 1):
        place_left(left, ref, columns(step), out_rows)
    left[:, :, columns(-(cols_n // 2))] = jnp.zeros((4, 2 * out_rows, width), left.dtype)
    total = jnp.zeros((2 * out_rows, width), jnp.float32)
    at = pl.ds(pl.multiple_of(row * here, here), here)
    for slot in range(4):
        total += jnp.dot(left[slot, :, at], near[slot], preferred_element_type=jnp.float32)
    total_ref[...] = total


def early_product(near, strip, ups, downs, cols_n):
    out_rows, width = strip.shape[1:]
    left = (4, 2 * out_rows, cols_n * width)
    operands = [near, strip] + ups + downs
    return pl.pallas_call(
        functools.partial(early_kernel, cols_n),
        in_specs=[VMEM] * len(operands),
        out_specs=[VMEM, VMEM],
        out_shape=[
            jax.ShapeDtypeStruct(left, near.dtype),
            jax.ShapeDtypeStruct((2 * out_rows, width), jnp.float32),
        ],
        compiler_params=params((near.shape, 2), (left, 4), ((2 * out_rows, width), 4)),
        cost_estimate=pl.CostEstimate(
            flops=2 * 8 * out_rows * near.shape[1] * width * 40,
            bytes_accessed=left[0] * left[1] * left[2] * 4,
            transcendentals=0,
        ),
        name="early_product",
    )(*operands)


def share_place(row, layer, index, rows_n, split, here, rows):
    other = lax.rem(row - index // split - 1 + rows_n, rows_n)
    return other * here + (lax.rem(layer, split) ^ (index % split)) * rows


def add_product(total, left, at_left, right, at_right):
    value = total[...]
    for slot in range(4):
        value += jnp.dot(
            left[slot, :, at_left], right[slot, at_right, :], preferred_element_type=jnp.float32
        )
    total[...] = value


def add_last(total, left_last, rights, cols_n, width):
    start = lax.rem(lax.axis_index("col") + cols_n - cols_n // 2, cols_n) * width
    for first, ref in rights:

        @pl.when((start >= first) & (start < first + ref.shape[1]))
        def _():
            at = pl.ds(pl.multiple_of(start - first, width), width)
            add_product(total, left_last, slice(None), ref, at)


def late_kernel(rows_n, cols_n, split, near, left, early, last, *refs):
    shares = refs[:-2]
    total, left_last = refs[-2:]
    out_rows, width = last.shape[1:]
    here = near.shape[1]
    row, layer = lax.axis_index("row"), lax.axis_index("depth")
    place_left(left_last, last, pl.ds(0, width), out_rows)
    total[...] = early[...]
    rights = [(row * here, near)]
    for shift, ref in enumerate(shares):
        rows = ref.shape[1]
        first = share_place(row, layer, shift * split, rows_n, split, here, rows)
        add_product(total, left, pl.ds(pl.multiple_of(first, rows), rows), ref, slice(None))
        rights.append((first, ref))
    add_last(total, left_last, rights, cols_n, width)


def product_kernel(rows_n, cols_n, split, here, damp, left, left_last, late, *refs):
    shares = refs[:-2]
    out_ref, total = refs[-2:]
    out_rows, width = damp.shape[1:]
    row, layer = lax.axis_index("row"), lax.axis_index("depth")
    total[...] = late[...]
    rights = []
    for shift, ref in enumerate(shares):
        rows = ref.shape[1]
        first = share_place(row, layer, shift * split + 1, rows_n, split, here, rows)
        add_product(total, left, pl.ds(pl.multiple_of(first, rows), rows), ref, slice(None))
        rights.append((first, ref))
    add_last(total, left_last, rights, cols_n, width)
    out_ref[0] = total[pl.ds(out_rows, out_rows), :] - damp[0]
    out_ref[1] = -total[pl.ds(0, out_rows), :] - damp[1]


def body(k_parts, p_parts, k_mask, p_mask, atoms, classes, rates):
    rows_n, cols_n, depth = (lax.axis_size(a) for a in ("row", "col", "depth"))
    here, width = k_parts.shape[1:]
    out_rows = here // depth
    split = 2 if depth % 2 == 0 else 1
    k_mask, p_mask = k_mask.T, p_mask.T
    strip = mask_strip(k_mask, p_mask, k_parts, p_parts, out_rows)
    near, share, damp = local_part(
        k_mask, p_mask, atoms, classes, rates, k_parts, p_parts, strip, here // split
    )
    ups, downs = [strip], [strip]
    for step in range(1, cols_n // 2 + 1):
        ups.append(lax.ppermute(ups[-1], "col", [(i, (i + 1) % cols_n) for i in range(cols_n)]))
    for step in range(1, cols_n - cols_n // 2):
        downs.append(lax.ppermute(downs[-1], "col", [(i, (i - 1) % cols_n) for i in range(cols_n)]))
    direct, swapped = [], []
    for shift in range(1, rows_n):
        perm = [(i, (i + shift) % rows_n) for i in range(rows_n)]
        direct.append(lax.ppermute(share, "row", perm))
        if split == 2:
            swapped.append(lax.ppermute(direct[-1], "depth", [(i, i ^ 1) for i in range(depth)]))
    left, early = early_product(near, strip, ups[1:-1], downs[1:], cols_n)
    block, total = (4, 2 * out_rows, width), (2 * out_rows, width)
    right = (4, rows_n * here, width)
    operands = [near, left, early, ups[-1]] + direct
    late, left_last = pl.pallas_call(
        functools.partial(late_kernel, rows_n, cols_n, split),
        in_specs=[VMEM] * len(operands),
        out_specs=[VMEM, VMEM],
        out_shape=[
            jax.ShapeDtypeStruct(total, jnp.float32),
            jax.ShapeDtypeStruct(block, strip.dtype),
        ],
        compiler_params=params((right, 2), (left.shape, 2), (block, 4), (total, 12)),
        cost_estimate=pl.CostEstimate(
            flops=2 * 4 * 2 * out_rows * here * width * 40,
            bytes_accessed=8 * here * width,
            transcendentals=0,
        ),
        name="late_product",
    )(*operands)
    operands = [damp, left, left_last, late] + swapped
    return pl.pallas_call(
        functools.partial(product_kernel, rows_n, cols_n, split, here),
        in_specs=[VMEM] * len(operands),
        out_specs=VMEM,
        out_shape=jax.ShapeDtypeStruct((2, out_rows, width), jnp.float32),
        scratch_shapes=[pltpu.VMEM(total, jnp.float32)],
        compiler_params=params((right, 2), (left.shape, 2), (block, 4), (total, 16)),
        name="commutator",
    )(*operands)


def solution(mesh):
    return jax.shard_map(
        body,
        mesh=mesh,
        in_specs=(
            P(None, "row", "col"),
            P(None, "row", "col"),
            P("row", "col"),
            P("row", "col"),
            P(),
            P(),
            P(),
        ),
        out_specs=P(None, ("row", "depth"), "col"),
        check_vma=False,
    )
```

```python
import functools

import jax
import jax.numpy as jnp
from jax import lax
from jax.experimental import pallas as pl
from jax.experimental.pallas import tpu as pltpu
from jax.sharding import PartitionSpec as P

TILE = 64

HBM = pl.BlockSpec(memory_space=pltpu.HBM)
SMEM = pl.BlockSpec(memory_space=pltpu.SMEM)
VMEM = pl.BlockSpec(memory_space=pltpu.VMEM)


def params(*shapes):
    total = sum(functools.reduce(lambda a, b: a * b, s) * w for s, w in shapes)
    return pltpu.CompilerParams(vmem_limit_bytes=2 * total + (4 << 20))


def tile_row(mask_ref, tile, width, dtype):
    lanes = lax.broadcasted_iota(jnp.int32, (1, width), 1) // TILE
    row = jnp.zeros((1, width), jnp.float32)
    for place in range(width // TILE):
        row = jnp.where(lanes == place, mask_ref[place, tile].astype(jnp.float32), row)
    return row.astype(dtype)


def fetch_masks(sources, masks, sems):
    copies = [
        pltpu.make_async_copy(ref, masks.at[i], sems.at[i]) for i, ref in enumerate(sources)
    ]
    for copy in copies:
        copy.start()
    return copies


def rows_kernel(places, first_mask, second_mask, first_ref, second_ref, *refs):
    out_refs = refs[:-4]
    held, masks, sems, mask_sems = refs[-4:]
    rows, width = held.shape[1:]
    each = 4 // len(out_refs)
    first = lax.rem(lax.axis_index("depth"), places) * rows
    mask_copies = fetch_masks((first_mask, second_mask), masks, mask_sems)
    span = pl.ds(pl.multiple_of(first, rows), rows)
    copies = [
        pltpu.make_async_copy(ref.at[:, span, :], held.at[pl.ds(2 * i, 2)], sems.at[i])
        for i, ref in enumerate((first_ref, second_ref))
    ]
    for copy in copies:
        copy.start()
    for copy in mask_copies:
        copy.wait()
    for i, copy in enumerate(copies):
        copy.wait()
        for tile in range(rows // TILE):
            factor = tile_row(masks.at[i], first // TILE + tile, width, held.dtype)
            at = pl.ds(tile * TILE, TILE)
            for part in (2 * i, 2 * i + 1):
                out_refs[part // each][part % each, at, :] = held[part, at, :] * factor


def mask_rows(first_mask, second_mask, first_parts, second_parts, places, arrays, name):
    here, width = first_parts.shape[1:]
    shape, dtype = (4, here // places, width), first_parts.dtype
    return pl.pallas_call(
        functools.partial(rows_kernel, places),
        in_specs=[HBM] * 4,
        out_specs=[VMEM] * arrays,
        out_shape=[jax.ShapeDtypeStruct((4 // arrays,) + shape[1:], dtype)] * arrays,
        scratch_shapes=[
            pltpu.VMEM(shape, dtype),
            pltpu.SMEM((2,) + first_mask.shape, first_mask.dtype),
            pltpu.SemaphoreType.DMA((2,)),
            pltpu.SemaphoreType.DMA((2,)),
        ],
        name=name,
    )(first_mask, second_mask, first_parts, second_parts)


def local_kernel(
    atoms,
    classes,
    rates,
    k_mask,
    p_mask,
    k_ref,
    p_ref,
    strip,
    near,
    damp,
    held,
    own,
    masks,
    sems,
    mask_sems,
):
    here, width = near.shape[1:]
    out_rows = damp.shape[1]
    row, col, layer = (lax.axis_index(a) for a in ("row", "col", "depth"))
    mask_copies = fetch_masks((k_mask, p_mask), masks, mask_sems)
    own_copy = pltpu.make_async_copy(strip.at[pl.ds(2, 2)], own, sems.at[2])
    copies = [
        pltpu.make_async_copy(ref, held.at[pl.ds(2 * i, 2)], sems.at[i])
        for i, ref in enumerate((p_ref, k_ref))
    ]
    for copy in copies + [own_copy]:
        copy.start()
    for copy in mask_copies:
        copy.wait()
    for i, copy in enumerate(copies):
        copy.wait()
        for tile in range(here // TILE):
            factor = tile_row(masks.at[1 - i], tile, width, held.dtype)
            at = pl.ds(tile * TILE, TILE)
            for part in (2 * i, 2 * i + 1):
                near[part, at, :] = held[part, at, :] * factor
    own_copy.wait()
    lanes = lax.broadcasted_iota(jnp.int32, (1, width), 1) // TILE
    row_tiles, col_tiles = out_rows // TILE, width // TILE
    first = (row * lax.axis_size("depth") + layer) * row_tiles
    for tile in range(row_tiles):
        at = pl.ds(tile * TILE, TILE)
        atom_row = atoms[first + tile]
        gamma = jnp.zeros((1, width), jnp.float32)
        for spot in range(col_tiles):
            atom_col = atoms[col * col_tiles + spot]
            rate = jnp.where(atom_row != atom_col, rates[classes[atom_row, atom_col]], 0.0)
            gamma = jnp.where(lanes == spot, rate, gamma)
        for part in range(2):
            damp[part, at, :] = gamma * own[part, at, :].astype(jnp.float32)


def local_part(k_mask, p_mask, atoms, classes, rates, k_parts, p_parts, strip):
    here, width = k_parts.shape[1:]
    out_rows, dtype = strip.shape[1], strip.dtype
    return pl.pallas_call(
        local_kernel,
        in_specs=[SMEM] * 3 + [HBM] * 5,
        out_specs=[VMEM] * 2,
        out_shape=[
            jax.ShapeDtypeStruct((4, here, width), dtype),
            jax.ShapeDtypeStruct((2, out_rows, width), jnp.float32),
        ],
        scratch_shapes=[
            pltpu.VMEM((4, here, width), dtype),
            pltpu.VMEM((2, out_rows, width), dtype),
            pltpu.SMEM((2,) + k_mask.shape, k_mask.dtype),
            pltpu.SemaphoreType.DMA((3,)),
            pltpu.SemaphoreType.DMA((2,)),
        ],
        cost_estimate=pl.CostEstimate(
            flops=8 * here * width, bytes_accessed=20 * here * width, transcendentals=0
        ),
        name="local_part",
    )(atoms, classes, rates, k_mask, p_mask, k_parts, p_parts, strip)


def place_left(left, ref, at, rows):
    k_re, k_im, p_re, p_im = ref[0], ref[1], ref[2], ref[3]
    top, low = pl.ds(0, rows), pl.ds(rows, rows)
    left[0, top, at] = k_re
    left[0, low, at] = k_im
    left[1, top, at] = -k_im
    left[1, low, at] = k_re
    left[2, top, at] = -p_re
    left[2, low, at] = -p_im
    left[3, top, at] = p_im
    left[3, low, at] = -p_re


def share_place(row, layer, index, rows_n, split, here, rows):
    other = lax.rem(row - index // split - 1 + rows_n, rows_n)
    return other * here + (lax.rem(layer, split) ^ (index % split)) * rows


def add_product(total, left, at_left, right, at_right):
    value = total[...]
    each = 4 // len(right)
    for slot in range(4):
        value += jnp.dot(
            left[slot, :, at_left],
            right[slot // each][slot % each, at_right, :],
            preferred_element_type=jnp.float32,
        )
    total[...] = value


def early_kernel(cols_n, near, own, *refs):
    blocks = refs[:-2]
    ups, downs = blocks[: cols_n // 2 - 1], blocks[cols_n // 2 - 1 :]
    left, total = refs[-2:]
    out_rows, width = own.shape[1:]
    here = near.shape[1]
    row, col = lax.axis_index("row"), lax.axis_index("col")

    def columns(shift):
        block = lax.rem(col + shift + cols_n, cols_n)
        return pl.ds(pl.multiple_of(block * width, width), width)

    place_left(left, own, columns(0), out_rows)
    for step, ref in enumerate(ups, 1):
        place_left(left, ref, columns(-step), out_rows)
    for step, ref in enumerate(downs, 1):
        place_left(left, ref, columns(step), out_rows)
    left[:, :, columns(-(cols_n // 2))] = jnp.zeros((4, 2 * out_rows, width), left.dtype)
    total[...] = jnp.zeros_like(total)
    at = pl.ds(pl.multiple_of(row * here, here), here)
    add_product(total, left, at, [near], slice(None))


def early_product(near, strip, blocks, cols_n):
    out_rows, width = strip.shape[1:]
    here = near.shape[1]
    left, total = (4, 2 * out_rows, cols_n * width), (2 * out_rows, width)
    operands = [near, strip] + blocks
    return pl.pallas_call(
        functools.partial(early_kernel, cols_n),
        in_specs=[VMEM] * len(operands),
        out_specs=[VMEM, VMEM],
        out_shape=[
            jax.ShapeDtypeStruct(left, near.dtype),
            jax.ShapeDtypeStruct(total, jnp.float32),
        ],
        compiler_params=params((near.shape, 2), (left, 4), (total, 8)),
        cost_estimate=pl.CostEstimate(
            flops=2 * 8 * out_rows * here * width * 40,
            bytes_accessed=left[0] * left[1] * left[2] * 4,
            transcendentals=0,
        ),
        name="early_product",
    )(*operands)


def product_kernel(rows_n, cols_n, split, damp, near, left, early, last, *refs):
    shares = refs[:-3]
    out_ref, left_last, total = refs[-3:]
    out_rows, width = last.shape[1:]
    here = near.shape[1]
    row, layer = lax.axis_index("row"), lax.axis_index("depth")
    place_left(left_last, last, pl.ds(0, width), out_rows)
    total[...] = early[...]
    rights = [(row * here, here, [near])]
    for index in range(len(shares) // 2):
        pair = shares[2 * index : 2 * index + 2]
        rows = pair[0].shape[1]
        first = share_place(row, layer, index, rows_n, split, here, rows)
        rights.append((first, rows, pair))
        at = pl.ds(pl.multiple_of(first, rows), rows)
        add_product(total, left, at, pair, slice(None))
    start = lax.rem(lax.axis_index("col") + cols_n - cols_n // 2, cols_n) * width
    for first, rows, right in rights:

        @pl.when((start >= first) & (start < first + rows))
        def _():
            at = pl.ds(pl.multiple_of(start - first, width), width)
            add_product(total, left_last, slice(None), right, at)

    out_ref[0] = total[pl.ds(out_rows, out_rows), :] - damp[0]
    out_ref[1] = -total[pl.ds(0, out_rows), :] - damp[1]


def body(k_parts, p_parts, k_mask, p_mask, atoms, classes, rates):
    rows_n, cols_n, depth = (lax.axis_size(a) for a in ("row", "col", "depth"))
    here, width = k_parts.shape[1:]
    out_rows = here // depth
    split = 2 if depth % 2 == 0 else 1
    k_mask, p_mask = k_mask.T, p_mask.T
    (strip,) = mask_rows(k_mask, p_mask, k_parts, p_parts, depth, 1, "mask_strip")
    share = mask_rows(p_mask, k_mask, p_parts, k_parts, split, 2, "mask_share")
    near, damp = local_part(k_mask, p_mask, atoms, classes, rates, k_parts, p_parts, strip)
    ups, downs = [strip], [strip]
    for step in range(1, cols_n // 2 + 1):
        ups.append(lax.ppermute(ups[-1], "col", [(i, (i + 1) % cols_n) for i in range(cols_n)]))
    for step in range(1, cols_n - cols_n // 2):
        downs.append(lax.ppermute(downs[-1], "col", [(i, (i - 1) % cols_n) for i in range(cols_n)]))
    shares = []
    for shift in range(1, rows_n):
        perm = [(i, (i + shift) % rows_n) for i in range(rows_n)]
        got = [lax.ppermute(part, "row", perm) for part in share]
        shares += got
        if split == 2:
            swap = [(i, i ^ 1) for i in range(depth)]
            shares += [lax.ppermute(part, "depth", swap) for part in got]
    blocks = ups[1:-1] + downs[1:]
    left, early = early_product(near, strip, blocks, cols_n)
    operands = [damp, near, left, early, ups[-1]] + shares
    block, total = (4, 2 * out_rows, width), (2 * out_rows, width)
    return pl.pallas_call(
        functools.partial(product_kernel, rows_n, cols_n, split),
        in_specs=[VMEM] * len(operands),
        out_specs=VMEM,
        out_shape=jax.ShapeDtypeStruct((2, out_rows, width), jnp.float32),
        scratch_shapes=[pltpu.VMEM(block, strip.dtype), pltpu.VMEM(total, jnp.float32)],
        compiler_params=params((near.shape, 2 * rows_n), (left.shape, 2), (block, 4), (total, 16)),
        name="commutator",
    )(*operands)


def solution(mesh):
    return jax.shard_map(
        body,
        mesh=mesh,
        in_specs=(
            P(None, "row", "col"),
            P(None, "row", "col"),
            P("row", "col"),
            P("row", "col"),
            P(),
            P(),
            P(),
        ),
        out_specs=P(None, ("row", "depth"), "col"),
        check_vma=False,
    )
```

```python
import functools

import jax
import jax.numpy as jnp
from jax import lax
from jax.experimental import pallas as pl
from jax.experimental.pallas import tpu as pltpu
from jax.sharding import PartitionSpec as P

TILE = 64

HBM = pl.BlockSpec(memory_space=pltpu.HBM)
SMEM = pl.BlockSpec(memory_space=pltpu.SMEM)
VMEM = pl.BlockSpec(memory_space=pltpu.VMEM)


def params(*shapes):
    total = sum(functools.reduce(lambda a, b: a * b, s) * w for s, w in shapes)
    return pltpu.CompilerParams(vmem_limit_bytes=2 * total + (4 << 20))


def tile_row(mask_ref, tile, width, dtype):
    lanes = lax.broadcasted_iota(jnp.int32, (1, width), 1) // TILE
    row = jnp.zeros((1, width), jnp.float32)
    for place in range(width // TILE):
        row = jnp.where(lanes == place, mask_ref[place, tile].astype(jnp.float32), row)
    return row.astype(dtype)


def fetch_masks(sources, masks, sems):
    copies = [
        pltpu.make_async_copy(ref, masks.at[i], sems.at[i]) for i, ref in enumerate(sources)
    ]
    for copy in copies:
        copy.start()
    return copies


def rows_kernel(places, first_mask, second_mask, first_ref, second_ref, *refs):
    out_refs = refs[:-6]
    held, masked, masks, sems, out_sems, mask_sems = refs[-6:]
    rows, width = held.shape[1:]
    each = 4 // len(out_refs)
    unit = masked.shape[1]
    first = lax.rem(lax.axis_index("depth"), places) * rows
    span = pl.ds(pl.multiple_of(first, rows), rows)
    mask_copies = fetch_masks((first_mask, second_mask), masks, mask_sems)
    copies = [
        pltpu.make_async_copy(ref.at[:, span, :], held.at[pl.ds(2 * i, 2)], sems.at[i])
        for i, ref in enumerate((first_ref, second_ref))
    ]
    for copy in copies:
        copy.start()
    for copy in mask_copies:
        copy.wait()
    out_copies = []
    for i, copy in enumerate(copies):
        copy.wait()
        for tile in range(rows // TILE):
            factor = tile_row(masks.at[i], first // TILE + tile, width, held.dtype)
            at = pl.ds(tile * TILE, TILE)
            block, within = divmod(tile * TILE, unit)
            for part in range(2):
                spot = 2 * (i * (rows // unit) + block) + part
                masked[spot, pl.ds(within, TILE), :] = held[2 * i + part, at, :] * factor
        size = 2 * (rows // unit)
        target = out_refs[i] if each == 2 else out_refs[0].at[pl.ds(i * size, size)]
        out_copies.append(
            pltpu.make_async_copy(masked.at[pl.ds(i * size, size)], target, out_sems.at[i])
        )
        out_copies[-1].start()
    for copy in out_copies:
        copy.wait()


def mask_rows(first_mask, second_mask, first_parts, second_parts, places, arrays, name):
    here, width = first_parts.shape[1:]
    rows, dtype = here // places, first_parts.dtype
    unit = min(rows, width)
    count = 4 * (rows // unit)
    return pl.pallas_call(
        functools.partial(rows_kernel, places),
        in_specs=[HBM] * 4,
        out_specs=[HBM] * arrays,
        out_shape=[jax.ShapeDtypeStruct((count // arrays, unit, width), dtype)] * arrays,
        scratch_shapes=[
            pltpu.VMEM((4, rows, width), dtype),
            pltpu.VMEM((count, unit, width), dtype),
            pltpu.SMEM((2,) + first_mask.shape, first_mask.dtype),
            pltpu.SemaphoreType.DMA((2,)),
            pltpu.SemaphoreType.DMA((2,)),
            pltpu.SemaphoreType.DMA((2,)),
        ],
        name=name,
    )(first_mask, second_mask, first_parts, second_parts)


def local_kernel(
    k_mask,
    p_mask,
    atoms_ref,
    classes_ref,
    rates_ref,
    k_ref,
    p_ref,
    strip,
    near_ref,
    damp,
    held,
    near,
    own,
    masks,
    atoms,
    classes,
    rates,
    sems,
    out_sems,
    small_sems,
):
    here, width = held.shape[1:]
    out_rows = damp.shape[1]
    row, col, layer = (lax.axis_index(a) for a in ("row", "col", "depth"))
    small = fetch_masks((k_mask, p_mask), masks, small_sems)
    copies = [
        pltpu.make_async_copy(ref, held.at[pl.ds(2 * i, 2)], sems.at[i])
        for i, ref in enumerate((p_ref, k_ref))
    ]
    own_copy = pltpu.make_async_copy(strip.at[pl.ds(2, 2)], own, sems.at[2])
    tables = [
        pltpu.make_async_copy(source, target, small_sems.at[2 + i])
        for i, (source, target) in enumerate(
            ((atoms_ref, atoms), (classes_ref, classes), (rates_ref, rates))
        )
    ]
    for copy in copies + [own_copy] + tables:
        copy.start()
    for copy in small + copies:
        copy.wait()
    out_copies = []
    for block in range(here // width):
        for tile in range(block * width // TILE, (block + 1) * width // TILE):
            at, spot = pl.ds(tile * TILE, TILE), pl.ds(tile * TILE - block * width, TILE)
            for i in range(2):
                factor = tile_row(masks.at[1 - i], tile, width, held.dtype)
                for part in (2 * i, 2 * i + 1):
                    near[4 * block + part, spot, :] = held[part, at, :] * factor
        span = pl.ds(4 * block, 4)
        out_copies.append(
            pltpu.make_async_copy(near.at[span], near_ref.at[span], out_sems.at[block])
        )
        out_copies[-1].start()
    for copy in [own_copy] + tables:
        copy.wait()
    lanes = lax.broadcasted_iota(jnp.int32, (1, width), 1) // TILE
    row_tiles, col_tiles = out_rows // TILE, width // TILE
    first = (row * lax.axis_size("depth") + layer) * row_tiles
    for tile in range(row_tiles):
        at = pl.ds(tile * TILE, TILE)
        atom_row = atoms[first + tile]
        gamma = jnp.zeros((1, width), jnp.float32)
        for spot in range(col_tiles):
            atom_col = atoms[col * col_tiles + spot]
            rate = jnp.where(atom_row != atom_col, rates[classes[atom_row, atom_col]], 0.0)
            gamma = jnp.where(lanes == spot, rate, gamma)
        for part in range(2):
            damp[part, at, :] = gamma * own[part, at, :].astype(jnp.float32)
    for copy in out_copies:
        copy.wait()


def local_part(k_mask, p_mask, atoms, classes, rates, k_parts, p_parts, strip):
    here, width = k_parts.shape[1:]
    out_rows, dtype = strip.shape[1], strip.dtype
    blocks = here // width
    near = (4 * blocks, width, width)
    return pl.pallas_call(
        local_kernel,
        in_specs=[HBM] * 8,
        out_specs=[HBM, VMEM],
        out_shape=[
            jax.ShapeDtypeStruct(near, dtype),
            jax.ShapeDtypeStruct((2, out_rows, width), jnp.float32),
        ],
        scratch_shapes=[
            pltpu.VMEM((4, here, width), dtype),
            pltpu.VMEM(near, dtype),
            pltpu.VMEM((2, out_rows, width), dtype),
            pltpu.SMEM((2,) + k_mask.shape, k_mask.dtype),
            pltpu.SMEM(atoms.shape, atoms.dtype),
            pltpu.SMEM(classes.shape, classes.dtype),
            pltpu.SMEM(rates.shape, rates.dtype),
            pltpu.SemaphoreType.DMA((3,)),
            pltpu.SemaphoreType.DMA((blocks,)),
            pltpu.SemaphoreType.DMA((5,)),
        ],
        cost_estimate=pl.CostEstimate(
            flops=8 * here * width, bytes_accessed=20 * here * width, transcendentals=0
        ),
        name="local_part",
    )(k_mask, p_mask, atoms, classes, rates, k_parts, p_parts, strip)


def place_left(left, ref, block):
    rows, width = ref.shape[1:]
    k_re, k_im, p_re, p_im = ref[0], ref[1], ref[2], ref[3]
    for half, parts in enumerate(((k_re, -k_im, -p_re, p_im), (k_im, k_re, -p_im, -p_re))):
        for slot, part in enumerate(parts):
            at = pl.multiple_of((4 * block + slot) * width, width)
            left[pl.ds(half * rows, rows), pl.ds(at, width)] = part


def share_block(row, layer, index, rows_n, split, here, size):
    other = lax.rem(row - index // split - 1 + rows_n, rows_n)
    return other * here + (lax.rem(layer, split) ^ (index % split)) * size


def products(left, block, right, first, count):
    each = 4 // len(right)
    width = right[0].shape[1]
    steps = [(0, count)] if each == 4 else [(step, 1) for step in range(count)]
    found = []
    for step, size in steps:
        for half, ref in enumerate(right):
            at = pl.multiple_of((4 * (block + step) + half * each) * width, width)
            value = ref[pl.ds((first + step) * each, size * each)]
            found.append(
                jnp.dot(
                    left[:, pl.ds(at, size * each * width)],
                    value.reshape(size * each * width, width),
                    preferred_element_type=jnp.float32,
                )
            )
    return sum(found[1:], found[0])


def early_kernel(cols_n, near, own, *refs):
    blocks = refs[:-2]
    ups, downs = blocks[: cols_n // 2 - 1], blocks[cols_n // 2 - 1 :]
    left, total = refs[-2:]
    width = own.shape[2]
    row, col = lax.axis_index("row"), lax.axis_index("col")
    place_left(left, own, col)
    for step, ref in enumerate(ups, 1):
        place_left(left, ref, lax.rem(col - step + cols_n, cols_n))
    for step, ref in enumerate(downs, 1):
        place_left(left, ref, lax.rem(col + step, cols_n))
    last = pl.multiple_of(lax.rem(col + cols_n - cols_n // 2, cols_n) * 4 * width, width)
    left[:, pl.ds(last, 4 * width)] = jnp.zeros((left.shape[0], 4 * width), left.dtype)
    count = near.shape[0] // 4
    total[...] = products(left, row * count, [near], 0, count)


def early_product(near, strip, blocks, cols_n):
    out_rows, width = strip.shape[1:]
    left, total = (2 * out_rows, cols_n * 4 * width), (2 * out_rows, width)
    operands = [near, strip] + blocks
    return pl.pallas_call(
        functools.partial(early_kernel, cols_n),
        in_specs=[VMEM] * len(operands),
        out_specs=[VMEM, VMEM],
        out_shape=[
            jax.ShapeDtypeStruct(left, near.dtype),
            jax.ShapeDtypeStruct(total, jnp.float32),
        ],
        compiler_params=params((near.shape, 2), (left, 4), (total, 8)),
        cost_estimate=pl.CostEstimate(
            flops=4 * out_rows * near.shape[0] * width * width * 40,
            bytes_accessed=left[0] * left[1] * 4,
            transcendentals=0,
        ),
        name="early_product",
    )(*operands)


def product_kernel(rows_n, cols_n, split, damp, near, left, early, last, *refs):
    shares = refs[:-3]
    out_ref, left_last, total = refs[-3:]
    out_rows = last.shape[1]
    row, layer = lax.axis_index("row"), lax.axis_index("depth")
    place_left(left_last, last, 0)
    here = near.shape[0] // 4
    rights = [(row * here, here, [near])]
    value = early[...]
    for index in range(len(shares) // 2):
        pair = shares[2 * index : 2 * index + 2]
        size = pair[0].shape[0] // 2
        block = share_block(row, layer, index, rows_n, split, here, size)
        rights.append((block, size, pair))
        value += products(left, block, pair, 0, size)
    total[...] = value
    wanted = lax.rem(lax.axis_index("col") + cols_n - cols_n // 2, cols_n)
    for block, size, right in rights:

        @pl.when((wanted >= block) & (wanted < block + size))
        def _():
            total[...] += products(left_last, 0, right, wanted - block, 1)

    out_ref[0] = total[pl.ds(out_rows, out_rows), :] - damp[0]
    out_ref[1] = -total[pl.ds(0, out_rows), :] - damp[1]


def body(k_parts, p_parts, k_mask, p_mask, atoms, classes, rates):
    rows_n, cols_n, depth = (lax.axis_size(a) for a in ("row", "col", "depth"))
    here, width = k_parts.shape[1:]
    out_rows = here // depth
    split = 2 if depth % 2 == 0 else 1
    k_mask, p_mask = k_mask.T, p_mask.T
    (strip,) = mask_rows(k_mask, p_mask, k_parts, p_parts, depth, 1, "mask_strip")
    share = mask_rows(p_mask, k_mask, p_parts, k_parts, split, 2, "mask_share")
    ups, downs = [strip], [strip]
    for step in range(1, cols_n // 2 + 1):
        ups.append(lax.ppermute(ups[-1], "col", [(i, (i + 1) % cols_n) for i in range(cols_n)]))
    for step in range(1, cols_n - cols_n // 2):
        downs.append(lax.ppermute(downs[-1], "col", [(i, (i - 1) % cols_n) for i in range(cols_n)]))
    near, damp = local_part(
        k_mask, p_mask, atoms, classes, rates, k_parts, p_parts, strip
    )
    shares = []
    for shift in range(1, rows_n):
        perm = [(i, (i + shift) % rows_n) for i in range(rows_n)]
        got = [lax.ppermute(part, "row", perm) for part in share]
        shares += got
        if split == 2:
            swap = [(i, i ^ 1) for i in range(depth)]
            shares += [lax.ppermute(part, "depth", swap) for part in got]
    blocks = ups[1:-1] + downs[1:]
    left, early = early_product(near, strip, blocks, cols_n)
    operands = [damp, near, left, early, ups[-1]] + shares
    block, total = (2 * out_rows, 4 * width), (2 * out_rows, width)
    return pl.pallas_call(
        functools.partial(product_kernel, rows_n, cols_n, split),
        in_specs=[VMEM] * len(operands),
        out_specs=VMEM,
        out_shape=jax.ShapeDtypeStruct((2, out_rows, width), jnp.float32),
        scratch_shapes=[pltpu.VMEM(block, strip.dtype), pltpu.VMEM(total, jnp.float32)],
        compiler_params=params((near.shape, 2 * rows_n), (left.shape, 2), (block, 4), (total, 16)),
        name="commutator",
    )(*operands)


def solution(mesh):
    return jax.shard_map(
        body,
        mesh=mesh,
        in_specs=(
            P(None, "row", "col"),
            P(None, "row", "col"),
            P("row", "col"),
            P("row", "col"),
            P(),
            P(),
            P(),
        ),
        out_specs=P(None, ("row", "depth"), "col"),
        check_vma=False,
    )
```

```python
import functools

import jax
import jax.numpy as jnp
from jax import lax
from jax.experimental import pallas as pl
from jax.experimental.pallas import tpu as pltpu
from jax.sharding import PartitionSpec as P

TILE = 64

HBM = pl.BlockSpec(memory_space=pltpu.HBM)
SMEM = pl.BlockSpec(memory_space=pltpu.SMEM)
VMEM = pl.BlockSpec(memory_space=pltpu.VMEM)


def params(*shapes):
    total = sum(functools.reduce(lambda a, b: a * b, s) * w for s, w in shapes)
    return pltpu.CompilerParams(vmem_limit_bytes=2 * total + (4 << 20))


def tile_row(mask_ref, tile, width, dtype):
    lanes = lax.broadcasted_iota(jnp.int32, (1, width), 1) // TILE
    row = jnp.zeros((1, width), jnp.float32)
    for place in range(width // TILE):
        row = jnp.where(lanes == place, mask_ref[place, tile].astype(jnp.float32), row)
    return row.astype(dtype)


def fetch_masks(sources, masks, sems):
    copies = [
        pltpu.make_async_copy(ref, masks.at[i], sems.at[i]) for i, ref in enumerate(sources)
    ]
    for copy in copies:
        copy.start()
    return copies


def rows_kernel(places, first_mask, second_mask, first_ref, second_ref, *refs):
    out_refs = refs[:-6]
    held, masked, masks, sems, out_sems, mask_sems = refs[-6:]
    rows, width = held.shape[1:]
    each = 4 // len(out_refs)
    unit = masked.shape[1]
    first = lax.rem(lax.axis_index("depth"), places) * rows
    span = pl.ds(pl.multiple_of(first, rows), rows)
    mask_copies = fetch_masks((first_mask, second_mask), masks, mask_sems)
    copies = [
        pltpu.make_async_copy(ref.at[:, span, :], held.at[pl.ds(2 * i, 2)], sems.at[i])
        for i, ref in enumerate((first_ref, second_ref))
    ]
    for copy in copies:
        copy.start()
    for copy in mask_copies:
        copy.wait()
    out_copies = []
    for i, copy in enumerate(copies):
        copy.wait()
        for tile in range(rows // TILE):
            factor = tile_row(masks.at[i], first // TILE + tile, width, held.dtype)
            at = pl.ds(tile * TILE, TILE)
            block, within = divmod(tile * TILE, unit)
            for part in range(2):
                spot = 2 * (i * (rows // unit) + block) + part
                masked[spot, pl.ds(within, TILE), :] = held[2 * i + part, at, :] * factor
        size = 2 * (rows // unit)
        target = out_refs[i] if each == 2 else out_refs[0].at[pl.ds(i * size, size)]
        out_copies.append(
            pltpu.make_async_copy(masked.at[pl.ds(i * size, size)], target, out_sems.at[i])
        )
        out_copies[-1].start()
    for copy in out_copies:
        copy.wait()


def mask_rows(first_mask, second_mask, first_parts, second_parts, places, arrays, name):
    here, width = first_parts.shape[1:]
    rows, dtype = here // places, first_parts.dtype
    unit = min(rows, width)
    count = 4 * (rows // unit)
    return pl.pallas_call(
        functools.partial(rows_kernel, places),
        in_specs=[HBM] * 4,
        out_specs=[HBM] * arrays,
        out_shape=[jax.ShapeDtypeStruct((count // arrays, unit, width), dtype)] * arrays,
        scratch_shapes=[
            pltpu.VMEM((4, rows, width), dtype),
            pltpu.VMEM((count, unit, width), dtype),
            pltpu.SMEM((2,) + first_mask.shape, first_mask.dtype),
            pltpu.SemaphoreType.DMA((2,)),
            pltpu.SemaphoreType.DMA((2,)),
            pltpu.SemaphoreType.DMA((2,)),
        ],
        name=name,
    )(first_mask, second_mask, first_parts, second_parts)


def local_kernel(
    k_mask,
    p_mask,
    atoms_ref,
    classes_ref,
    rates_ref,
    k_ref,
    p_ref,
    strip,
    near_ref,
    damp,
    held,
    near,
    own,
    masks,
    atoms,
    classes,
    rates,
    sems,
    out_sems,
    small_sems,
):
    here, width = held.shape[1:]
    out_rows = damp.shape[1]
    row, col, layer = (lax.axis_index(a) for a in ("row", "col", "depth"))
    small = fetch_masks((k_mask, p_mask), masks, small_sems)
    copies = [
        pltpu.make_async_copy(ref, held.at[pl.ds(2 * i, 2)], sems.at[i])
        for i, ref in enumerate((p_ref, k_ref))
    ]
    own_copy = pltpu.make_async_copy(strip.at[pl.ds(2, 2)], own, sems.at[2])
    tables = [
        pltpu.make_async_copy(source, target, small_sems.at[2 + i])
        for i, (source, target) in enumerate(
            ((atoms_ref, atoms), (classes_ref, classes), (rates_ref, rates))
        )
    ]
    for copy in copies + [own_copy] + tables:
        copy.start()
    for copy in small + copies:
        copy.wait()
    out_copies = []
    for block in range(here // width):
        for tile in range(block * width // TILE, (block + 1) * width // TILE):
            at, spot = pl.ds(tile * TILE, TILE), pl.ds(tile * TILE - block * width, TILE)
            for i in range(2):
                factor = tile_row(masks.at[1 - i], tile, width, held.dtype)
                for part in (2 * i, 2 * i + 1):
                    near[4 * block + part, spot, :] = held[part, at, :] * factor
        span = pl.ds(4 * block, 4)
        out_copies.append(
            pltpu.make_async_copy(near.at[span], near_ref.at[span], out_sems.at[block])
        )
        out_copies[-1].start()
    for copy in [own_copy] + tables:
        copy.wait()
    lanes = lax.broadcasted_iota(jnp.int32, (1, width), 1) // TILE
    row_tiles, col_tiles = out_rows // TILE, width // TILE
    first = (row * lax.axis_size("depth") + layer) * row_tiles
    for tile in range(row_tiles):
        at = pl.ds(tile * TILE, TILE)
        atom_row = atoms[first + tile]
        gamma = jnp.zeros((1, width), jnp.float32)
        for spot in range(col_tiles):
            atom_col = atoms[col * col_tiles + spot]
            rate = jnp.where(atom_row != atom_col, rates[classes[atom_row, atom_col]], 0.0)
            gamma = jnp.where(lanes == spot, rate, gamma)
        for part in range(2):
            damp[part, at, :] = gamma * own[part, at, :].astype(jnp.float32)
    for copy in out_copies:
        copy.wait()


def local_part(k_mask, p_mask, atoms, classes, rates, k_parts, p_parts, strip):
    here, width = k_parts.shape[1:]
    out_rows, dtype = strip.shape[1], strip.dtype
    blocks = here // width
    near = (4 * blocks, width, width)
    return pl.pallas_call(
        local_kernel,
        in_specs=[HBM] * 8,
        out_specs=[HBM, VMEM],
        out_shape=[
            jax.ShapeDtypeStruct(near, dtype),
            jax.ShapeDtypeStruct((2, out_rows, width), jnp.float32),
        ],
        scratch_shapes=[
            pltpu.VMEM((4, here, width), dtype),
            pltpu.VMEM(near, dtype),
            pltpu.VMEM((2, out_rows, width), dtype),
            pltpu.SMEM((2,) + k_mask.shape, k_mask.dtype),
            pltpu.SMEM(atoms.shape, atoms.dtype),
            pltpu.SMEM(classes.shape, classes.dtype),
            pltpu.SMEM(rates.shape, rates.dtype),
            pltpu.SemaphoreType.DMA((3,)),
            pltpu.SemaphoreType.DMA((blocks,)),
            pltpu.SemaphoreType.DMA((5,)),
        ],
        cost_estimate=pl.CostEstimate(
            flops=8 * here * width, bytes_accessed=20 * here * width, transcendentals=0
        ),
        name="local_part",
    )(k_mask, p_mask, atoms, classes, rates, k_parts, p_parts, strip)


def place_left(left, ref, block):
    rows, width = ref.shape[1:]
    k_re, k_im, p_re, p_im = ref[0], ref[1], ref[2], ref[3]
    for half, parts in enumerate(((k_re, -k_im, -p_re, p_im), (k_im, k_re, -p_im, -p_re))):
        for slot, part in enumerate(parts):
            at = pl.multiple_of((4 * block + slot) * width, width)
            left[pl.ds(half * rows, rows), pl.ds(at, width)] = part


def relay_kernel(block, out):
    out[...] = block[...]


def relay(block):
    return pl.pallas_call(
        relay_kernel,
        in_specs=[VMEM],
        out_specs=VMEM,
        out_shape=jax.ShapeDtypeStruct(block.shape, block.dtype),
        compiler_params=params((block.shape, 4)),
        cost_estimate=pl.CostEstimate(
            flops=100000000, bytes_accessed=4 * block.size, transcendentals=0
        ),
        name="relay",
    )(block)


def share_block(row, layer, index, rows_n, split, here, size):
    other = lax.rem(row - index // split - 1 + rows_n, rows_n)
    return other * here + (lax.rem(layer, split) ^ (index % split)) * size


def products(left, block, right, first, count):
    each = 4 // len(right)
    width = right[0].shape[1]
    steps = [(0, count)] if each == 4 else [(step, 1) for step in range(count)]
    found = []
    for step, size in steps:
        for half, ref in enumerate(right):
            at = pl.multiple_of((4 * (block + step) + half * each) * width, width)
            value = ref[pl.ds((first + step) * each, size * each)]
            found.append(
                jnp.dot(
                    left[:, pl.ds(at, size * each * width)],
                    value.reshape(size * each * width, width),
                    preferred_element_type=jnp.float32,
                )
            )
    return sum(found[1:], found[0])


def early_kernel(cols_n, near, own, *refs):
    blocks = refs[:-2]
    ups, downs = blocks[: cols_n // 2 - 1], blocks[cols_n // 2 - 1 :]
    left, total = refs[-2:]
    width = own.shape[2]
    row, col = lax.axis_index("row"), lax.axis_index("col")
    place_left(left, own, col)
    for step, ref in enumerate(ups, 1):
        place_left(left, ref, lax.rem(col - step + cols_n, cols_n))
    for step, ref in enumerate(downs, 1):
        place_left(left, ref, lax.rem(col + step, cols_n))
    last = pl.multiple_of(lax.rem(col + cols_n - cols_n // 2, cols_n) * 4 * width, width)
    left[:, pl.ds(last, 4 * width)] = jnp.zeros((left.shape[0], 4 * width), left.dtype)
    count = near.shape[0] // 4
    total[...] = products(left, row * count, [near], 0, count)


def early_product(near, strip, blocks, cols_n):
    out_rows, width = strip.shape[1:]
    left, total = (2 * out_rows, cols_n * 4 * width), (2 * out_rows, width)
    operands = [near, strip] + blocks
    return pl.pallas_call(
        functools.partial(early_kernel, cols_n),
        in_specs=[VMEM] * len(operands),
        out_specs=[VMEM, VMEM],
        out_shape=[
            jax.ShapeDtypeStruct(left, near.dtype),
            jax.ShapeDtypeStruct(total, jnp.float32),
        ],
        compiler_params=params((near.shape, 2), (left, 4), (total, 8)),
        cost_estimate=pl.CostEstimate(
            flops=4 * out_rows * near.shape[0] * width * width * 40,
            bytes_accessed=left[0] * left[1] * 4,
            transcendentals=0,
        ),
        name="early_product",
    )(*operands)


def shares_kernel(rows_n, split, here, left, early, *refs):
    shares, total = refs[:-1], refs[-1]
    row, layer = lax.axis_index("row"), lax.axis_index("depth")
    value = early[...]
    for index in range(len(shares) // 2):
        pair = shares[2 * index : 2 * index + 2]
        size = pair[0].shape[0] // 2
        block = share_block(row, layer, index, rows_n, split, here, size)
        value += products(left, block, pair, 0, size)
    total[...] = value


def shares_product(left, early, shares, rows_n, split, here):
    operands = [left, early] + shares
    return pl.pallas_call(
        functools.partial(shares_kernel, rows_n, split, here),
        in_specs=[VMEM] * len(operands),
        out_specs=VMEM,
        out_shape=jax.ShapeDtypeStruct(early.shape, early.dtype),
        compiler_params=params((left.shape, 4), (early.shape, 12)),
        cost_estimate=pl.CostEstimate(flops=1000000, bytes_accessed=1000000, transcendentals=0),
        name="shares_product",
    )(*operands)


def product_kernel(rows_n, cols_n, split, damp, near, middle, last, *refs):
    shares = refs[:-3]
    out_ref, left_last, total = refs[-3:]
    out_rows = last.shape[1]
    row, layer = lax.axis_index("row"), lax.axis_index("depth")
    place_left(left_last, last, 0)
    here = near.shape[0] // 4
    rights = [(row * here, here, [near])]
    for index in range(len(shares) // 2):
        pair = shares[2 * index : 2 * index + 2]
        size = pair[0].shape[0] // 2
        block = share_block(row, layer, index, rows_n, split, here, size)
        rights.append((block, size, pair))
    wanted = lax.rem(lax.axis_index("col") + cols_n - cols_n // 2, cols_n)
    for block, size, right in rights:

        @pl.when((wanted >= block) & (wanted < block + size))
        def _():
            total[...] = middle[...] + products(left_last, 0, right, wanted - block, 1)

    out_ref[0] = total[pl.ds(out_rows, out_rows), :] - damp[0]
    out_ref[1] = -total[pl.ds(0, out_rows), :] - damp[1]


def body(k_parts, p_parts, k_mask, p_mask, atoms, classes, rates):
    rows_n, cols_n, depth = (lax.axis_size(a) for a in ("row", "col", "depth"))
    here, width = k_parts.shape[1:]
    out_rows = here // depth
    split = 2 if depth % 2 == 0 else 1
    k_mask, p_mask = k_mask.T, p_mask.T
    (strip,) = mask_rows(k_mask, p_mask, k_parts, p_parts, depth, 1, "mask_strip")
    share = mask_rows(p_mask, k_mask, p_parts, k_parts, split, 2, "mask_share")
    ups, downs = [strip], [strip]
    for step in range(1, cols_n // 2 + 1):
        block = ups[-1] if step == 1 else relay(ups[-1])
        ups.append(lax.ppermute(block, "col", [(i, (i + 1) % cols_n) for i in range(cols_n)]))
    for step in range(1, cols_n - cols_n // 2):
        downs.append(lax.ppermute(downs[-1], "col", [(i, (i - 1) % cols_n) for i in range(cols_n)]))
    near, damp = local_part(
        k_mask, p_mask, atoms, classes, rates, k_parts, p_parts, strip
    )
    shares = []
    for shift in range(1, rows_n):
        perm = [(i, (i + shift) % rows_n) for i in range(rows_n)]
        got = [lax.ppermute(part, "row", perm) for part in share]
        shares += got
        if split == 2:
            swap = [(i, i ^ 1) for i in range(depth)]
            shares += [lax.ppermute(part, "depth", swap) for part in got]
    blocks = ups[1:-1] + downs[1:]
    left, early = early_product(near, strip, blocks, cols_n)
    middle = shares_product(left, early, shares, rows_n, split, here // width)
    operands = [damp, near, middle, ups[-1]] + shares
    block, total = (2 * out_rows, 4 * width), (2 * out_rows, width)
    return pl.pallas_call(
        functools.partial(product_kernel, rows_n, cols_n, split),
        in_specs=[VMEM] * len(operands),
        out_specs=VMEM,
        out_shape=jax.ShapeDtypeStruct((2, out_rows, width), jnp.float32),
        scratch_shapes=[pltpu.VMEM(block, strip.dtype), pltpu.VMEM(total, jnp.float32)],
        compiler_params=params((near.shape, 2 * rows_n), (left.shape, 2), (block, 4), (total, 16)),
        name="commutator",
    )(*operands)


def solution(mesh):
    return jax.shard_map(
        body,
        mesh=mesh,
        in_specs=(
            P(None, "row", "col"),
            P(None, "row", "col"),
            P("row", "col"),
            P("row", "col"),
            P(),
            P(),
            P(),
        ),
        out_specs=P(None, ("row", "depth"), "col"),
        check_vma=False,
    )
```

```python
import functools

import jax
import jax.numpy as jnp
from jax import lax
from jax.experimental import pallas as pl
from jax.experimental.pallas import tpu as pltpu
from jax.sharding import PartitionSpec as P

TILE = 64

HBM = pl.BlockSpec(memory_space=pltpu.HBM)
SMEM = pl.BlockSpec(memory_space=pltpu.SMEM)
VMEM = pl.BlockSpec(memory_space=pltpu.VMEM)


def params(*shapes):
    total = sum(functools.reduce(lambda a, b: a * b, s) * w for s, w in shapes)
    return pltpu.CompilerParams(vmem_limit_bytes=2 * total + (4 << 20))


def tile_row(mask_ref, tile, width, dtype):
    lanes = lax.broadcasted_iota(jnp.int32, (1, width), 1) // TILE
    row = jnp.zeros((1, width), jnp.float32)
    for place in range(width // TILE):
        row = jnp.where(lanes == place, mask_ref[place, tile].astype(jnp.float32), row)
    return row.astype(dtype)


def fetch_masks(sources, masks, sems):
    copies = [
        pltpu.make_async_copy(ref, masks.at[i], sems.at[i]) for i, ref in enumerate(sources)
    ]
    for copy in copies:
        copy.start()
    return copies


def rows_kernel(places, first_mask, second_mask, first_ref, second_ref, *refs):
    out_refs = refs[:-6]
    held, masked, masks, sems, out_sems, mask_sems = refs[-6:]
    rows, width = held.shape[1:]
    count = out_refs[0].shape[0]
    unit = masked.shape[1]
    first = lax.rem(lax.axis_index("depth"), places) * rows
    mask_copies = fetch_masks((first_mask, second_mask), masks, mask_sems)
    copies = []
    for i, ref in enumerate((first_ref, second_ref)):
        for tile in range(rows // TILE):
            for part in range(2):
                slot, to = 2 * i + part, pl.ds(tile * TILE, TILE)
                at = pl.ds(pl.multiple_of(first + tile * TILE, TILE), TILE)
                copies.append(
                    pltpu.make_async_copy(
                        ref.at[part, at], held.at[slot, to], sems.at[len(copies)]
                    )
                )
                copies[-1].start()
    for copy in mask_copies:
        copy.wait()
    out_copies = []
    for i in range(2):
        for tile in range(rows // TILE):
            factor = tile_row(masks.at[i], first // TILE + tile, width, held.dtype)
            at = pl.ds(tile * TILE, TILE)
            block, within = divmod(tile * TILE, unit)
            to = pl.ds(within, TILE)
            for part in range(2):
                copies[len(out_copies)].wait()
                spot = 2 * (i * (rows // unit) + block) + part
                masked[spot, to, :] = held[2 * i + part, at, :] * factor
                target = out_refs[spot // count].at[spot % count, to]
                out_copies.append(
                    pltpu.make_async_copy(
                        masked.at[spot, to], target, out_sems.at[len(out_copies)]
                    )
                )
                out_copies[-1].start()
    for copy in out_copies:
        copy.wait()


def mask_rows(first_mask, second_mask, first_parts, second_parts, places, arrays, name):
    here, width = first_parts.shape[1:]
    rows, dtype = here // places, first_parts.dtype
    unit = min(rows, width)
    count = 4 * (rows // unit)
    return pl.pallas_call(
        functools.partial(rows_kernel, places),
        in_specs=[HBM] * 4,
        out_specs=[HBM] * arrays,
        out_shape=[jax.ShapeDtypeStruct((count // arrays, unit, width), dtype)] * arrays,
        scratch_shapes=[
            pltpu.VMEM((4, rows, width), dtype),
            pltpu.VMEM((count, unit, width), dtype),
            pltpu.SMEM((2,) + first_mask.shape, first_mask.dtype),
            pltpu.SemaphoreType.DMA((4 * (rows // TILE),)),
            pltpu.SemaphoreType.DMA((4 * (rows // TILE),)),
            pltpu.SemaphoreType.DMA((2,)),
        ],
        name=name,
    )(first_mask, second_mask, first_parts, second_parts)


def local_kernel(
    k_mask,
    p_mask,
    atoms_ref,
    classes_ref,
    rates_ref,
    k_ref,
    p_ref,
    strip,
    near_ref,
    damp,
    held,
    near,
    own,
    masks,
    atoms,
    classes,
    rates,
    sems,
    out_sems,
    small_sems,
):
    here, width = held.shape[1:]
    out_rows = damp.shape[1]
    row, col, layer = (lax.axis_index(a) for a in ("row", "col", "depth"))
    small = fetch_masks((k_mask, p_mask), masks, small_sems)
    half = width // 2
    copies = [
        pltpu.make_async_copy(
            ref.at[part, pl.ds(start, half)],
            held.at[2 * i + part, pl.ds(start, half)],
            sems.at[1 + 4 * (start // half) + 2 * i + part],
        )
        for start in range(0, here, half)
        for i, ref in enumerate((p_ref, k_ref))
        for part in range(2)
    ]
    own_copy = pltpu.make_async_copy(strip.at[pl.ds(2, 2)], own, sems.at[0])
    tables = [
        pltpu.make_async_copy(source, target, small_sems.at[2 + i])
        for i, (source, target) in enumerate(
            ((atoms_ref, atoms), (classes_ref, classes), (rates_ref, rates))
        )
    ]
    for copy in copies + [own_copy] + tables:
        copy.start()
    for copy in small:
        copy.wait()
    out_copies = []
    for step in range(here // half):
        for copy in copies[4 * step : 4 * step + 4]:
            copy.wait()
        block, within = divmod(step * half, width)
        for tile in range(step * half // TILE, (step + 1) * half // TILE):
            at, spot = pl.ds(tile * TILE, TILE), pl.ds(tile * TILE - block * width, TILE)
            for i in range(2):
                factor = tile_row(masks.at[1 - i], tile, width, held.dtype)
                for part in (2 * i, 2 * i + 1):
                    near[4 * block + part, spot, :] = held[part, at, :] * factor
        for part in range(4):
            place = (4 * block + part, pl.ds(within, half))
            out_copies.append(
                pltpu.make_async_copy(
                    near.at[place], near_ref.at[place], out_sems.at[len(out_copies)]
                )
            )
            out_copies[-1].start()
    for copy in [own_copy] + tables:
        copy.wait()
    lanes = lax.broadcasted_iota(jnp.int32, (1, width), 1) // TILE
    row_tiles, col_tiles = out_rows // TILE, width // TILE
    first = (row * lax.axis_size("depth") + layer) * row_tiles
    for tile in range(row_tiles):
        at = pl.ds(tile * TILE, TILE)
        atom_row = atoms[first + tile]
        gamma = jnp.zeros((1, width), jnp.float32)
        for spot in range(col_tiles):
            atom_col = atoms[col * col_tiles + spot]
            rate = jnp.where(atom_row != atom_col, rates[classes[atom_row, atom_col]], 0.0)
            gamma = jnp.where(lanes == spot, rate, gamma)
        for part in range(2):
            damp[part, at, :] = gamma * own[part, at, :].astype(jnp.float32)
    for copy in out_copies:
        copy.wait()


def local_part(k_mask, p_mask, atoms, classes, rates, k_parts, p_parts, strip):
    here, width = k_parts.shape[1:]
    out_rows, dtype = strip.shape[1], strip.dtype
    blocks = here // width
    near = (4 * blocks, width, width)
    return pl.pallas_call(
        local_kernel,
        in_specs=[HBM] * 8,
        out_specs=[HBM, VMEM],
        out_shape=[
            jax.ShapeDtypeStruct(near, dtype),
            jax.ShapeDtypeStruct((2, out_rows, width), jnp.float32),
        ],
        scratch_shapes=[
            pltpu.VMEM((4, here, width), dtype),
            pltpu.VMEM(near, dtype),
            pltpu.VMEM((2, out_rows, width), dtype),
            pltpu.SMEM((2,) + k_mask.shape, k_mask.dtype),
            pltpu.SMEM(atoms.shape, atoms.dtype),
            pltpu.SMEM(classes.shape, classes.dtype),
            pltpu.SMEM(rates.shape, rates.dtype),
            pltpu.SemaphoreType.DMA((1 + 8 * blocks,)),
            pltpu.SemaphoreType.DMA((8 * blocks,)),
            pltpu.SemaphoreType.DMA((5,)),
        ],
        cost_estimate=pl.CostEstimate(
            flops=8 * here * width, bytes_accessed=20 * here * width, transcendentals=0
        ),
        name="local_part",
    )(k_mask, p_mask, atoms, classes, rates, k_parts, p_parts, strip)


def place_left(left, ref, block):
    rows, width = ref.shape[1:]
    k_re, k_im, p_re, p_im = ref[0], ref[1], ref[2], ref[3]
    for half, parts in enumerate(((k_re, -k_im, -p_re, p_im), (k_im, k_re, -p_im, -p_re))):
        for slot, part in enumerate(parts):
            at = pl.multiple_of((4 * block + slot) * width, width)
            left[pl.ds(half * rows, rows), pl.ds(at, width)] = part


def relay_kernel(block, out):
    out[...] = block[...]


def relay(block):
    return pl.pallas_call(
        relay_kernel,
        in_specs=[VMEM],
        out_specs=VMEM,
        out_shape=jax.ShapeDtypeStruct(block.shape, block.dtype),
        compiler_params=params((block.shape, 4)),
        cost_estimate=pl.CostEstimate(
            flops=100000000, bytes_accessed=4 * block.size, transcendentals=0
        ),
        name="relay",
    )(block)


def share_block(row, layer, index, rows_n, split, here, size):
    other = lax.rem(row - index // split - 1 + rows_n, rows_n)
    return other * here + (lax.rem(layer, split) ^ (index % split)) * size


def products(left, block, right, first, count):
    each = 4 // len(right)
    width = right[0].shape[1]
    steps = [(0, count)] if each == 4 else [(step, 1) for step in range(count)]
    found = []
    for step, size in steps:
        for half, ref in enumerate(right):
            at = pl.multiple_of((4 * (block + step) + half * each) * width, width)
            value = ref[pl.ds((first + step) * each, size * each)]
            found.append(
                jnp.dot(
                    left[:, pl.ds(at, size * each * width)],
                    value.reshape(size * each * width, width),
                    preferred_element_type=jnp.float32,
                )
            )
    return sum(found[1:], found[0])


def early_kernel(cols_n, near, own, *refs):
    blocks = refs[:-2]
    ups, downs = blocks[: cols_n // 2 - 1], blocks[cols_n // 2 - 1 :]
    left, total = refs[-2:]
    width = own.shape[2]
    row, col = lax.axis_index("row"), lax.axis_index("col")
    place_left(left, own, col)
    for step, ref in enumerate(ups, 1):
        place_left(left, ref, lax.rem(col - step + cols_n, cols_n))
    for step, ref in enumerate(downs, 1):
        place_left(left, ref, lax.rem(col + step, cols_n))
    last = pl.multiple_of(lax.rem(col + cols_n - cols_n // 2, cols_n) * 4 * width, width)
    left[:, pl.ds(last, 4 * width)] = jnp.zeros((left.shape[0], 4 * width), left.dtype)
    count = near.shape[0] // 4
    total[...] = products(left, row * count, [near], 0, count)


def early_product(near, strip, blocks, cols_n):
    out_rows, width = strip.shape[1:]
    left, total = (2 * out_rows, cols_n * 4 * width), (2 * out_rows, width)
    operands = [near, strip] + blocks
    return pl.pallas_call(
        functools.partial(early_kernel, cols_n),
        in_specs=[VMEM] * len(operands),
        out_specs=[VMEM, VMEM],
        out_shape=[
            jax.ShapeDtypeStruct(left, near.dtype),
            jax.ShapeDtypeStruct(total, jnp.float32),
        ],
        compiler_params=params((near.shape, 2), (left, 4), (total, 8)),
        cost_estimate=pl.CostEstimate(
            flops=4 * out_rows * near.shape[0] * width * width * 40,
            bytes_accessed=left[0] * left[1] * 4,
            transcendentals=0,
        ),
        name="early_product",
    )(*operands)


def shares_kernel(rows_n, split, here, left, early, *refs):
    shares, total = refs[:-1], refs[-1]
    row, layer = lax.axis_index("row"), lax.axis_index("depth")
    value = early[...]
    for index in range(len(shares) // 2):
        pair = shares[2 * index : 2 * index + 2]
        size = pair[0].shape[0] // 2
        block = share_block(row, layer, index, rows_n, split, here, size)
        value += products(left, block, pair, 0, size)
    total[...] = value


def shares_product(left, early, shares, rows_n, split, here):
    operands = [left, early] + shares
    return pl.pallas_call(
        functools.partial(shares_kernel, rows_n, split, here),
        in_specs=[VMEM] * len(operands),
        out_specs=VMEM,
        out_shape=jax.ShapeDtypeStruct(early.shape, early.dtype),
        compiler_params=params((left.shape, 4), (early.shape, 12)),
        cost_estimate=pl.CostEstimate(flops=1000000, bytes_accessed=1000000, transcendentals=0),
        name="shares_product",
    )(*operands)


def product_kernel(rows_n, cols_n, split, damp, near, middle, last, *refs):
    shares = refs[:-5]
    out_ref, left_last, total, result, sems = refs[-5:]
    out_rows = last.shape[1]
    row, layer = lax.axis_index("row"), lax.axis_index("depth")
    place_left(left_last, last, 0)
    here = near.shape[0] // 4
    rights = [(row * here, here, [near])]
    for index in range(len(shares) // 2):
        pair = shares[2 * index : 2 * index + 2]
        size = pair[0].shape[0] // 2
        block = share_block(row, layer, index, rows_n, split, here, size)
        rights.append((block, size, pair))
    wanted = lax.rem(lax.axis_index("col") + cols_n - cols_n // 2, cols_n)
    for block, size, right in rights:

        @pl.when((wanted >= block) & (wanted < block + size))
        def _():
            total[...] = middle[...] + products(left_last, 0, right, wanted - block, 1)

    copies = []
    rows = out_rows // 4
    for part in range(2):
        for start in range(0, out_rows, rows):
            at = pl.ds(start, rows)
            if part == 0:
                result[0, at, :] = total[pl.ds(out_rows + start, rows), :] - damp[0, at, :]
            else:
                result[1, at, :] = -total[at, :] - damp[1, at, :]
            copies.append(
                pltpu.make_async_copy(
                    result.at[part, at], out_ref.at[part, at], sems.at[len(copies)]
                )
            )
            copies[-1].start()
    for copy in copies:
        copy.wait()


def body(k_parts, p_parts, k_mask, p_mask, atoms, classes, rates):
    rows_n, cols_n, depth = (lax.axis_size(a) for a in ("row", "col", "depth"))
    here, width = k_parts.shape[1:]
    out_rows = here // depth
    split = 2 if depth % 2 == 0 else 1
    k_mask, p_mask = k_mask.T, p_mask.T
    (strip,) = mask_rows(k_mask, p_mask, k_parts, p_parts, depth, 1, "mask_strip")
    share = mask_rows(p_mask, k_mask, p_parts, k_parts, split, 2, "mask_share")
    ups, downs = [strip], [strip]
    for step in range(1, cols_n // 2 + 1):
        block = ups[-1] if step == 1 else relay(ups[-1])
        ups.append(lax.ppermute(block, "col", [(i, (i + 1) % cols_n) for i in range(cols_n)]))
    for step in range(1, cols_n - cols_n // 2):
        downs.append(lax.ppermute(downs[-1], "col", [(i, (i - 1) % cols_n) for i in range(cols_n)]))
    near, damp = local_part(
        k_mask, p_mask, atoms, classes, rates, k_parts, p_parts, strip
    )
    shares = []
    for shift in range(1, rows_n):
        perm = [(i, (i + shift) % rows_n) for i in range(rows_n)]
        got = [lax.ppermute(part, "row", perm) for part in share]
        shares += got
        if split == 2:
            swap = [(i, i ^ 1) for i in range(depth)]
            shares += [lax.ppermute(part, "depth", swap) for part in got]
    blocks = ups[1:-1] + downs[1:]
    left, early = early_product(near, strip, blocks, cols_n)
    middle = shares_product(left, early, shares, rows_n, split, here // width)
    operands = [damp, near, middle, ups[-1]] + shares
    block, total = (2 * out_rows, 4 * width), (2 * out_rows, width)
    return pl.pallas_call(
        functools.partial(product_kernel, rows_n, cols_n, split),
        in_specs=[VMEM] * len(operands),
        out_specs=HBM,
        out_shape=jax.ShapeDtypeStruct((2, out_rows, width), jnp.float32),
        scratch_shapes=[
            pltpu.VMEM(block, strip.dtype),
            pltpu.VMEM(total, jnp.float32),
            pltpu.VMEM((2, out_rows, width), jnp.float32),
            pltpu.SemaphoreType.DMA((8,)),
        ],
        compiler_params=params((near.shape, 2 * rows_n), (left.shape, 2), (block, 4), (total, 16)),
        name="commutator",
    )(*operands)


def solution(mesh):
    return jax.shard_map(
        body,
        mesh=mesh,
        in_specs=(
            P(None, "row", "col"),
            P(None, "row", "col"),
            P("row", "col"),
            P("row", "col"),
            P(),
            P(),
            P(),
        ),
        out_specs=P(None, ("row", "depth"), "col"),
        check_vma=False,
    )
```

```python
import functools

import jax
import jax.numpy as jnp
from jax import lax
from jax.experimental import pallas as pl
from jax.experimental.pallas import tpu as pltpu
from jax.sharding import PartitionSpec as P

TILE = 64

HBM = pl.BlockSpec(memory_space=pltpu.HBM)
SMEM = pl.BlockSpec(memory_space=pltpu.SMEM)
VMEM = pl.BlockSpec(memory_space=pltpu.VMEM)


def params(*shapes):
    total = sum(functools.reduce(lambda a, b: a * b, s) * w for s, w in shapes)
    return pltpu.CompilerParams(vmem_limit_bytes=2 * total + (4 << 20))


def tile_row(mask_ref, tile, width, dtype):
    lanes = lax.broadcasted_iota(jnp.int32, (1, width), 1) // TILE
    row = jnp.zeros((1, width), jnp.float32)
    for place in range(width // TILE):
        row = jnp.where(lanes == place, mask_ref[place, tile].astype(jnp.float32), row)
    return row.astype(dtype)


def fetch_masks(sources, masks, sems):
    copies = [
        pltpu.make_async_copy(ref, masks.at[i], sems.at[i]) for i, ref in enumerate(sources)
    ]
    for copy in copies:
        copy.start()
    return copies


def rows_kernel(places, first_mask, second_mask, first_ref, second_ref, *refs):
    out_refs = refs[:-6]
    held, masked, masks, sems, out_sems, mask_sems = refs[-6:]
    rows, width = held.shape[1:]
    each = 4 // len(out_refs)
    unit = masked.shape[1]
    first = lax.rem(lax.axis_index("depth"), places) * rows
    span = pl.ds(pl.multiple_of(first, rows), rows)
    mask_copies = fetch_masks((first_mask, second_mask), masks, mask_sems)
    copies = [
        pltpu.make_async_copy(ref.at[:, span, :], held.at[pl.ds(2 * i, 2)], sems.at[i])
        for i, ref in enumerate((first_ref, second_ref))
    ]
    for copy in copies:
        copy.start()
    for copy in mask_copies:
        copy.wait()
    out_copies = []
    for i, copy in enumerate(copies):
        copy.wait()
        for tile in range(rows // TILE):
            factor = tile_row(masks.at[i], first // TILE + tile, width, held.dtype)
            at = pl.ds(tile * TILE, TILE)
            block, within = divmod(tile * TILE, unit)
            for part in range(2):
                spot = 2 * (i * (rows // unit) + block) + part
                masked[spot, pl.ds(within, TILE), :] = held[2 * i + part, at, :] * factor
        size = 2 * (rows // unit)
        target = out_refs[i] if each == 2 else out_refs[0].at[pl.ds(i * size, size)]
        out_copies.append(
            pltpu.make_async_copy(masked.at[pl.ds(i * size, size)], target, out_sems.at[i])
        )
        out_copies[-1].start()
    for copy in out_copies:
        copy.wait()


def mask_rows(first_mask, second_mask, first_parts, second_parts, places, arrays, name):
    here, width = first_parts.shape[1:]
    rows, dtype = here // places, first_parts.dtype
    unit = min(rows, width)
    count = 4 * (rows // unit)
    return pl.pallas_call(
        functools.partial(rows_kernel, places),
        in_specs=[HBM] * 4,
        out_specs=[HBM] * arrays,
        out_shape=[jax.ShapeDtypeStruct((count // arrays, unit, width), dtype)] * arrays,
        scratch_shapes=[
            pltpu.VMEM((4, rows, width), dtype),
            pltpu.VMEM((count, unit, width), dtype),
            pltpu.SMEM((2,) + first_mask.shape, first_mask.dtype),
            pltpu.SemaphoreType.DMA((2,)),
            pltpu.SemaphoreType.DMA((2,)),
            pltpu.SemaphoreType.DMA((2,)),
        ],
        name=name,
    )(first_mask, second_mask, first_parts, second_parts)


def strip_kernel(k_ref, p_ref, strip_ref, sems):
    rows = strip_ref.shape[1]
    at = pl.ds(pl.multiple_of(lax.axis_index("depth") * rows, rows), rows)
    copies = [
        pltpu.make_async_copy(ref.at[:, at, :], strip_ref.at[pl.ds(2 * i, 2)], sems.at[i])
        for i, ref in enumerate((k_ref, p_ref))
    ]
    for copy in copies:
        copy.start()
    for copy in copies:
        copy.wait()


def cut_strip(k_parts, p_parts, out_rows):
    return pl.pallas_call(
        strip_kernel,
        in_specs=[HBM] * 2,
        out_specs=HBM,
        out_shape=jax.ShapeDtypeStruct((4, out_rows, k_parts.shape[2]), k_parts.dtype),
        scratch_shapes=[pltpu.SemaphoreType.DMA((2,))],
        name="cut_strip",
    )(k_parts, p_parts)


def factors_kernel(*refs):
    masks, out_ref = refs[:-1], refs[-1]
    rows, width = out_ref.shape[2:]
    tiles = rows // TILE
    first = lax.axis_index("depth") * tiles
    for index, mask in enumerate(masks):
        for i in range(2):
            for tile in range(tiles):
                factor = tile_row(mask.at[i], first + tile, width, out_ref.dtype)
                out_ref[index, i, pl.ds(tile * TILE, TILE), :] = jnp.broadcast_to(
                    factor, (TILE, width)
                )


def expand_factors(masks, out_rows, width, dtype):
    shape = (len(masks), 2, out_rows, width)
    return pl.pallas_call(
        factors_kernel,
        in_specs=[SMEM] * len(masks),
        out_specs=VMEM,
        out_shape=jax.ShapeDtypeStruct(shape, dtype),
        compiler_params=params((shape, 2)),
        name="expand_factors",
    )(*masks)


def local_kernel(
    k_mask,
    p_mask,
    atoms_ref,
    classes_ref,
    rates_ref,
    k_ref,
    p_ref,
    near_ref,
    damp,
    held,
    near,
    masks,
    atoms,
    classes,
    rates,
    sems,
    out_sems,
    small_sems,
):
    here, width = held.shape[1:]
    out_rows = damp.shape[1]
    row, col, layer = (lax.axis_index(a) for a in ("row", "col", "depth"))
    small = fetch_masks((k_mask, p_mask), masks, small_sems)
    copies = [
        pltpu.make_async_copy(ref, held.at[pl.ds(2 * i, 2)], sems.at[i])
        for i, ref in enumerate((p_ref, k_ref))
    ]
    tables = [
        pltpu.make_async_copy(source, target, small_sems.at[2 + i])
        for i, (source, target) in enumerate(
            ((atoms_ref, atoms), (classes_ref, classes), (rates_ref, rates))
        )
    ]
    for copy in copies + tables:
        copy.start()
    for copy in small + copies:
        copy.wait()
    out_copies = []
    for block in range(here // width):
        for tile in range(block * width // TILE, (block + 1) * width // TILE):
            at, spot = pl.ds(tile * TILE, TILE), pl.ds(tile * TILE - block * width, TILE)
            for i in range(2):
                factor = tile_row(masks.at[1 - i], tile, width, held.dtype)
                for part in (2 * i, 2 * i + 1):
                    near[4 * block + part, spot, :] = held[part, at, :] * factor
        span = pl.ds(4 * block, 4)
        out_copies.append(
            pltpu.make_async_copy(near.at[span], near_ref.at[span], out_sems.at[block])
        )
        out_copies[-1].start()
    for copy in tables:
        copy.wait()
    lanes = lax.broadcasted_iota(jnp.int32, (1, width), 1) // TILE
    row_tiles, col_tiles = out_rows // TILE, width // TILE
    first = (row * lax.axis_size("depth") + layer) * row_tiles
    for tile in range(row_tiles):
        at = pl.ds(tile * TILE, TILE)
        atom_row = atoms[first + tile]
        gamma = jnp.zeros((1, width), jnp.float32)
        for spot in range(col_tiles):
            atom_col = atoms[col * col_tiles + spot]
            rate = jnp.where(atom_row != atom_col, rates[classes[atom_row, atom_col]], 0.0)
            gamma = jnp.where(lanes == spot, rate, gamma)
        for part in range(2):
            start = layer * out_rows + tile * TILE
            within = pl.ds(pl.multiple_of(lax.rem(start, width), TILE), TILE)
            own = near[4 * (start // width) + part, within, :]
            damp[part, at, :] = gamma * own.astype(jnp.float32)
    for copy in out_copies:
        copy.wait()


def local_part(k_mask, p_mask, atoms, classes, rates, k_parts, p_parts, out_rows):
    here, width = k_parts.shape[1:]
    dtype = k_parts.dtype
    blocks = here // width
    near = (4 * blocks, width, width)
    return pl.pallas_call(
        local_kernel,
        in_specs=[HBM] * 7,
        out_specs=[HBM, VMEM],
        out_shape=[
            jax.ShapeDtypeStruct(near, dtype),
            jax.ShapeDtypeStruct((2, out_rows, width), jnp.float32),
        ],
        scratch_shapes=[
            pltpu.VMEM((4, here, width), dtype),
            pltpu.VMEM(near, dtype),
            pltpu.SMEM((2,) + k_mask.shape, k_mask.dtype),
            pltpu.SMEM(atoms.shape, atoms.dtype),
            pltpu.SMEM(classes.shape, classes.dtype),
            pltpu.SMEM(rates.shape, rates.dtype),
            pltpu.SemaphoreType.DMA((2,)),
            pltpu.SemaphoreType.DMA((blocks,)),
            pltpu.SemaphoreType.DMA((5,)),
        ],
        cost_estimate=pl.CostEstimate(
            flops=8 * here * width, bytes_accessed=20 * here * width, transcendentals=0
        ),
        name="local_part",
    )(k_mask, p_mask, atoms, classes, rates, k_parts, p_parts)


def place_left(left, ref, block, factors, index):
    rows, width = ref.shape[1:]
    k_factor, p_factor = factors[index, 0], factors[index, 1]
    k_re, k_im = ref[0] * k_factor, ref[1] * k_factor
    p_re, p_im = ref[2] * p_factor, ref[3] * p_factor
    for half, parts in enumerate(((k_re, -k_im, -p_re, p_im), (k_im, k_re, -p_im, -p_re))):
        for slot, part in enumerate(parts):
            at = pl.multiple_of((4 * block + slot) * width, width)
            left[pl.ds(half * rows, rows), pl.ds(at, width)] = part


def relay_kernel(block, out):
    out[...] = block[...]


def relay(block):
    return pl.pallas_call(
        relay_kernel,
        in_specs=[VMEM],
        out_specs=VMEM,
        out_shape=jax.ShapeDtypeStruct(block.shape, block.dtype),
        compiler_params=params((block.shape, 4)),
        cost_estimate=pl.CostEstimate(
            flops=100000000, bytes_accessed=4 * block.size, transcendentals=0
        ),
        name="relay",
    )(block)


def share_block(row, layer, index, rows_n, split, here, size):
    other = lax.rem(row - index // split - 1 + rows_n, rows_n)
    return other * here + (lax.rem(layer, split) ^ (index % split)) * size


def products(left, block, right, first, count):
    each = 4 // len(right)
    width = right[0].shape[1]
    steps = [(0, count)] if each == 4 else [(step, 1) for step in range(count)]
    found = []
    for step, size in steps:
        for half, ref in enumerate(right):
            at = pl.multiple_of((4 * (block + step) + half * each) * width, width)
            value = ref[pl.ds((first + step) * each, size * each)]
            found.append(
                jnp.dot(
                    left[:, pl.ds(at, size * each * width)],
                    value.reshape(size * each * width, width),
                    preferred_element_type=jnp.float32,
                )
            )
    return sum(found[1:], found[0])


def early_kernel(cols_n, near, factors, own, *refs):
    blocks = refs[:-2]
    ups, downs = blocks[: cols_n // 2 - 1], blocks[cols_n // 2 - 1 :]
    left, total = refs[-2:]
    width = own.shape[2]
    row, col = lax.axis_index("row"), lax.axis_index("col")
    place_left(left, own, col, factors, 0)
    for step, ref in enumerate(ups, 1):
        place_left(left, ref, lax.rem(col - step + cols_n, cols_n), factors, step)
    for step, ref in enumerate(downs, 1):
        place_left(left, ref, lax.rem(col + step, cols_n), factors, cols_n - step)
    last = pl.multiple_of(lax.rem(col + cols_n - cols_n // 2, cols_n) * 4 * width, width)
    left[:, pl.ds(last, 4 * width)] = jnp.zeros((left.shape[0], 4 * width), left.dtype)
    count = near.shape[0] // 4
    total[...] = products(left, row * count, [near], 0, count)


def early_product(near, factors, strip, blocks, cols_n):
    out_rows, width = strip.shape[1:]
    left, total = (2 * out_rows, cols_n * 4 * width), (2 * out_rows, width)
    operands = [near, factors, strip] + blocks
    return pl.pallas_call(
        functools.partial(early_kernel, cols_n),
        in_specs=[VMEM] * len(operands),
        out_specs=[VMEM, VMEM],
        out_shape=[
            jax.ShapeDtypeStruct(left, near.dtype),
            jax.ShapeDtypeStruct(total, jnp.float32),
        ],
        compiler_params=params((near.shape, 2), (left, 4), (total, 8)),
        cost_estimate=pl.CostEstimate(
            flops=4 * out_rows * near.shape[0] * width * width * 40,
            bytes_accessed=left[0] * left[1] * 4,
            transcendentals=0,
        ),
        name="early_product",
    )(*operands)


def shares_kernel(rows_n, split, here, left, early, *refs):
    shares, total = refs[:-1], refs[-1]
    row, layer = lax.axis_index("row"), lax.axis_index("depth")
    value = early[...]
    for index in range(len(shares) // 2):
        pair = shares[2 * index : 2 * index + 2]
        size = pair[0].shape[0] // 2
        block = share_block(row, layer, index, rows_n, split, here, size)
        value += products(left, block, pair, 0, size)
    total[...] = value


def shares_product(left, early, shares, rows_n, split, here):
    operands = [left, early] + shares
    return pl.pallas_call(
        functools.partial(shares_kernel, rows_n, split, here),
        in_specs=[VMEM] * len(operands),
        out_specs=VMEM,
        out_shape=jax.ShapeDtypeStruct(early.shape, early.dtype),
        compiler_params=params((left.shape, 4), (early.shape, 12)),
        cost_estimate=pl.CostEstimate(flops=1000000, bytes_accessed=1000000, transcendentals=0),
        name="shares_product",
    )(*operands)


def product_kernel(rows_n, cols_n, split, damp, near, factors, middle, last, *refs):
    shares = refs[:-3]
    out_ref, left_last, total = refs[-3:]
    out_rows = last.shape[1]
    row, layer = lax.axis_index("row"), lax.axis_index("depth")
    place_left(left_last, last, 0, factors, cols_n // 2)
    here = near.shape[0] // 4
    rights = [(row * here, here, [near])]
    for index in range(len(shares) // 2):
        pair = shares[2 * index : 2 * index + 2]
        size = pair[0].shape[0] // 2
        block = share_block(row, layer, index, rows_n, split, here, size)
        rights.append((block, size, pair))
    wanted = lax.rem(lax.axis_index("col") + cols_n - cols_n // 2, cols_n)
    for block, size, right in rights:

        @pl.when((wanted >= block) & (wanted < block + size))
        def _():
            total[...] = middle[...] + products(left_last, 0, right, wanted - block, 1)

    out_ref[0] = total[pl.ds(out_rows, out_rows), :] - damp[0]
    out_ref[1] = -total[pl.ds(0, out_rows), :] - damp[1]


def body(k_parts, p_parts, k_mask, p_mask, atoms, classes, rates):
    rows_n, cols_n, depth = (lax.axis_size(a) for a in ("row", "col", "depth"))
    here, width = k_parts.shape[1:]
    out_rows = here // depth
    split = 2 if depth % 2 == 0 else 1
    k_mask, p_mask = k_mask.T, p_mask.T
    strip = cut_strip(k_parts, p_parts, out_rows)
    share = mask_rows(p_mask, k_mask, p_parts, k_parts, split, 2, "mask_share")
    ups, downs = [strip], [strip]
    for step in range(1, cols_n // 2 + 1):
        block = ups[-1] if step == 1 else relay(ups[-1])
        ups.append(lax.ppermute(block, "col", [(i, (i + 1) % cols_n) for i in range(cols_n)]))
    for step in range(1, cols_n - cols_n // 2):
        downs.append(lax.ppermute(downs[-1], "col", [(i, (i - 1) % cols_n) for i in range(cols_n)]))
    masks = [jnp.stack((k_mask, p_mask))]
    for shift in range(1, cols_n):
        perm = [(i, (i + shift) % cols_n) for i in range(cols_n)]
        masks.append(lax.ppermute(masks[0], "col", perm))
    factors = expand_factors(masks, out_rows, width, strip.dtype)
    near, damp = local_part(
        k_mask, p_mask, atoms, classes, rates, k_parts, p_parts, out_rows
    )
    shares = []
    for shift in range(1, rows_n):
        perm = [(i, (i + shift) % rows_n) for i in range(rows_n)]
        got = [lax.ppermute(part, "row", perm) for part in share]
        shares += got
        if split == 2:
            swap = [(i, i ^ 1) for i in range(depth)]
            shares += [lax.ppermute(part, "depth", swap) for part in got]
    blocks = ups[1:-1] + downs[1:]
    left, early = early_product(near, factors, strip, blocks, cols_n)
    middle = shares_product(left, early, shares, rows_n, split, here // width)
    operands = [damp, near, factors, middle, ups[-1]] + shares
    block, total = (2 * out_rows, 4 * width), (2 * out_rows, width)
    return pl.pallas_call(
        functools.partial(product_kernel, rows_n, cols_n, split),
        in_specs=[VMEM] * len(operands),
        out_specs=VMEM,
        out_shape=jax.ShapeDtypeStruct((2, out_rows, width), jnp.float32),
        scratch_shapes=[pltpu.VMEM(block, strip.dtype), pltpu.VMEM(total, jnp.float32)],
        compiler_params=params((near.shape, 2 * rows_n), (left.shape, 2), (block, 4), (total, 16)),
        name="commutator",
    )(*operands)


def solution(mesh):
    return jax.shard_map(
        body,
        mesh=mesh,
        in_specs=(
            P(None, "row", "col"),
            P(None, "row", "col"),
            P("row", "col"),
            P("row", "col"),
            P(),
            P(),
            P(),
        ),
        out_specs=P(None, ("row", "depth"), "col"),
        check_vma=False,
    )
```

```python
import functools

import jax
import jax.numpy as jnp
from jax import lax
from jax.experimental import pallas as pl
from jax.experimental.pallas import tpu as pltpu
from jax.sharding import PartitionSpec as P

TILE = 64

HBM = pl.BlockSpec(memory_space=pltpu.HBM)
SMEM = pl.BlockSpec(memory_space=pltpu.SMEM)
VMEM = pl.BlockSpec(memory_space=pltpu.VMEM)


def params(*shapes):
    total = sum(functools.reduce(lambda a, b: a * b, s) * w for s, w in shapes)
    return pltpu.CompilerParams(vmem_limit_bytes=2 * total + (4 << 20))


def tile_row(mask_ref, tile, width, dtype):
    lanes = lax.broadcasted_iota(jnp.int32, (1, width), 1) // TILE
    row = jnp.zeros((1, width), jnp.float32)
    for place in range(width // TILE):
        row = jnp.where(lanes == place, mask_ref[place, tile].astype(jnp.float32), row)
    return row.astype(dtype)


def fetch_masks(sources, masks, sems):
    copies = [
        pltpu.make_async_copy(ref, masks.at[i], sems.at[i]) for i, ref in enumerate(sources)
    ]
    for copy in copies:
        copy.start()
    return copies


def rows_kernel(places, first_mask, second_mask, first_ref, second_ref, *refs):
    out_refs = refs[:-6]
    held, masked, masks, sems, out_sems, mask_sems = refs[-6:]
    rows, width = held.shape[1:]
    each = 4 // len(out_refs)
    unit = masked.shape[1]
    first = lax.rem(lax.axis_index("depth"), places) * rows
    span = pl.ds(pl.multiple_of(first, rows), rows)
    mask_copies = fetch_masks((first_mask, second_mask), masks, mask_sems)
    copies = [
        pltpu.make_async_copy(ref.at[:, span, :], held.at[pl.ds(2 * i, 2)], sems.at[i])
        for i, ref in enumerate((first_ref, second_ref))
    ]
    for copy in copies:
        copy.start()
    for copy in mask_copies:
        copy.wait()
    out_copies = []
    for i, copy in enumerate(copies):
        copy.wait()
        for tile in range(rows // TILE):
            factor = tile_row(masks.at[i], first // TILE + tile, width, held.dtype)
            at = pl.ds(tile * TILE, TILE)
            block, within = divmod(tile * TILE, unit)
            for part in range(2):
                spot = 2 * (i * (rows // unit) + block) + part
                masked[spot, pl.ds(within, TILE), :] = held[2 * i + part, at, :] * factor
        size = 2 * (rows // unit)
        target = out_refs[i] if each == 2 else out_refs[0].at[pl.ds(i * size, size)]
        out_copies.append(
            pltpu.make_async_copy(masked.at[pl.ds(i * size, size)], target, out_sems.at[i])
        )
        out_copies[-1].start()
    for copy in out_copies:
        copy.wait()


def mask_rows(first_mask, second_mask, first_parts, second_parts, places, arrays, name):
    here, width = first_parts.shape[1:]
    rows, dtype = here // places, first_parts.dtype
    unit = min(rows, width)
    count = 4 * (rows // unit)
    return pl.pallas_call(
        functools.partial(rows_kernel, places),
        in_specs=[HBM] * 4,
        out_specs=[HBM] * arrays,
        out_shape=[jax.ShapeDtypeStruct((count // arrays, unit, width), dtype)] * arrays,
        scratch_shapes=[
            pltpu.VMEM((4, rows, width), dtype),
            pltpu.VMEM((count, unit, width), dtype),
            pltpu.SMEM((2,) + first_mask.shape, first_mask.dtype),
            pltpu.SemaphoreType.DMA((2,)),
            pltpu.SemaphoreType.DMA((2,)),
            pltpu.SemaphoreType.DMA((2,)),
        ],
        name=name,
    )(first_mask, second_mask, first_parts, second_parts)


def local_kernel(
    k_mask,
    p_mask,
    atoms_ref,
    classes_ref,
    rates_ref,
    k_ref,
    p_ref,
    strip,
    near_ref,
    damp,
    held,
    near,
    own,
    masks,
    atoms,
    classes,
    rates,
    sems,
    out_sems,
    small_sems,
):
    here, width = held.shape[1:]
    out_rows = damp.shape[1]
    row, col, layer = (lax.axis_index(a) for a in ("row", "col", "depth"))
    small = fetch_masks((k_mask, p_mask), masks, small_sems)
    copies = [
        pltpu.make_async_copy(ref, held.at[pl.ds(2 * i, 2)], sems.at[i])
        for i, ref in enumerate((p_ref, k_ref))
    ]
    own_copy = pltpu.make_async_copy(strip.at[pl.ds(2, 2)], own, sems.at[2])
    tables = [
        pltpu.make_async_copy(source, target, small_sems.at[2 + i])
        for i, (source, target) in enumerate(
            ((atoms_ref, atoms), (classes_ref, classes), (rates_ref, rates))
        )
    ]
    for copy in copies + [own_copy] + tables:
        copy.start()
    for copy in small + copies:
        copy.wait()
    out_copies = []
    for block in range(here // width):
        for tile in range(block * width // TILE, (block + 1) * width // TILE):
            at, spot = pl.ds(tile * TILE, TILE), pl.ds(tile * TILE - block * width, TILE)
            for i in range(2):
                factor = tile_row(masks.at[1 - i], tile, width, held.dtype)
                for part in (2 * i, 2 * i + 1):
                    near[4 * block + part, spot, :] = held[part, at, :] * factor
        span = pl.ds(4 * block, 4)
        out_copies.append(
            pltpu.make_async_copy(near.at[span], near_ref.at[span], out_sems.at[block])
        )
        out_copies[-1].start()
    for copy in [own_copy] + tables:
        copy.wait()
    lanes = lax.broadcasted_iota(jnp.int32, (1, width), 1) // TILE
    row_tiles, col_tiles = out_rows // TILE, width // TILE
    first = (row * lax.axis_size("depth") + layer) * row_tiles
    for tile in range(row_tiles):
        at = pl.ds(tile * TILE, TILE)
        atom_row = atoms[first + tile]
        gamma = jnp.zeros((1, width), jnp.float32)
        for spot in range(col_tiles):
            atom_col = atoms[col * col_tiles + spot]
            rate = jnp.where(atom_row != atom_col, rates[classes[atom_row, atom_col]], 0.0)
            gamma = jnp.where(lanes == spot, rate, gamma)
        for part in range(2):
            damp[part, at, :] = gamma * own[part, at, :].astype(jnp.float32)
    for copy in out_copies:
        copy.wait()


def local_part(k_mask, p_mask, atoms, classes, rates, k_parts, p_parts, strip):
    here, width = k_parts.shape[1:]
    out_rows, dtype = strip.shape[1], strip.dtype
    blocks = here // width
    near = (4 * blocks, width, width)
    return pl.pallas_call(
        local_kernel,
        in_specs=[HBM] * 8,
        out_specs=[HBM, VMEM],
        out_shape=[
            jax.ShapeDtypeStruct(near, dtype),
            jax.ShapeDtypeStruct((2, out_rows, width), jnp.float32),
        ],
        scratch_shapes=[
            pltpu.VMEM((4, here, width), dtype),
            pltpu.VMEM(near, dtype),
            pltpu.VMEM((2, out_rows, width), dtype),
            pltpu.SMEM((2,) + k_mask.shape, k_mask.dtype),
            pltpu.SMEM(atoms.shape, atoms.dtype),
            pltpu.SMEM(classes.shape, classes.dtype),
            pltpu.SMEM(rates.shape, rates.dtype),
            pltpu.SemaphoreType.DMA((3,)),
            pltpu.SemaphoreType.DMA((blocks,)),
            pltpu.SemaphoreType.DMA((5,)),
        ],
        cost_estimate=pl.CostEstimate(
            flops=8 * here * width, bytes_accessed=20 * here * width, transcendentals=0
        ),
        name="local_part",
    )(k_mask, p_mask, atoms, classes, rates, k_parts, p_parts, strip)


def place_left(left, ref, block):
    rows, width = ref.shape[1:]
    k_re, k_im, p_re, p_im = ref[0], ref[1], ref[2], ref[3]
    for half, parts in enumerate(((k_re, -k_im, -p_re, p_im), (k_im, k_re, -p_im, -p_re))):
        for slot, part in enumerate(parts):
            at = pl.multiple_of((4 * block + slot) * width, width)
            left[pl.ds(half * rows, rows), pl.ds(at, width)] = part


def relay_kernel(block, out):
    out[...] = block[...]


def relay(block):
    return pl.pallas_call(
        relay_kernel,
        in_specs=[VMEM],
        out_specs=VMEM,
        out_shape=jax.ShapeDtypeStruct(block.shape, block.dtype),
        compiler_params=params((block.shape, 4)),
        cost_estimate=pl.CostEstimate(
            flops=40000000000, bytes_accessed=4 * block.size, transcendentals=0
        ),
        name="relay",
    )(block)


def products(left, block, right, first, count):
    each = 4 // len(right)
    width = right[0].shape[1]
    steps = [(0, count)] if each == 4 else [(step, 1) for step in range(count)]
    found = []
    for step, size in steps:
        for half, ref in enumerate(right):
            at = pl.multiple_of((4 * (block + step) + half * each) * width, width)
            value = ref[pl.ds((first + step) * each, size * each)]
            found.append(
                jnp.dot(
                    left[:, pl.ds(at, size * each * width)],
                    value.reshape(size * each * width, width),
                    preferred_element_type=jnp.float32,
                )
            )
    return sum(found[1:], found[0])


def early_kernel(cols_n, near, own, *refs):
    blocks = refs[:-2]
    ups, downs = blocks[: cols_n // 2 - 1], blocks[cols_n // 2 - 1 :]
    left, total = refs[-2:]
    width = own.shape[2]
    row, col = lax.axis_index("row"), lax.axis_index("col")
    place_left(left, own, col)
    for step, ref in enumerate(ups, 1):
        place_left(left, ref, lax.rem(col - step + cols_n, cols_n))
    for step, ref in enumerate(downs, 1):
        place_left(left, ref, lax.rem(col + step, cols_n))
    last = pl.multiple_of(lax.rem(col + cols_n - cols_n // 2, cols_n) * 4 * width, width)
    left[:, pl.ds(last, 4 * width)] = jnp.zeros((left.shape[0], 4 * width), left.dtype)
    count = near.shape[0] // 4
    total[...] = products(left, row * count, [near], 0, count)


def early_product(near, strip, blocks, cols_n):
    out_rows, width = strip.shape[1:]
    left, total = (2 * out_rows, cols_n * 4 * width), (2 * out_rows, width)
    operands = [near, strip] + blocks
    return pl.pallas_call(
        functools.partial(early_kernel, cols_n),
        in_specs=[VMEM] * len(operands),
        out_specs=[VMEM, VMEM],
        out_shape=[
            jax.ShapeDtypeStruct(left, near.dtype),
            jax.ShapeDtypeStruct(total, jnp.float32),
        ],
        compiler_params=params((near.shape, 2), (left, 4), (total, 8)),
        cost_estimate=pl.CostEstimate(
            flops=4 * out_rows * near.shape[0] * width * width * 40,
            bytes_accessed=left[0] * left[1] * 4,
            transcendentals=0,
        ),
        name="early_product",
    )(*operands)


def shares_kernel(rows_n, depth, left, early, *refs):
    strips, total, far = refs[:-2], refs[-2], refs[-1]
    rows, width = strips[0].shape[1:]
    row, layer = lax.axis_index("row"), lax.axis_index("depth")
    count = far.shape[0] // (4 * (rows_n - 1))
    for index, ref in enumerate(strips):
        start = (layer ^ (index % depth)) * rows
        block = (index // depth) * count + start // width
        at = pl.ds(pl.multiple_of(lax.rem(start, width), rows), rows)
        for slot in range(4):
            far[4 * block + slot, at, :] = ref[(slot + 2) % 4]
    value = early[...]
    for shift in range(rows_n - 1):
        block = lax.rem(row - shift - 1 + rows_n, rows_n) * count
        value += products(left, block, [far], shift * count, count)
    total[...] = value


def shares_product(left, early, strips, rows_n, depth):
    operands = [left, early] + strips
    rows, width = strips[0].shape[1:]
    far = (4 * len(strips) * rows // width, width, width)
    return pl.pallas_call(
        functools.partial(shares_kernel, rows_n, depth),
        in_specs=[VMEM] * len(operands),
        out_specs=[VMEM, VMEM],
        out_shape=[
            jax.ShapeDtypeStruct(early.shape, early.dtype),
            jax.ShapeDtypeStruct(far, left.dtype),
        ],
        compiler_params=params((left.shape, 4), (far, 4), (early.shape, 12)),
        cost_estimate=pl.CostEstimate(flops=1000000, bytes_accessed=1000000, transcendentals=0),
        name="shares_product",
    )(*operands)


def product_kernel(rows_n, cols_n, damp, near, far, middle, last, *refs):
    out_ref, left_last, total = refs
    out_rows = last.shape[1]
    row = lax.axis_index("row")
    place_left(left_last, last, 0)
    count = near.shape[0] // 4
    rights = [(row * count, count, near, 0)]
    for shift in range(rows_n - 1):
        other = lax.rem(row - shift - 1 + rows_n, rows_n)
        rights.append((other * count, count, far, shift * count))
    wanted = lax.rem(lax.axis_index("col") + cols_n - cols_n // 2, cols_n)
    for block, size, right, base in rights:

        @pl.when((wanted >= block) & (wanted < block + size))
        def _():
            total[...] = middle[...] + products(left_last, 0, [right], base + wanted - block, 1)

    out_ref[0] = total[pl.ds(out_rows, out_rows), :] - damp[0]
    out_ref[1] = -total[pl.ds(0, out_rows), :] - damp[1]


def body(k_parts, p_parts, k_mask, p_mask, atoms, classes, rates):
    rows_n, cols_n, depth = (lax.axis_size(a) for a in ("row", "col", "depth"))
    here, width = k_parts.shape[1:]
    out_rows = here // depth
    k_mask, p_mask = k_mask.T, p_mask.T
    (strip,) = mask_rows(k_mask, p_mask, k_parts, p_parts, depth, 1, "mask_strip")
    ups, downs = [strip], [strip]
    for step in range(1, cols_n // 2 + 1):
        block = ups[-1] if step == 1 else relay(ups[-1])
        ups.append(lax.ppermute(block, "col", [(i, (i + 1) % cols_n) for i in range(cols_n)]))
    for step in range(1, cols_n - cols_n // 2):
        downs.append(lax.ppermute(downs[-1], "col", [(i, (i - 1) % cols_n) for i in range(cols_n)]))
    near, damp = local_part(
        k_mask, p_mask, atoms, classes, rates, k_parts, p_parts, strip
    )
    strips = []
    for shift in range(1, rows_n):
        perm = [(i, (i + shift) % rows_n) for i in range(rows_n)]
        got = {0: lax.ppermute(strip, "row", perm)}
        stride = depth // 2
        while stride:
            perm = [(i, i ^ stride) for i in range(depth)]
            for flip in list(got):
                got[flip ^ stride] = lax.ppermute(got[flip], "depth", perm)
            stride //= 2
        strips += [got[flip] for flip in range(depth)]
    blocks = ups[1:-1] + downs[1:]
    left, early = early_product(near, strip, blocks, cols_n)
    middle, far = shares_product(left, early, strips, rows_n, depth)
    operands = [damp, near, far, middle, ups[-1]]
    block, total = (2 * out_rows, 4 * width), (2 * out_rows, width)
    return pl.pallas_call(
        functools.partial(product_kernel, rows_n, cols_n),
        in_specs=[VMEM] * len(operands),
        out_specs=VMEM,
        out_shape=jax.ShapeDtypeStruct((2, out_rows, width), jnp.float32),
        scratch_shapes=[pltpu.VMEM(block, strip.dtype), pltpu.VMEM(total, jnp.float32)],
        compiler_params=params((near.shape, 2 * rows_n), (left.shape, 2), (block, 4), (total, 16)),
        name="commutator",
    )(*operands)


def solution(mesh):
    return jax.shard_map(
        body,
        mesh=mesh,
        in_specs=(
            P(None, "row", "col"),
            P(None, "row", "col"),
            P("row", "col"),
            P("row", "col"),
            P(),
            P(),
            P(),
        ),
        out_specs=P(None, ("row", "depth"), "col"),
        check_vma=False,
    )
```

```python
import functools

import jax
import jax.numpy as jnp
from jax import lax
from jax.experimental import pallas as pl
from jax.experimental.pallas import tpu as pltpu
from jax.sharding import PartitionSpec as P

TILE = 64

HBM = pl.BlockSpec(memory_space=pltpu.HBM)
SMEM = pl.BlockSpec(memory_space=pltpu.SMEM)
VMEM = pl.BlockSpec(memory_space=pltpu.VMEM)


def params(*shapes):
    total = sum(functools.reduce(lambda a, b: a * b, s) * w for s, w in shapes)
    return pltpu.CompilerParams(vmem_limit_bytes=2 * total + (4 << 20))


def tile_row(mask_ref, tile, width, dtype):
    lanes = lax.broadcasted_iota(jnp.int32, (1, width), 1) // TILE
    row = jnp.zeros((1, width), jnp.float32)
    for place in range(width // TILE):
        row = jnp.where(lanes == place, mask_ref[place, tile].astype(jnp.float32), row)
    return row.astype(dtype)


def fetch_masks(sources, masks, sems):
    copies = [
        pltpu.make_async_copy(ref, masks.at[i], sems.at[i]) for i, ref in enumerate(sources)
    ]
    for copy in copies:
        copy.start()
    return copies


def rows_kernel(places, first_mask, second_mask, first_ref, second_ref, *refs):
    out_refs = refs[:-6]
    held, masked, masks, sems, out_sems, mask_sems = refs[-6:]
    rows, width = held.shape[1:]
    each = 4 // len(out_refs)
    unit = masked.shape[1]
    first = lax.rem(lax.axis_index("depth"), places) * rows
    span = pl.ds(pl.multiple_of(first, rows), rows)
    mask_copies = fetch_masks((first_mask, second_mask), masks, mask_sems)
    copies = [
        pltpu.make_async_copy(ref.at[:, span, :], held.at[pl.ds(2 * i, 2)], sems.at[i])
        for i, ref in enumerate((first_ref, second_ref))
    ]
    for copy in copies:
        copy.start()
    for copy in mask_copies:
        copy.wait()
    out_copies = []
    for i, copy in enumerate(copies):
        copy.wait()
        for tile in range(rows // TILE):
            factor = tile_row(masks.at[i], first // TILE + tile, width, held.dtype)
            at = pl.ds(tile * TILE, TILE)
            block, within = divmod(tile * TILE, unit)
            for part in range(2):
                spot = 2 * (i * (rows // unit) + block) + part
                masked[spot, pl.ds(within, TILE), :] = held[2 * i + part, at, :] * factor
        size = 2 * (rows // unit)
        target = out_refs[i] if each == 2 else out_refs[0].at[pl.ds(i * size, size)]
        out_copies.append(
            pltpu.make_async_copy(masked.at[pl.ds(i * size, size)], target, out_sems.at[i])
        )
        out_copies[-1].start()
    for copy in out_copies:
        copy.wait()


def mask_rows(first_mask, second_mask, first_parts, second_parts, places, arrays, name):
    here, width = first_parts.shape[1:]
    rows, dtype = here // places, first_parts.dtype
    unit = min(rows, width)
    count = 4 * (rows // unit)
    return pl.pallas_call(
        functools.partial(rows_kernel, places),
        in_specs=[HBM] * 4,
        out_specs=[HBM] * arrays,
        out_shape=[jax.ShapeDtypeStruct((count // arrays, unit, width), dtype)] * arrays,
        scratch_shapes=[
            pltpu.VMEM((4, rows, width), dtype),
            pltpu.VMEM((count, unit, width), dtype),
            pltpu.SMEM((2,) + first_mask.shape, first_mask.dtype),
            pltpu.SemaphoreType.DMA((2,)),
            pltpu.SemaphoreType.DMA((2,)),
            pltpu.SemaphoreType.DMA((2,)),
        ],
        name=name,
    )(first_mask, second_mask, first_parts, second_parts)


def local_kernel(
    k_mask,
    p_mask,
    atoms_ref,
    classes_ref,
    rates_ref,
    k_ref,
    p_ref,
    strip,
    near_ref,
    damp,
    held,
    near,
    own,
    masks,
    atoms,
    classes,
    rates,
    sems,
    out_sems,
    small_sems,
):
    here, width = held.shape[1:]
    out_rows = damp.shape[1]
    row, col, layer = (lax.axis_index(a) for a in ("row", "col", "depth"))
    small = fetch_masks((k_mask, p_mask), masks, small_sems)
    copies = [
        pltpu.make_async_copy(ref, held.at[pl.ds(2 * i, 2)], sems.at[i])
        for i, ref in enumerate((p_ref, k_ref))
    ]
    own_copy = pltpu.make_async_copy(strip.at[pl.ds(2, 2)], own, sems.at[2])
    tables = [
        pltpu.make_async_copy(source, target, small_sems.at[2 + i])
        for i, (source, target) in enumerate(
            ((atoms_ref, atoms), (classes_ref, classes), (rates_ref, rates))
        )
    ]
    for copy in copies + [own_copy] + tables:
        copy.start()
    for copy in small + copies:
        copy.wait()
    out_copies = []
    for block in range(here // width):
        for tile in range(block * width // TILE, (block + 1) * width // TILE):
            at, spot = pl.ds(tile * TILE, TILE), pl.ds(tile * TILE - block * width, TILE)
            for i in range(2):
                factor = tile_row(masks.at[1 - i], tile, width, held.dtype)
                for part in (2 * i, 2 * i + 1):
                    near[4 * block + part, spot, :] = held[part, at, :] * factor
        span = pl.ds(4 * block, 4)
        out_copies.append(
            pltpu.make_async_copy(near.at[span], near_ref.at[span], out_sems.at[block])
        )
        out_copies[-1].start()
    for copy in [own_copy] + tables:
        copy.wait()
    lanes = lax.broadcasted_iota(jnp.int32, (1, width), 1) // TILE
    row_tiles, col_tiles = out_rows // TILE, width // TILE
    first = (row * lax.axis_size("depth") + layer) * row_tiles
    for tile in range(row_tiles):
        at = pl.ds(tile * TILE, TILE)
        atom_row = atoms[first + tile]
        gamma = jnp.zeros((1, width), jnp.float32)
        for spot in range(col_tiles):
            atom_col = atoms[col * col_tiles + spot]
            rate = jnp.where(atom_row != atom_col, rates[classes[atom_row, atom_col]], 0.0)
            gamma = jnp.where(lanes == spot, rate, gamma)
        for part in range(2):
            damp[part, at, :] = gamma * own[part, at, :].astype(jnp.float32)
    for copy in out_copies:
        copy.wait()


def local_part(k_mask, p_mask, atoms, classes, rates, k_parts, p_parts, strip):
    here, width = k_parts.shape[1:]
    out_rows, dtype = strip.shape[1], strip.dtype
    blocks = here // width
    near = (4 * blocks, width, width)
    return pl.pallas_call(
        local_kernel,
        in_specs=[HBM] * 8,
        out_specs=[HBM, VMEM],
        out_shape=[
            jax.ShapeDtypeStruct(near, dtype),
            jax.ShapeDtypeStruct((2, out_rows, width), jnp.float32),
        ],
        scratch_shapes=[
            pltpu.VMEM((4, here, width), dtype),
            pltpu.VMEM(near, dtype),
            pltpu.VMEM((2, out_rows, width), dtype),
            pltpu.SMEM((2,) + k_mask.shape, k_mask.dtype),
            pltpu.SMEM(atoms.shape, atoms.dtype),
            pltpu.SMEM(classes.shape, classes.dtype),
            pltpu.SMEM(rates.shape, rates.dtype),
            pltpu.SemaphoreType.DMA((3,)),
            pltpu.SemaphoreType.DMA((blocks,)),
            pltpu.SemaphoreType.DMA((5,)),
        ],
        cost_estimate=pl.CostEstimate(
            flops=8 * here * width, bytes_accessed=20 * here * width, transcendentals=0
        ),
        name="local_part",
    )(k_mask, p_mask, atoms, classes, rates, k_parts, p_parts, strip)


def place_left(left, ref, block):
    rows, width = ref.shape[1:]
    k_re, k_im, p_re, p_im = ref[0], ref[1], ref[2], ref[3]
    for half, parts in enumerate(((k_re, -k_im, -p_re, p_im), (k_im, k_re, -p_im, -p_re))):
        for slot, part in enumerate(parts):
            at = pl.multiple_of((4 * block + slot) * width, width)
            left[pl.ds(half * rows, rows), pl.ds(at, width)] = part


def relay_kernel(block, out):
    out[...] = block[...]


def relay(block):
    return pl.pallas_call(
        relay_kernel,
        in_specs=[VMEM],
        out_specs=VMEM,
        out_shape=jax.ShapeDtypeStruct(block.shape, block.dtype),
        compiler_params=params((block.shape, 4)),
        cost_estimate=pl.CostEstimate(
            flops=100000000, bytes_accessed=4 * block.size, transcendentals=0
        ),
        name="relay",
    )(block)


def share_block(row, layer, index, rows_n, split, here, size):
    other = lax.rem(row - index // split - 1 + rows_n, rows_n)
    return other * here + (lax.rem(layer, split) ^ (index % split)) * size


def products(left, block, right, first, count):
    each = 4 // len(right)
    width = right[0].shape[1]
    steps = [(0, count)] if each == 4 else [(step, 1) for step in range(count)]
    found = []
    for step, size in steps:
        for half, ref in enumerate(right):
            at = pl.multiple_of((4 * (block + step) + half * each) * width, width)
            value = ref[pl.ds((first + step) * each, size * each)]
            found.append(
                jnp.dot(
                    left[:, pl.ds(at, size * each * width)],
                    value.reshape(size * each * width, width),
                    preferred_element_type=jnp.float32,
                )
            )
    return sum(found[1:], found[0])


def early_kernel(cols_n, near, own, *refs):
    blocks = refs[:-2]
    ups, downs = blocks[: cols_n // 2 - 1], blocks[cols_n // 2 - 1 :]
    left, total = refs[-2:]
    width = own.shape[2]
    row, col = lax.axis_index("row"), lax.axis_index("col")
    place_left(left, own, col)
    for step, ref in enumerate(ups, 1):
        place_left(left, ref, lax.rem(col - step + cols_n, cols_n))
    for step, ref in enumerate(downs, 1):
        place_left(left, ref, lax.rem(col + step, cols_n))
    last = pl.multiple_of(lax.rem(col + cols_n - cols_n // 2, cols_n) * 4 * width, width)
    left[:, pl.ds(last, 4 * width)] = jnp.zeros((left.shape[0], 4 * width), left.dtype)
    count = near.shape[0] // 4
    total[...] = products(left, row * count, [near], 0, count)


def early_product(near, strip, blocks, cols_n):
    out_rows, width = strip.shape[1:]
    left, total = (2 * out_rows, cols_n * 4 * width), (2 * out_rows, width)
    operands = [near, strip] + blocks
    return pl.pallas_call(
        functools.partial(early_kernel, cols_n),
        in_specs=[VMEM] * len(operands),
        out_specs=[VMEM, VMEM],
        out_shape=[
            jax.ShapeDtypeStruct(left, near.dtype),
            jax.ShapeDtypeStruct(total, jnp.float32),
        ],
        compiler_params=params((near.shape, 2), (left, 4), (total, 8)),
        cost_estimate=pl.CostEstimate(
            flops=4 * out_rows * near.shape[0] * width * width * 40,
            bytes_accessed=left[0] * left[1] * 4,
            transcendentals=0,
        ),
        name="early_product",
    )(*operands)


def shares_kernel(rows_n, split, here, left, early, *refs):
    shares, total = refs[:-1], refs[-1]
    row, layer = lax.axis_index("row"), lax.axis_index("depth")
    value = early[...]
    for index in range(len(shares) // 2):
        pair = shares[2 * index : 2 * index + 2]
        size = pair[0].shape[0] // 2
        block = share_block(row, layer, index, rows_n, split, here, size)
        value += products(left, block, pair, 0, size)
    total[...] = value


def shares_product(left, early, shares, rows_n, split, here):
    operands = [left, early] + shares
    return pl.pallas_call(
        functools.partial(shares_kernel, rows_n, split, here),
        in_specs=[VMEM] * len(operands),
        out_specs=VMEM,
        out_shape=jax.ShapeDtypeStruct(early.shape, early.dtype),
        compiler_params=params((left.shape, 4), (early.shape, 12)),
        cost_estimate=pl.CostEstimate(flops=1000000, bytes_accessed=1000000, transcendentals=0),
        name="shares_product",
    )(*operands)


def product_kernel(rows_n, cols_n, split, damp, near, middle, last, *refs):
    shares = refs[:-3]
    out_ref, left_last, total = refs[-3:]
    out_rows = last.shape[1]
    row, layer = lax.axis_index("row"), lax.axis_index("depth")
    place_left(left_last, last, 0)
    here = near.shape[0] // 4
    rights = [(row * here, here, [near])]
    for index in range(len(shares) // 2):
        pair = shares[2 * index : 2 * index + 2]
        size = pair[0].shape[0] // 2
        block = share_block(row, layer, index, rows_n, split, here, size)
        rights.append((block, size, pair))
    wanted = lax.rem(lax.axis_index("col") + cols_n - cols_n // 2, cols_n)
    for block, size, right in rights:

        @pl.when((wanted >= block) & (wanted < block + size))
        def _():
            total[...] = middle[...] + products(left_last, 0, right, wanted - block, 1)

    out_ref[0] = total[pl.ds(out_rows, out_rows), :] - damp[0]
    out_ref[1] = -total[pl.ds(0, out_rows), :] - damp[1]


def body(k_parts, p_parts, k_mask, p_mask, atoms, classes, rates):
    rows_n, cols_n, depth = (lax.axis_size(a) for a in ("row", "col", "depth"))
    here, width = k_parts.shape[1:]
    out_rows = here // depth
    split = 2 if depth % 2 == 0 else 1
    k_mask, p_mask = k_mask.T, p_mask.T
    (strip,) = mask_rows(k_mask, p_mask, k_parts, p_parts, depth, 1, "mask_strip")
    share = mask_rows(p_mask, k_mask, p_parts, k_parts, split, 2, "mask_share")
    ups, downs = [strip], [strip]
    for step in range(1, cols_n // 2 + 1):
        block = ups[-1] if step == 1 else relay(ups[-1])
        ups.append(lax.ppermute(block, "col", [(i, (i + 1) % cols_n) for i in range(cols_n)]))
    downs[0] = lax.optimization_barrier((strip, ups[1]))[0]
    for step in range(1, cols_n - cols_n // 2):
        downs.append(lax.ppermute(downs[-1], "col", [(i, (i - 1) % cols_n) for i in range(cols_n)]))
    near, damp = local_part(
        k_mask, p_mask, atoms, classes, rates, k_parts, p_parts, strip
    )
    shares = []
    for shift in range(1, rows_n):
        perm = [(i, (i + shift) % rows_n) for i in range(rows_n)]
        got = [lax.ppermute(part, "row", perm) for part in share]
        shares += got
        if split == 2:
            swap = [(i, i ^ 1) for i in range(depth)]
            shares += [lax.ppermute(part, "depth", swap) for part in got]
    blocks = ups[1:-1] + downs[1:]
    left, early = early_product(near, strip, blocks, cols_n)
    middle = shares_product(left, early, shares, rows_n, split, here // width)
    operands = [damp, near, middle, ups[-1]] + shares
    block, total = (2 * out_rows, 4 * width), (2 * out_rows, width)
    return pl.pallas_call(
        functools.partial(product_kernel, rows_n, cols_n, split),
        in_specs=[VMEM] * len(operands),
        out_specs=VMEM,
        out_shape=jax.ShapeDtypeStruct((2, out_rows, width), jnp.float32),
        scratch_shapes=[pltpu.VMEM(block, strip.dtype), pltpu.VMEM(total, jnp.float32)],
        compiler_params=params((near.shape, 2 * rows_n), (left.shape, 2), (block, 4), (total, 16)),
        name="commutator",
    )(*operands)


def solution(mesh):
    return jax.shard_map(
        body,
        mesh=mesh,
        in_specs=(
            P(None, "row", "col"),
            P(None, "row", "col"),
            P("row", "col"),
            P("row", "col"),
            P(),
            P(),
            P(),
        ),
        out_specs=P(None, ("row", "depth"), "col"),
        check_vma=False,
    )
```

```python
import functools

import jax
import jax.numpy as jnp
from jax import lax
from jax.experimental import pallas as pl
from jax.experimental.pallas import tpu as pltpu
from jax.sharding import PartitionSpec as P

TILE = 64

HBM = pl.BlockSpec(memory_space=pltpu.HBM)
SMEM = pl.BlockSpec(memory_space=pltpu.SMEM)
VMEM = pl.BlockSpec(memory_space=pltpu.VMEM)


def params(*shapes):
    total = sum(functools.reduce(lambda a, b: a * b, s) * w for s, w in shapes)
    return pltpu.CompilerParams(vmem_limit_bytes=2 * total + (4 << 20))


def tile_row(mask_ref, tile, width, dtype):
    lanes = lax.broadcasted_iota(jnp.int32, (1, width), 1) // TILE
    row = jnp.zeros((1, width), jnp.float32)
    for place in range(width // TILE):
        row = jnp.where(lanes == place, mask_ref[place, tile].astype(jnp.float32), row)
    return row.astype(dtype)


def fetch_masks(sources, masks, sems):
    copies = [
        pltpu.make_async_copy(ref, masks.at[i], sems.at[i]) for i, ref in enumerate(sources)
    ]
    for copy in copies:
        copy.start()
    return copies


def rows_kernel(places, first_mask, second_mask, first_ref, second_ref, *refs):
    out_refs = refs[:-6]
    held, masked, masks, sems, out_sems, mask_sems = refs[-6:]
    rows, width = held.shape[1:]
    each = 4 // len(out_refs)
    unit = masked.shape[1]
    first = lax.rem(lax.axis_index("depth"), places) * rows
    span = pl.ds(pl.multiple_of(first, rows), rows)
    mask_copies = fetch_masks((first_mask, second_mask), masks, mask_sems)
    copies = [
        pltpu.make_async_copy(ref.at[:, span, :], held.at[pl.ds(2 * i, 2)], sems.at[i])
        for i, ref in enumerate((first_ref, second_ref))
    ]
    for copy in copies:
        copy.start()
    for copy in mask_copies:
        copy.wait()
    out_copies = []
    for i, copy in enumerate(copies):
        copy.wait()
        for tile in range(rows // TILE):
            factor = tile_row(masks.at[i], first // TILE + tile, width, held.dtype)
            at = pl.ds(tile * TILE, TILE)
            block, within = divmod(tile * TILE, unit)
            for part in range(2):
                spot = 2 * (i * (rows // unit) + block) + part
                masked[spot, pl.ds(within, TILE), :] = held[2 * i + part, at, :] * factor
        size = 2 * (rows // unit)
        target = out_refs[i] if each == 2 else out_refs[0].at[pl.ds(i * size, size)]
        out_copies.append(
            pltpu.make_async_copy(masked.at[pl.ds(i * size, size)], target, out_sems.at[i])
        )
        out_copies[-1].start()
    for copy in out_copies:
        copy.wait()


def mask_rows(first_mask, second_mask, first_parts, second_parts, places, arrays, name):
    here, width = first_parts.shape[1:]
    rows, dtype = here // places, first_parts.dtype
    unit = min(rows, width)
    count = 4 * (rows // unit)
    return pl.pallas_call(
        functools.partial(rows_kernel, places),
        in_specs=[HBM] * 4,
        out_specs=[HBM] * arrays,
        out_shape=[jax.ShapeDtypeStruct((count // arrays, unit, width), dtype)] * arrays,
        scratch_shapes=[
            pltpu.VMEM((4, rows, width), dtype),
            pltpu.VMEM((count, unit, width), dtype),
            pltpu.SMEM((2,) + first_mask.shape, first_mask.dtype),
            pltpu.SemaphoreType.DMA((2,)),
            pltpu.SemaphoreType.DMA((2,)),
            pltpu.SemaphoreType.DMA((2,)),
        ],
        name=name,
    )(first_mask, second_mask, first_parts, second_parts)


def local_kernel(
    k_mask,
    p_mask,
    atoms_ref,
    classes_ref,
    rates_ref,
    k_ref,
    p_ref,
    strip,
    near_ref,
    damp,
    held,
    near,
    own,
    masks,
    atoms,
    classes,
    rates,
    sems,
    out_sems,
    small_sems,
):
    here, width = held.shape[1:]
    out_rows = damp.shape[1]
    row, col, layer = (lax.axis_index(a) for a in ("row", "col", "depth"))
    small = fetch_masks((k_mask, p_mask), masks, small_sems)
    copies = [
        pltpu.make_async_copy(ref, held.at[pl.ds(2 * i, 2)], sems.at[i])
        for i, ref in enumerate((p_ref, k_ref))
    ]
    own_copy = pltpu.make_async_copy(strip.at[pl.ds(2, 2)], own, sems.at[2])
    tables = [
        pltpu.make_async_copy(source, target, small_sems.at[2 + i])
        for i, (source, target) in enumerate(
            ((atoms_ref, atoms), (classes_ref, classes), (rates_ref, rates))
        )
    ]
    for copy in copies + [own_copy] + tables:
        copy.start()
    for copy in small + copies:
        copy.wait()
    out_copies = []
    for block in range(here // width):
        for tile in range(block * width // TILE, (block + 1) * width // TILE):
            at, spot = pl.ds(tile * TILE, TILE), pl.ds(tile * TILE - block * width, TILE)
            for i in range(2):
                factor = tile_row(masks.at[1 - i], tile, width, held.dtype)
                for part in (2 * i, 2 * i + 1):
                    near[4 * block + part, spot, :] = held[part, at, :] * factor
        span = pl.ds(4 * block, 4)
        out_copies.append(
            pltpu.make_async_copy(near.at[span], near_ref.at[span], out_sems.at[block])
        )
        out_copies[-1].start()
    for copy in [own_copy] + tables:
        copy.wait()
    lanes = lax.broadcasted_iota(jnp.int32, (1, width), 1) // TILE
    row_tiles, col_tiles = out_rows // TILE, width // TILE
    first = (row * lax.axis_size("depth") + layer) * row_tiles
    for tile in range(row_tiles):
        at = pl.ds(tile * TILE, TILE)
        atom_row = atoms[first + tile]
        gamma = jnp.zeros((1, width), jnp.float32)
        for spot in range(col_tiles):
            atom_col = atoms[col * col_tiles + spot]
            rate = jnp.where(atom_row != atom_col, rates[classes[atom_row, atom_col]], 0.0)
            gamma = jnp.where(lanes == spot, rate, gamma)
        for part in range(2):
            damp[part, at, :] = gamma * own[part, at, :].astype(jnp.float32)
    for copy in out_copies:
        copy.wait()


def local_part(k_mask, p_mask, atoms, classes, rates, k_parts, p_parts, strip):
    here, width = k_parts.shape[1:]
    out_rows, dtype = strip.shape[1], strip.dtype
    blocks = here // width
    near = (4 * blocks, width, width)
    return pl.pallas_call(
        local_kernel,
        in_specs=[HBM] * 8,
        out_specs=[HBM, VMEM],
        out_shape=[
            jax.ShapeDtypeStruct(near, dtype),
            jax.ShapeDtypeStruct((2, out_rows, width), jnp.float32),
        ],
        scratch_shapes=[
            pltpu.VMEM((4, here, width), dtype),
            pltpu.VMEM(near, dtype),
            pltpu.VMEM((2, out_rows, width), dtype),
            pltpu.SMEM((2,) + k_mask.shape, k_mask.dtype),
            pltpu.SMEM(atoms.shape, atoms.dtype),
            pltpu.SMEM(classes.shape, classes.dtype),
            pltpu.SMEM(rates.shape, rates.dtype),
            pltpu.SemaphoreType.DMA((3,)),
            pltpu.SemaphoreType.DMA((blocks,)),
            pltpu.SemaphoreType.DMA((5,)),
        ],
        cost_estimate=pl.CostEstimate(
            flops=8 * here * width, bytes_accessed=20 * here * width, transcendentals=0
        ),
        name="local_part",
    )(k_mask, p_mask, atoms, classes, rates, k_parts, p_parts, strip)


def place_left(left, ref, block):
    k_ref, p_ref = ref if isinstance(ref, tuple) else (ref.at[pl.ds(0, 2)], ref.at[pl.ds(2, 2)])
    rows, width = k_ref.shape[1:]
    k_re, k_im, p_re, p_im = k_ref[0], k_ref[1], p_ref[0], p_ref[1]
    for half, parts in enumerate(((k_re, -k_im, -p_re, p_im), (k_im, k_re, -p_im, -p_re))):
        for slot, part in enumerate(parts):
            at = pl.multiple_of((4 * block + slot) * width, width)
            left[pl.ds(half * rows, rows), pl.ds(at, width)] = part


def relay_kernel(block, k_out, p_out):
    k_out[...] = block[:2]
    p_out[...] = block[2:]


def relay(block):
    return pl.pallas_call(
        relay_kernel,
        in_specs=[VMEM],
        out_specs=[VMEM] * 2,
        out_shape=[jax.ShapeDtypeStruct((2,) + block.shape[1:], block.dtype)] * 2,
        compiler_params=params((block.shape, 4)),
        cost_estimate=pl.CostEstimate(
            flops=100000000, bytes_accessed=4 * block.size, transcendentals=0
        ),
        name="relay",
    )(block)


def share_block(row, layer, index, rows_n, split, here, size):
    other = lax.rem(row - index // split - 1 + rows_n, rows_n)
    return other * here + (lax.rem(layer, split) ^ (index % split)) * size


def products(left, block, right, first, count):
    each = 4 // len(right)
    width = right[0].shape[1]
    steps = [(0, count)] if each == 4 else [(step, 1) for step in range(count)]
    found = []
    for step, size in steps:
        for half, ref in enumerate(right):
            at = pl.multiple_of((4 * (block + step) + half * each) * width, width)
            value = ref[pl.ds((first + step) * each, size * each)]
            found.append(
                jnp.dot(
                    left[:, pl.ds(at, size * each * width)],
                    value.reshape(size * each * width, width),
                    preferred_element_type=jnp.float32,
                )
            )
    return sum(found[1:], found[0])


def early_kernel(cols_n, near, own, *refs):
    blocks = refs[:-2]
    ups, downs = blocks[: cols_n // 2 - 1], blocks[cols_n // 2 - 1 :]
    left, total = refs[-2:]
    width = own.shape[2]
    row, col = lax.axis_index("row"), lax.axis_index("col")
    place_left(left, own, col)
    for step, ref in enumerate(ups, 1):
        place_left(left, ref, lax.rem(col - step + cols_n, cols_n))
    for step, ref in enumerate(downs, 1):
        place_left(left, ref, lax.rem(col + step, cols_n))
    last = pl.multiple_of(lax.rem(col + cols_n - cols_n // 2, cols_n) * 4 * width, width)
    left[:, pl.ds(last, 4 * width)] = jnp.zeros((left.shape[0], 4 * width), left.dtype)
    count = near.shape[0] // 4
    total[...] = products(left, row * count, [near], 0, count)


def early_product(near, strip, blocks, cols_n):
    out_rows, width = strip.shape[1:]
    left, total = (2 * out_rows, cols_n * 4 * width), (2 * out_rows, width)
    operands = [near, strip] + blocks
    return pl.pallas_call(
        functools.partial(early_kernel, cols_n),
        in_specs=[VMEM] * len(operands),
        out_specs=[VMEM, VMEM],
        out_shape=[
            jax.ShapeDtypeStruct(left, near.dtype),
            jax.ShapeDtypeStruct(total, jnp.float32),
        ],
        compiler_params=params((near.shape, 2), (left, 4), (total, 8)),
        cost_estimate=pl.CostEstimate(
            flops=4 * out_rows * near.shape[0] * width * width * 40,
            bytes_accessed=left[0] * left[1] * 4,
            transcendentals=0,
        ),
        name="early_product",
    )(*operands)


def shares_kernel(rows_n, split, here, left, early, *refs):
    shares, total = refs[:-1], refs[-1]
    row, layer = lax.axis_index("row"), lax.axis_index("depth")
    value = early[...]
    for index in range(len(shares) // 2):
        pair = shares[2 * index : 2 * index + 2]
        size = pair[0].shape[0] // 2
        block = share_block(row, layer, index, rows_n, split, here, size)
        value += products(left, block, pair, 0, size)
    total[...] = value


def shares_product(left, early, shares, rows_n, split, here):
    operands = [left, early] + shares
    return pl.pallas_call(
        functools.partial(shares_kernel, rows_n, split, here),
        in_specs=[VMEM] * len(operands),
        out_specs=VMEM,
        out_shape=jax.ShapeDtypeStruct(early.shape, early.dtype),
        compiler_params=params((left.shape, 4), (early.shape, 12)),
        cost_estimate=pl.CostEstimate(flops=1000000, bytes_accessed=1000000, transcendentals=0),
        name="shares_product",
    )(*operands)


def product_kernel(rows_n, cols_n, split, damp, near, middle, last_k, last_p, *refs):
    shares = refs[:-3]
    out_ref, left_last, total = refs[-3:]
    out_rows = last_k.shape[1]
    row, layer = lax.axis_index("row"), lax.axis_index("depth")
    place_left(left_last, (last_k, last_p), 0)
    here = near.shape[0] // 4
    rights = [(row * here, here, [near])]
    for index in range(len(shares) // 2):
        pair = shares[2 * index : 2 * index + 2]
        size = pair[0].shape[0] // 2
        block = share_block(row, layer, index, rows_n, split, here, size)
        rights.append((block, size, pair))
    wanted = lax.rem(lax.axis_index("col") + cols_n - cols_n // 2, cols_n)
    for block, size, right in rights:

        @pl.when((wanted >= block) & (wanted < block + size))
        def _():
            total[...] = middle[...] + products(left_last, 0, right, wanted - block, 1)

    out_ref[0] = total[pl.ds(out_rows, out_rows), :] - damp[0]
    out_ref[1] = -total[pl.ds(0, out_rows), :] - damp[1]


def body(k_parts, p_parts, k_mask, p_mask, atoms, classes, rates):
    rows_n, cols_n, depth = (lax.axis_size(a) for a in ("row", "col", "depth"))
    here, width = k_parts.shape[1:]
    out_rows = here // depth
    split = 2 if depth % 2 == 0 else 1
    k_mask, p_mask = k_mask.T, p_mask.T
    (strip,) = mask_rows(k_mask, p_mask, k_parts, p_parts, depth, 1, "mask_strip")
    share = mask_rows(p_mask, k_mask, p_parts, k_parts, split, 2, "mask_share")
    ups, downs = [strip], [strip]
    up = [(i, (i + 1) % cols_n) for i in range(cols_n)]
    for step in range(1, cols_n // 2):
        block = ups[-1] if step == 1 else jnp.concatenate(relay(ups[-1]))
        ups.append(lax.ppermute(block, "col", up))
    last = [lax.ppermute(half, "col", up) for half in relay(ups[-1])]
    for step in range(1, cols_n - cols_n // 2):
        downs.append(lax.ppermute(downs[-1], "col", [(i, (i - 1) % cols_n) for i in range(cols_n)]))
    near, damp = local_part(
        k_mask, p_mask, atoms, classes, rates, k_parts, p_parts, strip
    )
    shares = []
    for shift in range(1, rows_n):
        perm = [(i, (i + shift) % rows_n) for i in range(rows_n)]
        got = [lax.ppermute(part, "row", perm) for part in share]
        shares += got
        if split == 2:
            swap = [(i, i ^ 1) for i in range(depth)]
            shares += [lax.ppermute(part, "depth", swap) for part in got]
    blocks = ups[1:] + downs[1:]
    left, early = early_product(near, strip, blocks, cols_n)
    middle = shares_product(left, early, shares, rows_n, split, here // width)
    operands = [damp, near, middle] + last + shares
    block, total = (2 * out_rows, 4 * width), (2 * out_rows, width)
    return pl.pallas_call(
        functools.partial(product_kernel, rows_n, cols_n, split),
        in_specs=[VMEM] * len(operands),
        out_specs=VMEM,
        out_shape=jax.ShapeDtypeStruct((2, out_rows, width), jnp.float32),
        scratch_shapes=[pltpu.VMEM(block, strip.dtype), pltpu.VMEM(total, jnp.float32)],
        compiler_params=params((near.shape, 2 * rows_n), (left.shape, 2), (block, 4), (total, 16)),
        name="commutator",
    )(*operands)


def solution(mesh):
    return jax.shard_map(
        body,
        mesh=mesh,
        in_specs=(
            P(None, "row", "col"),
            P(None, "row", "col"),
            P("row", "col"),
            P("row", "col"),
            P(),
            P(),
            P(),
        ),
        out_specs=P(None, ("row", "depth"), "col"),
        check_vma=False,
    )
```

```python
import functools

import jax
import jax.numpy as jnp
from jax import lax
from jax.experimental import pallas as pl
from jax.experimental.pallas import tpu as pltpu
from jax.sharding import PartitionSpec as P

TILE = 64

HBM = pl.BlockSpec(memory_space=pltpu.HBM)
SMEM = pl.BlockSpec(memory_space=pltpu.SMEM)
VMEM = pl.BlockSpec(memory_space=pltpu.VMEM)


def params(*shapes):
    total = sum(functools.reduce(lambda a, b: a * b, s) * w for s, w in shapes)
    return pltpu.CompilerParams(vmem_limit_bytes=2 * total + (4 << 20))


def tile_row(mask_ref, tile, width, dtype):
    lanes = lax.broadcasted_iota(jnp.int32, (1, width), 1) // TILE
    row = jnp.zeros((1, width), jnp.float32)
    for place in range(width // TILE):
        row = jnp.where(lanes == place, mask_ref[place, tile].astype(jnp.float32), row)
    return row.astype(dtype)


def fetch_masks(sources, masks, sems):
    copies = [
        pltpu.make_async_copy(ref, masks.at[i], sems.at[i]) for i, ref in enumerate(sources)
    ]
    for copy in copies:
        copy.start()
    return copies


def rows_kernel(places, first_mask, second_mask, first_ref, second_ref, *refs):
    out_refs = refs[:-6]
    held, masked, masks, sems, out_sems, mask_sems = refs[-6:]
    rows, width = held.shape[1:]
    each = 4 // len(out_refs)
    unit = masked.shape[1]
    first = lax.rem(lax.axis_index("depth"), places) * rows
    span = pl.ds(pl.multiple_of(first, rows), rows)
    mask_copies = fetch_masks((first_mask, second_mask), masks, mask_sems)
    copies = [
        pltpu.make_async_copy(ref.at[:, span, :], held.at[pl.ds(2 * i, 2)], sems.at[i])
        for i, ref in enumerate((first_ref, second_ref))
    ]
    for copy in copies:
        copy.start()
    for copy in mask_copies:
        copy.wait()
    out_copies = []
    for i, copy in enumerate(copies):
        copy.wait()
        for tile in range(rows // TILE):
            factor = tile_row(masks.at[i], first // TILE + tile, width, held.dtype)
            at = pl.ds(tile * TILE, TILE)
            block, within = divmod(tile * TILE, unit)
            for part in range(2):
                spot = 2 * (i * (rows // unit) + block) + part
                masked[spot, pl.ds(within, TILE), :] = held[2 * i + part, at, :] * factor
        size = 2 * (rows // unit)
        target = out_refs[i] if each == 2 else out_refs[0].at[pl.ds(i * size, size)]
        out_copies.append(
            pltpu.make_async_copy(masked.at[pl.ds(i * size, size)], target, out_sems.at[i])
        )
        out_copies[-1].start()
    for copy in out_copies:
        copy.wait()


def mask_rows(first_mask, second_mask, first_parts, second_parts, places, arrays, name):
    here, width = first_parts.shape[1:]
    rows, dtype = here // places, first_parts.dtype
    unit = min(rows, width)
    count = 4 * (rows // unit)
    return pl.pallas_call(
        functools.partial(rows_kernel, places),
        in_specs=[HBM] * 4,
        out_specs=[HBM] * arrays,
        out_shape=[jax.ShapeDtypeStruct((count // arrays, unit, width), dtype)] * arrays,
        scratch_shapes=[
            pltpu.VMEM((4, rows, width), dtype),
            pltpu.VMEM((count, unit, width), dtype),
            pltpu.SMEM((2,) + first_mask.shape, first_mask.dtype),
            pltpu.SemaphoreType.DMA((2,)),
            pltpu.SemaphoreType.DMA((2,)),
            pltpu.SemaphoreType.DMA((2,)),
        ],
        name=name,
    )(first_mask, second_mask, first_parts, second_parts)


def local_kernel(
    k_mask,
    p_mask,
    atoms_ref,
    classes_ref,
    rates_ref,
    k_ref,
    p_ref,
    strip,
    near_ref,
    damp,
    held,
    near,
    own,
    masks,
    atoms,
    classes,
    rates,
    sems,
    out_sems,
    small_sems,
):
    here, width = held.shape[1:]
    out_rows = damp.shape[1]
    row, col, layer = (lax.axis_index(a) for a in ("row", "col", "depth"))
    small = fetch_masks((k_mask, p_mask), masks, small_sems)
    copies = [
        pltpu.make_async_copy(ref, held.at[pl.ds(2 * i, 2)], sems.at[i])
        for i, ref in enumerate((p_ref, k_ref))
    ]
    own_copy = pltpu.make_async_copy(strip.at[pl.ds(2, 2)], own, sems.at[2])
    tables = [
        pltpu.make_async_copy(source, target, small_sems.at[2 + i])
        for i, (source, target) in enumerate(
            ((atoms_ref, atoms), (classes_ref, classes), (rates_ref, rates))
        )
    ]
    for copy in copies + [own_copy] + tables:
        copy.start()
    for copy in small + copies:
        copy.wait()
    out_copies = []
    for block in range(here // width):
        for tile in range(block * width // TILE, (block + 1) * width // TILE):
            at, spot = pl.ds(tile * TILE, TILE), pl.ds(tile * TILE - block * width, TILE)
            for i in range(2):
                factor = tile_row(masks.at[1 - i], tile, width, held.dtype)
                for part in (2 * i, 2 * i + 1):
                    near[4 * block + part, spot, :] = held[part, at, :] * factor
        span = pl.ds(4 * block, 4)
        out_copies.append(
            pltpu.make_async_copy(near.at[span], near_ref.at[span], out_sems.at[block])
        )
        out_copies[-1].start()
    for copy in [own_copy] + tables:
        copy.wait()
    lanes = lax.broadcasted_iota(jnp.int32, (1, width), 1) // TILE
    row_tiles, col_tiles = out_rows // TILE, width // TILE
    first = (row * lax.axis_size("depth") + layer) * row_tiles
    for tile in range(row_tiles):
        at = pl.ds(tile * TILE, TILE)
        atom_row = atoms[first + tile]
        gamma = jnp.zeros((1, width), jnp.float32)
        for spot in range(col_tiles):
            atom_col = atoms[col * col_tiles + spot]
            rate = jnp.where(atom_row != atom_col, rates[classes[atom_row, atom_col]], 0.0)
            gamma = jnp.where(lanes == spot, rate, gamma)
        for part in range(2):
            damp[part, at, :] = gamma * own[part, at, :].astype(jnp.float32)
    for copy in out_copies:
        copy.wait()


def local_part(k_mask, p_mask, atoms, classes, rates, k_parts, p_parts, strip):
    here, width = k_parts.shape[1:]
    out_rows, dtype = strip.shape[1], strip.dtype
    blocks = here // width
    near = (4 * blocks, width, width)
    return pl.pallas_call(
        local_kernel,
        in_specs=[HBM] * 8,
        out_specs=[HBM, VMEM],
        out_shape=[
            jax.ShapeDtypeStruct(near, dtype),
            jax.ShapeDtypeStruct((2, out_rows, width), jnp.float32),
        ],
        scratch_shapes=[
            pltpu.VMEM((4, here, width), dtype),
            pltpu.VMEM(near, dtype),
            pltpu.VMEM((2, out_rows, width), dtype),
            pltpu.SMEM((2,) + k_mask.shape, k_mask.dtype),
            pltpu.SMEM(atoms.shape, atoms.dtype),
            pltpu.SMEM(classes.shape, classes.dtype),
            pltpu.SMEM(rates.shape, rates.dtype),
            pltpu.SemaphoreType.DMA((3,)),
            pltpu.SemaphoreType.DMA((blocks,)),
            pltpu.SemaphoreType.DMA((5,)),
        ],
        cost_estimate=pl.CostEstimate(
            flops=8 * here * width, bytes_accessed=20 * here * width, transcendentals=0
        ),
        name="local_part",
    )(k_mask, p_mask, atoms, classes, rates, k_parts, p_parts, strip)


def place_left(left, ref, block):
    k_ref, p_ref = ref if isinstance(ref, tuple) else (ref.at[pl.ds(0, 2)], ref.at[pl.ds(2, 2)])
    rows, width = k_ref.shape[1:]
    k_re, k_im, p_re, p_im = k_ref[0], k_ref[1], p_ref[0], p_ref[1]
    for half, parts in enumerate(((k_re, -k_im, -p_re, p_im), (k_im, k_re, -p_im, -p_re))):
        for slot, part in enumerate(parts):
            at = pl.multiple_of((4 * block + slot) * width, width)
            left[pl.ds(half * rows, rows), pl.ds(at, width)] = part


def relay_kernel(block, k_out, p_out):
    k_out[...] = block[:2]
    p_out[...] = block[2:]


def relay(block):
    return pl.pallas_call(
        relay_kernel,
        in_specs=[VMEM],
        out_specs=[VMEM] * 2,
        out_shape=[jax.ShapeDtypeStruct((2,) + block.shape[1:], block.dtype)] * 2,
        compiler_params=params((block.shape, 4)),
        cost_estimate=pl.CostEstimate(
            flops=10000000000, bytes_accessed=4 * block.size, transcendentals=0
        ),
        name="relay",
    )(block)


def share_block(row, layer, index, rows_n, split, here, size):
    other = lax.rem(row - index // split - 1 + rows_n, rows_n)
    return other * here + (lax.rem(layer, split) ^ (index % split)) * size


def products(left, block, right, first, count):
    each = 4 // len(right)
    width = right[0].shape[1]
    steps = [(0, count)] if each == 4 else [(step, 1) for step in range(count)]
    found = []
    for step, size in steps:
        for half, ref in enumerate(right):
            at = pl.multiple_of((4 * (block + step) + half * each) * width, width)
            value = ref[pl.ds((first + step) * each, size * each)]
            found.append(
                jnp.dot(
                    left[:, pl.ds(at, size * each * width)],
                    value.reshape(size * each * width, width),
                    preferred_element_type=jnp.float32,
                )
            )
    return sum(found[1:], found[0])


def early_kernel(cols_n, near, own, *refs):
    blocks = refs[:-2]
    ups, downs = blocks[: cols_n // 2 - 1], blocks[cols_n // 2 - 1 :]
    left, total = refs[-2:]
    width = own.shape[2]
    row, col = lax.axis_index("row"), lax.axis_index("col")
    place_left(left, own, col)
    for step, ref in enumerate(ups, 1):
        place_left(left, ref, lax.rem(col - step + cols_n, cols_n))
    for step, ref in enumerate(downs, 1):
        place_left(left, ref, lax.rem(col + step, cols_n))
    last = pl.multiple_of(lax.rem(col + cols_n - cols_n // 2, cols_n) * 4 * width, width)
    left[:, pl.ds(last, 4 * width)] = jnp.zeros((left.shape[0], 4 * width), left.dtype)
    count = near.shape[0] // 4
    total[...] = products(left, row * count, [near], 0, count)


def early_product(near, strip, blocks, cols_n):
    out_rows, width = strip.shape[1:]
    left, total = (2 * out_rows, cols_n * 4 * width), (2 * out_rows, width)
    operands = [near, strip] + blocks
    return pl.pallas_call(
        functools.partial(early_kernel, cols_n),
        in_specs=[VMEM] * len(operands),
        out_specs=[VMEM, VMEM],
        out_shape=[
            jax.ShapeDtypeStruct(left, near.dtype),
            jax.ShapeDtypeStruct(total, jnp.float32),
        ],
        compiler_params=params((near.shape, 2), (left, 4), (total, 8)),
        cost_estimate=pl.CostEstimate(
            flops=4 * out_rows * near.shape[0] * width * width * 40,
            bytes_accessed=left[0] * left[1] * 4,
            transcendentals=0,
        ),
        name="early_product",
    )(*operands)


def shares_kernel(rows_n, split, here, left, early, *refs):
    shares, total = refs[:-1], refs[-1]
    row, layer = lax.axis_index("row"), lax.axis_index("depth")
    value = early[...]
    for index in range(len(shares) // 2):
        pair = shares[2 * index : 2 * index + 2]
        size = pair[0].shape[0] // 2
        block = share_block(row, layer, index, rows_n, split, here, size)
        value += products(left, block, pair, 0, size)
    total[...] = value


def shares_product(left, early, shares, rows_n, split, here):
    operands = [left, early] + shares
    return pl.pallas_call(
        functools.partial(shares_kernel, rows_n, split, here),
        in_specs=[VMEM] * len(operands),
        out_specs=VMEM,
        out_shape=jax.ShapeDtypeStruct(early.shape, early.dtype),
        compiler_params=params((left.shape, 4), (early.shape, 12)),
        cost_estimate=pl.CostEstimate(flops=1000000, bytes_accessed=1000000, transcendentals=0),
        name="shares_product",
    )(*operands)


def product_kernel(rows_n, cols_n, split, damp, near, middle, last_k, last_p, *refs):
    shares = refs[:-3]
    out_ref, left_last, total = refs[-3:]
    out_rows = last_k.shape[1]
    row, layer = lax.axis_index("row"), lax.axis_index("depth")
    place_left(left_last, (last_k, last_p), 0)
    here = near.shape[0] // 4
    rights = [(row * here, here, [near])]
    for index in range(len(shares) // 2):
        pair = shares[2 * index : 2 * index + 2]
        size = pair[0].shape[0] // 2
        block = share_block(row, layer, index, rows_n, split, here, size)
        rights.append((block, size, pair))
    wanted = lax.rem(lax.axis_index("col") + cols_n - cols_n // 2, cols_n)
    for block, size, right in rights:

        @pl.when((wanted >= block) & (wanted < block + size))
        def _():
            total[...] = middle[...] + products(left_last, 0, right, wanted - block, 1)

    out_ref[0] = total[pl.ds(out_rows, out_rows), :] - damp[0]
    out_ref[1] = -total[pl.ds(0, out_rows), :] - damp[1]


def body(k_parts, p_parts, k_mask, p_mask, atoms, classes, rates):
    rows_n, cols_n, depth = (lax.axis_size(a) for a in ("row", "col", "depth"))
    here, width = k_parts.shape[1:]
    out_rows = here // depth
    split = 2 if depth % 2 == 0 else 1
    k_mask, p_mask = k_mask.T, p_mask.T
    (strip,) = mask_rows(k_mask, p_mask, k_parts, p_parts, depth, 1, "mask_strip")
    share = mask_rows(p_mask, k_mask, p_parts, k_parts, split, 2, "mask_share")
    ups, downs = [strip], [strip]
    up = [(i, (i + 1) % cols_n) for i in range(cols_n)]
    for step in range(1, cols_n // 2):
        block = ups[-1] if step == 1 else jnp.concatenate(relay(ups[-1]))
        ups.append(lax.ppermute(block, "col", up))
    last = [lax.ppermute(half, "col", up) for half in relay(ups[-1])]
    for step in range(1, cols_n - cols_n // 2):
        downs.append(lax.ppermute(downs[-1], "col", [(i, (i - 1) % cols_n) for i in range(cols_n)]))
    near, damp = local_part(
        k_mask, p_mask, atoms, classes, rates, k_parts, p_parts, strip
    )
    shares = []
    for shift in range(1, rows_n):
        perm = [(i, (i + shift) % rows_n) for i in range(rows_n)]
        got = [lax.ppermute(part, "row", perm) for part in share]
        shares += got
        if split == 2:
            swap = [(i, i ^ 1) for i in range(depth)]
            shares += [lax.ppermute(part, "depth", swap) for part in got]
    blocks = ups[1:] + downs[1:]
    left, early = early_product(near, strip, blocks, cols_n)
    middle = shares_product(left, early, shares, rows_n, split, here // width)
    operands = [damp, near, middle] + last + shares
    block, total = (2 * out_rows, 4 * width), (2 * out_rows, width)
    return pl.pallas_call(
        functools.partial(product_kernel, rows_n, cols_n, split),
        in_specs=[VMEM] * len(operands),
        out_specs=VMEM,
        out_shape=jax.ShapeDtypeStruct((2, out_rows, width), jnp.float32),
        scratch_shapes=[pltpu.VMEM(block, strip.dtype), pltpu.VMEM(total, jnp.float32)],
        compiler_params=params((near.shape, 2 * rows_n), (left.shape, 2), (block, 4), (total, 16)),
        name="commutator",
    )(*operands)


def solution(mesh):
    return jax.shard_map(
        body,
        mesh=mesh,
        in_specs=(
            P(None, "row", "col"),
            P(None, "row", "col"),
            P("row", "col"),
            P("row", "col"),
            P(),
            P(),
            P(),
        ),
        out_specs=P(None, ("row", "depth"), "col"),
        check_vma=False,
    )
```

```python
import functools

import jax
import jax.numpy as jnp
from jax import lax
from jax.experimental import pallas as pl
from jax.experimental.pallas import tpu as pltpu
from jax.sharding import PartitionSpec as P

TILE = 64

HBM = pl.BlockSpec(memory_space=pltpu.HBM)
SMEM = pl.BlockSpec(memory_space=pltpu.SMEM)
VMEM = pl.BlockSpec(memory_space=pltpu.VMEM)


def params(*shapes):
    total = sum(functools.reduce(lambda a, b: a * b, s) * w for s, w in shapes)
    return pltpu.CompilerParams(vmem_limit_bytes=2 * total + (4 << 20))


def tile_row(mask_ref, tile, width, dtype):
    lanes = lax.broadcasted_iota(jnp.int32, (1, width), 1) // TILE
    row = jnp.zeros((1, width), jnp.float32)
    for place in range(width // TILE):
        row = jnp.where(lanes == place, mask_ref[place, tile].astype(jnp.float32), row)
    return row.astype(dtype)


def fetch_masks(sources, masks, sems):
    copies = [
        pltpu.make_async_copy(ref, masks.at[i], sems.at[i]) for i, ref in enumerate(sources)
    ]
    for copy in copies:
        copy.start()
    return copies


def rows_kernel(places, first_mask, second_mask, first_ref, second_ref, *refs):
    out_refs = refs[:-6]
    held, masked, masks, sems, out_sems, mask_sems = refs[-6:]
    rows, width = held.shape[1:]
    each = 4 // len(out_refs)
    unit = masked.shape[1]
    first = lax.rem(lax.axis_index("depth"), places) * rows
    span = pl.ds(pl.multiple_of(first, rows), rows)
    copies = [
        pltpu.make_async_copy(ref.at[:, span, :], held.at[pl.ds(2 * i, 2)], sems.at[i])
        for i, ref in enumerate((first_ref, second_ref))
    ]
    for copy in copies:
        copy.start()
    mask_copies = fetch_masks((first_mask, second_mask), masks, mask_sems)
    for copy in mask_copies:
        copy.wait()
    out_copies = []
    for i, copy in enumerate(copies):
        copy.wait()
        for tile in range(rows // TILE):
            factor = tile_row(masks.at[i], first // TILE + tile, width, held.dtype)
            at = pl.ds(tile * TILE, TILE)
            block, within = divmod(tile * TILE, unit)
            for part in range(2):
                spot = 2 * (i * (rows // unit) + block) + part
                masked[spot, pl.ds(within, TILE), :] = held[2 * i + part, at, :] * factor
        size = 2 * (rows // unit)
        target = out_refs[i] if each == 2 else out_refs[0].at[pl.ds(i * size, size)]
        out_copies.append(
            pltpu.make_async_copy(masked.at[pl.ds(i * size, size)], target, out_sems.at[i])
        )
        out_copies[-1].start()
    for copy in out_copies:
        copy.wait()


def mask_rows(first_mask, second_mask, first_parts, second_parts, places, arrays, name):
    here, width = first_parts.shape[1:]
    rows, dtype = here // places, first_parts.dtype
    unit = min(rows, width)
    count = 4 * (rows // unit)
    return pl.pallas_call(
        functools.partial(rows_kernel, places),
        in_specs=[HBM] * 4,
        out_specs=[HBM] * arrays,
        out_shape=[jax.ShapeDtypeStruct((count // arrays, unit, width), dtype)] * arrays,
        scratch_shapes=[
            pltpu.VMEM((4, rows, width), dtype),
            pltpu.VMEM((count, unit, width), dtype),
            pltpu.SMEM((2,) + first_mask.shape, first_mask.dtype),
            pltpu.SemaphoreType.DMA((2,)),
            pltpu.SemaphoreType.DMA((2,)),
            pltpu.SemaphoreType.DMA((2,)),
        ],
        name=name,
    )(first_mask, second_mask, first_parts, second_parts)


def local_kernel(
    k_mask,
    p_mask,
    atoms_ref,
    classes_ref,
    rates_ref,
    k_ref,
    p_ref,
    strip,
    near_ref,
    damp,
    held,
    near,
    own,
    masks,
    atoms,
    classes,
    rates,
    sems,
    out_sems,
    small_sems,
):
    here, width = held.shape[1:]
    out_rows = damp.shape[1]
    row, col, layer = (lax.axis_index(a) for a in ("row", "col", "depth"))
    small = fetch_masks((k_mask, p_mask), masks, small_sems)
    copies = [
        pltpu.make_async_copy(ref, held.at[pl.ds(2 * i, 2)], sems.at[i])
        for i, ref in enumerate((p_ref, k_ref))
    ]
    own_copy = pltpu.make_async_copy(strip.at[pl.ds(2, 2)], own, sems.at[2])
    tables = [
        pltpu.make_async_copy(source, target, small_sems.at[2 + i])
        for i, (source, target) in enumerate(
            ((atoms_ref, atoms), (classes_ref, classes), (rates_ref, rates))
        )
    ]
    for copy in copies + [own_copy] + tables:
        copy.start()
    for copy in small + copies:
        copy.wait()
    out_copies = []
    for block in range(here // width):
        for tile in range(block * width // TILE, (block + 1) * width // TILE):
            at, spot = pl.ds(tile * TILE, TILE), pl.ds(tile * TILE - block * width, TILE)
            for i in range(2):
                factor = tile_row(masks.at[1 - i], tile, width, held.dtype)
                for part in (2 * i, 2 * i + 1):
                    near[4 * block + part, spot, :] = held[part, at, :] * factor
        span = pl.ds(4 * block, 4)
        out_copies.append(
            pltpu.make_async_copy(near.at[span], near_ref.at[span], out_sems.at[block])
        )
        out_copies[-1].start()
    for copy in [own_copy] + tables:
        copy.wait()
    lanes = lax.broadcasted_iota(jnp.int32, (1, width), 1) // TILE
    row_tiles, col_tiles = out_rows // TILE, width // TILE
    first = (row * lax.axis_size("depth") + layer) * row_tiles
    for tile in range(row_tiles):
        at = pl.ds(tile * TILE, TILE)
        atom_row = atoms[first + tile]
        gamma = jnp.zeros((1, width), jnp.float32)
        for spot in range(col_tiles):
            atom_col = atoms[col * col_tiles + spot]
            rate = jnp.where(atom_row != atom_col, rates[classes[atom_row, atom_col]], 0.0)
            gamma = jnp.where(lanes == spot, rate, gamma)
        for part in range(2):
            damp[part, at, :] = gamma * own[part, at, :].astype(jnp.float32)
    for copy in out_copies:
        copy.wait()


def local_part(k_mask, p_mask, atoms, classes, rates, k_parts, p_parts, strip):
    here, width = k_parts.shape[1:]
    out_rows, dtype = strip.shape[1], strip.dtype
    blocks = here // width
    near = (4 * blocks, width, width)
    return pl.pallas_call(
        local_kernel,
        in_specs=[HBM] * 8,
        out_specs=[HBM, VMEM],
        out_shape=[
            jax.ShapeDtypeStruct(near, dtype),
            jax.ShapeDtypeStruct((2, out_rows, width), jnp.float32),
        ],
        scratch_shapes=[
            pltpu.VMEM((4, here, width), dtype),
            pltpu.VMEM(near, dtype),
            pltpu.VMEM((2, out_rows, width), dtype),
            pltpu.SMEM((2,) + k_mask.shape, k_mask.dtype),
            pltpu.SMEM(atoms.shape, atoms.dtype),
            pltpu.SMEM(classes.shape, classes.dtype),
            pltpu.SMEM(rates.shape, rates.dtype),
            pltpu.SemaphoreType.DMA((3,)),
            pltpu.SemaphoreType.DMA((blocks,)),
            pltpu.SemaphoreType.DMA((5,)),
        ],
        cost_estimate=pl.CostEstimate(
            flops=8 * here * width, bytes_accessed=20 * here * width, transcendentals=0
        ),
        name="local_part",
    )(k_mask, p_mask, atoms, classes, rates, k_parts, p_parts, strip)


def place_left(left, ref, block):
    k_ref, p_ref = ref if isinstance(ref, tuple) else (ref.at[pl.ds(0, 2)], ref.at[pl.ds(2, 2)])
    rows, width = k_ref.shape[1:]
    k_re, k_im, p_re, p_im = k_ref[0], k_ref[1], p_ref[0], p_ref[1]
    for half, parts in enumerate(((k_re, -k_im, -p_re, p_im), (k_im, k_re, -p_im, -p_re))):
        for slot, part in enumerate(parts):
            at = pl.multiple_of((4 * block + slot) * width, width)
            left[pl.ds(half * rows, rows), pl.ds(at, width)] = part


def relay_kernel(block, k_out, p_out):
    k_out[...] = block[:2]
    p_out[...] = block[2:]


def relay(block):
    return pl.pallas_call(
        relay_kernel,
        in_specs=[VMEM],
        out_specs=[VMEM] * 2,
        out_shape=[jax.ShapeDtypeStruct((2,) + block.shape[1:], block.dtype)] * 2,
        compiler_params=params((block.shape, 4)),
        cost_estimate=pl.CostEstimate(
            flops=100000000, bytes_accessed=4 * block.size, transcendentals=0
        ),
        name="relay",
    )(block)


def share_block(row, layer, index, rows_n, split, here, size):
    other = lax.rem(row - index // split - 1 + rows_n, rows_n)
    return other * here + (lax.rem(layer, split) ^ (index % split)) * size


def products(left, block, right, first, count):
    each = 4 // len(right)
    width = right[0].shape[1]
    steps = [(0, count)] if each == 4 else [(step, 1) for step in range(count)]
    found = []
    for step, size in steps:
        for half, ref in enumerate(right):
            at = pl.multiple_of((4 * (block + step) + half * each) * width, width)
            value = ref[pl.ds((first + step) * each, size * each)]
            found.append(
                jnp.dot(
                    left[:, pl.ds(at, size * each * width)],
                    value.reshape(size * each * width, width),
                    preferred_element_type=jnp.float32,
                )
            )
    return sum(found[1:], found[0])


def early_kernel(cols_n, near, own, *refs):
    blocks = refs[:-2]
    ups, downs = blocks[: cols_n // 2 - 1], blocks[cols_n // 2 - 1 :]
    left, total = refs[-2:]
    width = own.shape[2]
    row, col = lax.axis_index("row"), lax.axis_index("col")
    place_left(left, own, col)
    for step, ref in enumerate(ups, 1):
        place_left(left, ref, lax.rem(col - step + cols_n, cols_n))
    for step, ref in enumerate(downs, 1):
        place_left(left, ref, lax.rem(col + step, cols_n))
    last = pl.multiple_of(lax.rem(col + cols_n - cols_n // 2, cols_n) * 4 * width, width)
    left[:, pl.ds(last, 4 * width)] = jnp.zeros((left.shape[0], 4 * width), left.dtype)
    count = near.shape[0] // 4
    total[...] = products(left, row * count, [near], 0, count)


def early_product(near, strip, blocks, cols_n):
    out_rows, width = strip.shape[1:]
    left, total = (2 * out_rows, cols_n * 4 * width), (2 * out_rows, width)
    operands = [near, strip] + blocks
    return pl.pallas_call(
        functools.partial(early_kernel, cols_n),
        in_specs=[VMEM] * len(operands),
        out_specs=[VMEM, VMEM],
        out_shape=[
            jax.ShapeDtypeStruct(left, near.dtype),
            jax.ShapeDtypeStruct(total, jnp.float32),
        ],
        compiler_params=params((near.shape, 2), (left, 4), (total, 8)),
        cost_estimate=pl.CostEstimate(
            flops=4 * out_rows * near.shape[0] * width * width * 40,
            bytes_accessed=left[0] * left[1] * 4,
            transcendentals=0,
        ),
        name="early_product",
    )(*operands)


def shares_kernel(rows_n, split, here, left, early, *refs):
    shares, total = refs[:-1], refs[-1]
    row, layer = lax.axis_index("row"), lax.axis_index("depth")
    value = early[...]
    for index in range(len(shares) // 2):
        pair = shares[2 * index : 2 * index + 2]
        size = pair[0].shape[0] // 2
        block = share_block(row, layer, index, rows_n, split, here, size)
        value += products(left, block, pair, 0, size)
    total[...] = value


def shares_product(left, early, shares, rows_n, split, here):
    operands = [left, early] + shares
    return pl.pallas_call(
        functools.partial(shares_kernel, rows_n, split, here),
        in_specs=[VMEM] * len(operands),
        out_specs=VMEM,
        out_shape=jax.ShapeDtypeStruct(early.shape, early.dtype),
        compiler_params=params((left.shape, 4), (early.shape, 12)),
        cost_estimate=pl.CostEstimate(flops=1000000, bytes_accessed=1000000, transcendentals=0),
        name="shares_product",
    )(*operands)


def product_kernel(rows_n, cols_n, split, damp, near, middle, last_k, last_p, *refs):
    shares = refs[:-3]
    out_ref, left_last, total = refs[-3:]
    out_rows = last_k.shape[1]
    row, layer = lax.axis_index("row"), lax.axis_index("depth")
    place_left(left_last, (last_k, last_p), 0)
    here = near.shape[0] // 4
    rights = [(row * here, here, [near])]
    for index in range(len(shares) // 2):
        pair = shares[2 * index : 2 * index + 2]
        size = pair[0].shape[0] // 2
        block = share_block(row, layer, index, rows_n, split, here, size)
        rights.append((block, size, pair))
    wanted = lax.rem(lax.axis_index("col") + cols_n - cols_n // 2, cols_n)
    for block, size, right in rights:

        @pl.when((wanted >= block) & (wanted < block + size))
        def _():
            total[...] = middle[...] + products(left_last, 0, right, wanted - block, 1)

    out_ref[0] = total[pl.ds(out_rows, out_rows), :] - damp[0]
    out_ref[1] = -total[pl.ds(0, out_rows), :] - damp[1]


def body(k_parts, p_parts, k_mask, p_mask, atoms, classes, rates):
    rows_n, cols_n, depth = (lax.axis_size(a) for a in ("row", "col", "depth"))
    here, width = k_parts.shape[1:]
    out_rows = here // depth
    split = 2 if depth % 2 == 0 else 1
    k_mask, p_mask = k_mask.T, p_mask.T
    (strip,) = mask_rows(k_mask, p_mask, k_parts, p_parts, depth, 1, "mask_strip")
    share = mask_rows(p_mask, k_mask, p_parts, k_parts, split, 2, "mask_share")
    ups, downs = [strip], [strip]
    up = [(i, (i + 1) % cols_n) for i in range(cols_n)]
    for step in range(1, cols_n // 2):
        block = ups[-1] if step == 1 else jnp.concatenate(relay(ups[-1]))
        ups.append(lax.ppermute(block, "col", up))
    last = [lax.ppermute(half, "col", up) for half in relay(ups[-1])]
    for step in range(1, cols_n - cols_n // 2):
        downs.append(lax.ppermute(downs[-1], "col", [(i, (i - 1) % cols_n) for i in range(cols_n)]))
    near, damp = local_part(
        k_mask, p_mask, atoms, classes, rates, k_parts, p_parts, strip
    )
    shares = []
    for shift in range(1, rows_n):
        perm = [(i, (i + shift) % rows_n) for i in range(rows_n)]
        got = [lax.ppermute(part, "row", perm) for part in share]
        shares += got
        if split == 2:
            swap = [(i, i ^ 1) for i in range(depth)]
            shares += [lax.ppermute(part, "depth", swap) for part in got]
    blocks = ups[1:] + downs[1:]
    left, early = early_product(near, strip, blocks, cols_n)
    middle = shares_product(left, early, shares, rows_n, split, here // width)
    operands = [damp, near, middle] + last + shares
    block, total = (2 * out_rows, 4 * width), (2 * out_rows, width)
    return pl.pallas_call(
        functools.partial(product_kernel, rows_n, cols_n, split),
        in_specs=[VMEM] * len(operands),
        out_specs=VMEM,
        out_shape=jax.ShapeDtypeStruct((2, out_rows, width), jnp.float32),
        scratch_shapes=[pltpu.VMEM(block, strip.dtype), pltpu.VMEM(total, jnp.float32)],
        compiler_params=params((near.shape, 2 * rows_n), (left.shape, 2), (block, 4), (total, 16)),
        name="commutator",
    )(*operands)


def solution(mesh):
    return jax.shard_map(
        body,
        mesh=mesh,
        in_specs=(
            P(None, "row", "col"),
            P(None, "row", "col"),
            P("row", "col"),
            P("row", "col"),
            P(),
            P(),
            P(),
        ),
        out_specs=P(None, ("row", "depth"), "col"),
        check_vma=False,
    )
```

```python
import functools

import jax
import jax.numpy as jnp
from jax import lax
from jax.experimental import pallas as pl
from jax.experimental.pallas import tpu as pltpu
from jax.sharding import PartitionSpec as P

TILE = 64

HBM = pl.BlockSpec(memory_space=pltpu.HBM)
SMEM = pl.BlockSpec(memory_space=pltpu.SMEM)
VMEM = pl.BlockSpec(memory_space=pltpu.VMEM)


def params(*shapes):
    total = sum(functools.reduce(lambda a, b: a * b, s) * w for s, w in shapes)
    return pltpu.CompilerParams(vmem_limit_bytes=2 * total + (4 << 20))


def tile_row(mask_ref, tile, width, dtype):
    lanes = lax.broadcasted_iota(jnp.int32, (1, width), 1) // TILE
    row = jnp.zeros((1, width), jnp.float32)
    for place in range(width // TILE):
        row = jnp.where(lanes == place, mask_ref[place, tile].astype(jnp.float32), row)
    return row.astype(dtype)


def fetch_masks(sources, masks, sems):
    copies = [
        pltpu.make_async_copy(ref, masks.at[i], sems.at[i]) for i, ref in enumerate(sources)
    ]
    for copy in copies:
        copy.start()
    return copies


def rows_kernel(places, first_mask, second_mask, first_ref, second_ref, *refs):
    out_refs = refs[:-6]
    held, masked, masks, sems, out_sems, mask_sems = refs[-6:]
    rows, width = held.shape[1:]
    each = 4 // len(out_refs)
    unit = masked.shape[1]
    first = lax.rem(lax.axis_index("depth"), places) * rows
    span = pl.ds(pl.multiple_of(first, rows), rows)
    copies = [
        pltpu.make_async_copy(ref.at[:, span, :], held.at[pl.ds(2 * i, 2)], sems.at[i])
        for i, ref in enumerate((first_ref, second_ref))
    ]
    for copy in copies:
        copy.start()
    mask_copies = fetch_masks((first_mask, second_mask), masks, mask_sems)
    for copy in mask_copies:
        copy.wait()
    out_copies = []
    for i, copy in enumerate(copies):
        copy.wait()
        for tile in range(rows // TILE):
            factor = tile_row(masks.at[i], first // TILE + tile, width, held.dtype)
            at = pl.ds(tile * TILE, TILE)
            block, within = divmod(tile * TILE, unit)
            for part in range(2):
                spot = 2 * (i * (rows // unit) + block) + part
                masked[spot, pl.ds(within, TILE), :] = held[2 * i + part, at, :] * factor
        size = 2 * (rows // unit)
        target = out_refs[i] if each == 2 else out_refs[0].at[pl.ds(i * size, size)]
        out_copies.append(
            pltpu.make_async_copy(masked.at[pl.ds(i * size, size)], target, out_sems.at[i])
        )
        out_copies[-1].start()
    for copy in out_copies:
        copy.wait()


def mask_rows(first_mask, second_mask, first_parts, second_parts, places, arrays, name):
    here, width = first_parts.shape[1:]
    rows, dtype = here // places, first_parts.dtype
    unit = min(rows, width)
    count = 4 * (rows // unit)
    return pl.pallas_call(
        functools.partial(rows_kernel, places),
        in_specs=[HBM] * 4,
        out_specs=[HBM] * arrays,
        out_shape=[jax.ShapeDtypeStruct((count // arrays, unit, width), dtype)] * arrays,
        scratch_shapes=[
            pltpu.VMEM((4, rows, width), dtype),
            pltpu.VMEM((count, unit, width), dtype),
            pltpu.SMEM((2,) + first_mask.shape, first_mask.dtype),
            pltpu.SemaphoreType.DMA((2,)),
            pltpu.SemaphoreType.DMA((2,)),
            pltpu.SemaphoreType.DMA((2,)),
        ],
        name=name,
    )(first_mask, second_mask, first_parts, second_parts)


def local_kernel(
    k_mask,
    p_mask,
    atoms_ref,
    classes_ref,
    rates_ref,
    k_ref,
    p_ref,
    strip,
    near_ref,
    damp,
    held,
    near,
    own,
    masks,
    atoms,
    classes,
    rates,
    sems,
    out_sems,
    small_sems,
):
    here, width = held.shape[1:]
    out_rows = damp.shape[1]
    row, col, layer = (lax.axis_index(a) for a in ("row", "col", "depth"))
    copies = [
        pltpu.make_async_copy(ref, held.at[pl.ds(2 * i, 2)], sems.at[i])
        for i, ref in enumerate((p_ref, k_ref))
    ]
    own_copy = pltpu.make_async_copy(strip.at[pl.ds(2, 2)], own, sems.at[2])
    tables = [
        pltpu.make_async_copy(source, target, small_sems.at[2 + i])
        for i, (source, target) in enumerate(
            ((atoms_ref, atoms), (classes_ref, classes), (rates_ref, rates))
        )
    ]
    for copy in copies + [own_copy] + tables:
        copy.start()
    small = fetch_masks((k_mask, p_mask), masks, small_sems)
    for copy in small + copies:
        copy.wait()
    out_copies = []
    for block in range(here // width):
        for tile in range(block * width // TILE, (block + 1) * width // TILE):
            at, spot = pl.ds(tile * TILE, TILE), pl.ds(tile * TILE - block * width, TILE)
            for i in range(2):
                factor = tile_row(masks.at[1 - i], tile, width, held.dtype)
                for part in (2 * i, 2 * i + 1):
                    near[4 * block + part, spot, :] = held[part, at, :] * factor
        span = pl.ds(4 * block, 4)
        out_copies.append(
            pltpu.make_async_copy(near.at[span], near_ref.at[span], out_sems.at[block])
        )
        out_copies[-1].start()
    for copy in [own_copy] + tables:
        copy.wait()
    lanes = lax.broadcasted_iota(jnp.int32, (1, width), 1) // TILE
    row_tiles, col_tiles = out_rows // TILE, width // TILE
    first = (row * lax.axis_size("depth") + layer) * row_tiles
    for tile in range(row_tiles):
        at = pl.ds(tile * TILE, TILE)
        atom_row = atoms[first + tile]
        gamma = jnp.zeros((1, width), jnp.float32)
        for spot in range(col_tiles):
            atom_col = atoms[col * col_tiles + spot]
            rate = jnp.where(atom_row != atom_col, rates[classes[atom_row, atom_col]], 0.0)
            gamma = jnp.where(lanes == spot, rate, gamma)
        for part in range(2):
            damp[part, at, :] = gamma * own[part, at, :].astype(jnp.float32)
    for copy in out_copies:
        copy.wait()


def local_part(k_mask, p_mask, atoms, classes, rates, k_parts, p_parts, strip):
    here, width = k_parts.shape[1:]
    out_rows, dtype = strip.shape[1], strip.dtype
    blocks = here // width
    near = (4 * blocks, width, width)
    return pl.pallas_call(
        local_kernel,
        in_specs=[HBM] * 8,
        out_specs=[HBM, VMEM],
        out_shape=[
            jax.ShapeDtypeStruct(near, dtype),
            jax.ShapeDtypeStruct((2, out_rows, width), jnp.float32),
        ],
        scratch_shapes=[
            pltpu.VMEM((4, here, width), dtype),
            pltpu.VMEM(near, dtype),
            pltpu.VMEM((2, out_rows, width), dtype),
            pltpu.SMEM((2,) + k_mask.shape, k_mask.dtype),
            pltpu.SMEM(atoms.shape, atoms.dtype),
            pltpu.SMEM(classes.shape, classes.dtype),
            pltpu.SMEM(rates.shape, rates.dtype),
            pltpu.SemaphoreType.DMA((3,)),
            pltpu.SemaphoreType.DMA((blocks,)),
            pltpu.SemaphoreType.DMA((5,)),
        ],
        cost_estimate=pl.CostEstimate(
            flops=8 * here * width, bytes_accessed=20 * here * width, transcendentals=0
        ),
        name="local_part",
    )(k_mask, p_mask, atoms, classes, rates, k_parts, p_parts, strip)


def place_left(left, ref, block):
    k_ref, p_ref = ref if isinstance(ref, tuple) else (ref.at[pl.ds(0, 2)], ref.at[pl.ds(2, 2)])
    rows, width = k_ref.shape[1:]
    k_re, k_im, p_re, p_im = k_ref[0], k_ref[1], p_ref[0], p_ref[1]
    for half, parts in enumerate(((k_re, -k_im, -p_re, p_im), (k_im, k_re, -p_im, -p_re))):
        for slot, part in enumerate(parts):
            at = pl.multiple_of((4 * block + slot) * width, width)
            left[pl.ds(half * rows, rows), pl.ds(at, width)] = part


def relay_kernel(block, k_out, p_out):
    k_out[...] = block[:2]
    p_out[...] = block[2:]


def relay(block):
    return pl.pallas_call(
        relay_kernel,
        in_specs=[VMEM],
        out_specs=[VMEM] * 2,
        out_shape=[jax.ShapeDtypeStruct((2,) + block.shape[1:], block.dtype)] * 2,
        compiler_params=params((block.shape, 4)),
        cost_estimate=pl.CostEstimate(
            flops=100000000, bytes_accessed=4 * block.size, transcendentals=0
        ),
        name="relay",
    )(block)


def share_block(row, layer, index, rows_n, split, here, size):
    other = lax.rem(row - index // split - 1 + rows_n, rows_n)
    return other * here + (lax.rem(layer, split) ^ (index % split)) * size


def products(left, block, right, first, count):
    each = 4 // len(right)
    width = right[0].shape[1]
    steps = [(0, count)] if each == 4 else [(step, 1) for step in range(count)]
    found = []
    for step, size in steps:
        for half, ref in enumerate(right):
            at = pl.multiple_of((4 * (block + step) + half * each) * width, width)
            value = ref[pl.ds((first + step) * each, size * each)]
            found.append(
                jnp.dot(
                    left[:, pl.ds(at, size * each * width)],
                    value.reshape(size * each * width, width),
                    preferred_element_type=jnp.float32,
                )
            )
    return sum(found[1:], found[0])


def early_kernel(cols_n, near, own, *refs):
    blocks = refs[:-2]
    ups, downs = blocks[: cols_n // 2 - 1], blocks[cols_n // 2 - 1 :]
    left, total = refs[-2:]
    width = own.shape[2]
    row, col = lax.axis_index("row"), lax.axis_index("col")
    place_left(left, own, col)
    for step, ref in enumerate(ups, 1):
        place_left(left, ref, lax.rem(col - step + cols_n, cols_n))
    for step, ref in enumerate(downs, 1):
        place_left(left, ref, lax.rem(col + step, cols_n))
    last = pl.multiple_of(lax.rem(col + cols_n - cols_n // 2, cols_n) * 4 * width, width)
    left[:, pl.ds(last, 4 * width)] = jnp.zeros((left.shape[0], 4 * width), left.dtype)
    count = near.shape[0] // 4
    total[...] = products(left, row * count, [near], 0, count)


def early_product(near, strip, blocks, cols_n):
    out_rows, width = strip.shape[1:]
    left, total = (2 * out_rows, cols_n * 4 * width), (2 * out_rows, width)
    operands = [near, strip] + blocks
    return pl.pallas_call(
        functools.partial(early_kernel, cols_n),
        in_specs=[VMEM] * len(operands),
        out_specs=[VMEM, VMEM],
        out_shape=[
            jax.ShapeDtypeStruct(left, near.dtype),
            jax.ShapeDtypeStruct(total, jnp.float32),
        ],
        compiler_params=params((near.shape, 2), (left, 4), (total, 8)),
        cost_estimate=pl.CostEstimate(
            flops=4 * out_rows * near.shape[0] * width * width * 40,
            bytes_accessed=left[0] * left[1] * 4,
            transcendentals=0,
        ),
        name="early_product",
    )(*operands)


def shares_kernel(rows_n, split, here, left, early, *refs):
    shares, total = refs[:-1], refs[-1]
    row, layer = lax.axis_index("row"), lax.axis_index("depth")
    value = early[...]
    for index in range(len(shares) // 2):
        pair = shares[2 * index : 2 * index + 2]
        size = pair[0].shape[0] // 2
        block = share_block(row, layer, index, rows_n, split, here, size)
        value += products(left, block, pair, 0, size)
    total[...] = value


def shares_product(left, early, shares, rows_n, split, here):
    operands = [left, early] + shares
    return pl.pallas_call(
        functools.partial(shares_kernel, rows_n, split, here),
        in_specs=[VMEM] * len(operands),
        out_specs=VMEM,
        out_shape=jax.ShapeDtypeStruct(early.shape, early.dtype),
        compiler_params=params((left.shape, 4), (early.shape, 12)),
        cost_estimate=pl.CostEstimate(flops=1000000, bytes_accessed=1000000, transcendentals=0),
        name="shares_product",
    )(*operands)


def product_kernel(rows_n, cols_n, split, damp, near, middle, last_k, last_p, *refs):
    shares = refs[:-3]
    out_ref, left_last, total = refs[-3:]
    out_rows = last_k.shape[1]
    row, layer = lax.axis_index("row"), lax.axis_index("depth")
    place_left(left_last, (last_k, last_p), 0)
    here = near.shape[0] // 4
    rights = [(row * here, here, [near])]
    for index in range(len(shares) // 2):
        pair = shares[2 * index : 2 * index + 2]
        size = pair[0].shape[0] // 2
        block = share_block(row, layer, index, rows_n, split, here, size)
        rights.append((block, size, pair))
    wanted = lax.rem(lax.axis_index("col") + cols_n - cols_n // 2, cols_n)
    for block, size, right in rights:

        @pl.when((wanted >= block) & (wanted < block + size))
        def _():
            total[...] = middle[...] + products(left_last, 0, right, wanted - block, 1)

    out_ref[0] = total[pl.ds(out_rows, out_rows), :] - damp[0]
    out_ref[1] = -total[pl.ds(0, out_rows), :] - damp[1]


def body(k_parts, p_parts, k_mask, p_mask, atoms, classes, rates):
    rows_n, cols_n, depth = (lax.axis_size(a) for a in ("row", "col", "depth"))
    here, width = k_parts.shape[1:]
    out_rows = here // depth
    split = 2 if depth % 2 == 0 else 1
    k_mask, p_mask = k_mask.T, p_mask.T
    (strip,) = mask_rows(k_mask, p_mask, k_parts, p_parts, depth, 1, "mask_strip")
    share = mask_rows(p_mask, k_mask, p_parts, k_parts, split, 2, "mask_share")
    ups, downs = [strip], [strip]
    up = [(i, (i + 1) % cols_n) for i in range(cols_n)]
    for step in range(1, cols_n // 2):
        block = ups[-1] if step == 1 else jnp.concatenate(relay(ups[-1]))
        ups.append(lax.ppermute(block, "col", up))
    last = [lax.ppermute(half, "col", up) for half in relay(ups[-1])]
    for step in range(1, cols_n - cols_n // 2):
        downs.append(lax.ppermute(downs[-1], "col", [(i, (i - 1) % cols_n) for i in range(cols_n)]))
    near, damp = local_part(
        k_mask, p_mask, atoms, classes, rates, k_parts, p_parts, strip
    )
    shares = []
    for shift in range(1, rows_n):
        perm = [(i, (i + shift) % rows_n) for i in range(rows_n)]
        got = [lax.ppermute(part, "row", perm) for part in share]
        shares += got
        if split == 2:
            swap = [(i, i ^ 1) for i in range(depth)]
            shares += [lax.ppermute(part, "depth", swap) for part in got]
    blocks = ups[1:] + downs[1:]
    left, early = early_product(near, strip, blocks, cols_n)
    middle = shares_product(left, early, shares, rows_n, split, here // width)
    operands = [damp, near, middle] + last + shares
    block, total = (2 * out_rows, 4 * width), (2 * out_rows, width)
    return pl.pallas_call(
        functools.partial(product_kernel, rows_n, cols_n, split),
        in_specs=[VMEM] * len(operands),
        out_specs=VMEM,
        out_shape=jax.ShapeDtypeStruct((2, out_rows, width), jnp.float32),
        scratch_shapes=[pltpu.VMEM(block, strip.dtype), pltpu.VMEM(total, jnp.float32)],
        compiler_params=params((near.shape, 2 * rows_n), (left.shape, 2), (block, 4), (total, 16)),
        name="commutator",
    )(*operands)


def solution(mesh):
    return jax.shard_map(
        body,
        mesh=mesh,
        in_specs=(
            P(None, "row", "col"),
            P(None, "row", "col"),
            P("row", "col"),
            P("row", "col"),
            P(),
            P(),
            P(),
        ),
        out_specs=P(None, ("row", "depth"), "col"),
        check_vma=False,
    )
```
